32 devices in a mesh: dp: 4 (over y, core), rep: 8 (over z, x).
Axes of the slice: x: 2, y: 2, z: 4, core: 2. Of those that a mesh axis runs over, the one named last changes fastest.
Arguments:
- images: bfloat16 [512, 50, 768], P(('dp', 'rep')), may hold values from -6 to 6
- qkv_weight: bfloat16 [768, 2304], replicated, may hold values from -0.21875 to 0.21875
- out_weight: bfloat16 [768, 768], replicated, may hold values from -0.625 to 0.625
- fc1_weight: bfloat16 [768, 3072], replicated, may hold values from -0.21875 to 0.21875
- fc1_bias: float32 [3072], replicated, may hold values from -3 to 3
- fc2_weight: bfloat16 [3072, 768], replicated, may hold values from -0.109375 to 0.109375
- ln1_gain: float32 [768], replicated, may hold values from 0.5 to 1.5
- ln1_bias: float32 [768], replicated, may hold values from -1 to 1
- ln2_gain: float32 [768], replicated, may hold values from 0.5 to 1.5
- ln2_bias: float32 [768], replicated, may hold values from -1 to 1
- post_gain: float32 [768], replicated, may hold values from 0.5 to 1.5
- post_bias: float32 [768], replicated, may hold values from -1 to 1
- image_proj: bfloat16 [768, 512], replicated, may hold values from -0.21875 to 0.21875
- text_feats: bfloat16 [1536, 512], P(('dp', 'rep')), may hold values from -6 to 6
- text_gain: float32 [512], replicated, may hold values from 0.5 to 1.5
- text_bias: float32 [512], replicated, may hold values from -1 to 1
- text_proj: bfloat16 [512, 512], replicated, may hold values from -0.25 to 0.25
- log_scale: float32 [1], replicated, may hold values from 3.4 to 4
- caption_counts: int32 [512], P(('dp', 'rep')), may hold values from 1 to 5, as said below
- positives: int32 [1536], P(('dp', 'rep')), may hold values from 0 to 511, as said below
Outputs:
- block_out: bfloat16 [512, 50, 768], P(('dp', 'rep'))
- loss: float32 [], replicated
- grad_images: float32 [512, 50, 768], P(('dp', 'rep'))
- grad_qkv_weight: float32 [768, 2304], P('rep', 'dp')
- grad_out_weight: float32 [768, 768], P('rep', 'dp')
- grad_fc1_weight: float32 [768, 3072], P('rep', 'dp')
- grad_fc1_bias: float32 [3072], replicated
- grad_fc2_weight: float32 [3072, 768], P('rep', 'dp')
- grad_ln1_gain: float32 [768], replicated
- grad_ln1_bias: float32 [768], replicated
- grad_ln2_gain: float32 [768], replicated
- grad_ln2_bias: float32 [768], replicated
- grad_post_gain: float32 [768], replicated
- grad_post_bias: float32 [768], replicated
- grad_image_proj: float32 [768, 512], P('rep', 'dp')
- grad_text_feats: float32 [1536, 512], P(('dp', 'rep'))
- grad_text_gain: float32 [512], replicated
- grad_text_bias: float32 [512], replicated
- grad_text_proj: float32 [512, 512], P('rep', 'dp')
- grad_log_scale: float32 [1], replicated
The draws below stay inside these ranges and needn't reach their ends.
Inputs may be any that keep to these rules, and one draw needn't show every extreme that they name: caption_counts[i] is the number of captions c with positives[c] = i; the counts sum to 1536. `positives`: the captions of an image stand anywhere among all captions.
All inputs are finite; a program needn't handle non-finite values.
Results may differ from the reference program's by a relative error of at most 0.015.
The reference program's roundings to bfloat16 on the way count: a program that leaves them out, or rounds other values in their place, can miss the bound.
Values may be sent and summed in bfloat16 or wider, within the bound.
A program may use at most 192 MiB of HBM per device.

```python
import math
import jax
import jax.numpy as jnp
from jax import lax

D = 768
HEADS = 12
HDIM = 64
FF = 3072
EMB = 512
TEXTW = 512
PATCH = 50
IMAGES = 512
CAPTIONS = 1536


def caption_layout(key):
    key_first = jax.random.fold_in(key, 11)
    key_second = jax.random.fold_in(key, 12)
    key_order = jax.random.fold_in(key, 13)
    key_shuffle = jax.random.fold_in(key, 14)
    slot_count = 4 * IMAGES
    slot_ids = jnp.arange(slot_count, dtype=jnp.int32)
    owner = slot_ids // 4
    fullest = jax.random.randint(key_first, (), 0, IMAGES, dtype=jnp.int32)
    emptiest = (fullest + 1 + jax.random.randint(key_second, (), 0, IMAGES - 1, dtype=jnp.int32)) % IMAGES
    ranking = jax.random.permutation(key_order, slot_count).astype(jnp.int32)
    ranking = jnp.where(owner == fullest, slot_ids % 4 - 4, jnp.where(owner == emptiest, slot_count + slot_ids % 4, ranking))
    ordering = jnp.argsort(ranking, stable=True)
    chosen = jnp.zeros((slot_count,), jnp.int32).at[ordering[:2 * IMAGES]].set(1)
    counts = 1 + jnp.sum(chosen.reshape(IMAGES, 4), 1)
    ends = jnp.cumsum(counts)
    caption_owner = jnp.searchsorted(ends, jnp.arange(CAPTIONS, dtype=jnp.int32), side='right').astype(jnp.int32)
    shuffle = jax.random.permutation(key_shuffle, CAPTIONS)
    return (counts.astype(jnp.int32), caption_owner[shuffle].astype(jnp.int32))


def draw_caption_counts(key, part):
    return caption_layout(key)[0]


def draw_positives(key, part):
    return caption_layout(key)[1]


def steps_of(rng, dims, split, least, top_value):
    factor_of, own = 1.0, jax.random.fold_in(rng, 6)
    for position, shards_of in split:
        heights = jnp.exp(jax.random.uniform(jax.random.fold_in(own, position), (shards_of,), jnp.float32, least / len(split), top_value / len(split)))
        factor_of = factor_of * jnp.repeat(heights, dims[position] // shards_of).reshape([-1 if axis == position else 1 for axis in range(len(dims))])
    return factor_of


def noise(own_key, extent, width, bound, cuts=(), kind=jnp.bfloat16):
    level = steps_of(own_key, extent, cuts, -0.22, 0.18) if cuts else 1.0
    entries = jax.random.normal(own_key, extent, jnp.float32) * width * level
    return jnp.minimum(jnp.maximum(entries, -bound), bound).astype(kind)


def setup_inputs(seed: int = 0) -> dict:
    arg_keys = jax.random.split(jax.random.key(seed), 21)
    images = noise(arg_keys[0], (IMAGES, PATCH, D), 1.0, 6.0, ((0, 32),))
    qkv_weight = noise(arg_keys[1], (D, 3 * D), D ** -0.5, 0.21875)
    out_weight = noise(arg_keys[2], (D, D), (D // 8) ** -0.5, 0.625)
    fc1_weight = noise(arg_keys[3], (D, FF), D ** -0.5, 0.21875)
    fc1_bias = noise(arg_keys[4], (FF,), 0.5, 3.0, (), jnp.float32)
    fc2_weight = noise(arg_keys[5], (FF, D), FF ** -0.5, 0.109375)
    ln1_gain = jnp.clip(1.0 + 0.1 * jax.random.normal(arg_keys[6], (D,), jnp.float32), 0.5, 1.5)
    ln1_bias = noise(arg_keys[7], (D,), 0.2, 1.0, (), jnp.float32)
    ln2_gain = jnp.clip(1.0 + 0.1 * jax.random.normal(arg_keys[8], (D,), jnp.float32), 0.5, 1.5)
    ln2_bias = noise(arg_keys[9], (D,), 0.2, 1.0, (), jnp.float32)
    post_gain = jnp.clip(1.0 + 0.1 * jax.random.normal(arg_keys[10], (D,), jnp.float32), 0.5, 1.5)
    post_bias = noise(arg_keys[11], (D,), 0.2, 1.0, (), jnp.float32)
    image_proj = noise(arg_keys[12], (D, EMB), D ** -0.5, 0.21875)
    text_feats = noise(arg_keys[13], (CAPTIONS, TEXTW), 1.0, 6.0, ((0, 32),))
    text_gain = jnp.clip(1.0 + 0.1 * jax.random.normal(arg_keys[14], (TEXTW,), jnp.float32), 0.5, 1.5)
    text_bias = noise(arg_keys[15], (TEXTW,), 0.2, 1.0, (), jnp.float32)
    text_proj = noise(arg_keys[16], (TEXTW, EMB), TEXTW ** -0.5, 0.25)
    log_scale = jnp.clip(jax.random.uniform(arg_keys[17], (1,), jnp.float32, 3.4, 4.0), 3.4, 4.0)
    caption_counts = draw_caption_counts(jax.random.fold_in(arg_keys[20], 71), 0)
    positives = draw_positives(jax.random.fold_in(arg_keys[20], 71), 0)
    return {"images": images, "qkv_weight": qkv_weight, "out_weight": out_weight, "fc1_weight": fc1_weight, "fc1_bias": fc1_bias, "fc2_weight": fc2_weight, "ln1_gain": ln1_gain, "ln1_bias": ln1_bias, "ln2_gain": ln2_gain, "ln2_bias": ln2_bias, "post_gain": post_gain, "post_bias": post_bias, "image_proj": image_proj, "text_feats": text_feats, "text_gain": text_gain, "text_bias": text_bias, "text_proj": text_proj, "log_scale": log_scale, "caption_counts": caption_counts, "positives": positives}


@jax.custom_vjp
def low(v):
    return lax.optimization_barrier(v.astype(jnp.bfloat16)).astype(jnp.float32)

@jax.custom_vjp
def low_back(v):
    return v

def low_keep(v):
    return (low(v), None)

def low_pass(kept, grad):
    return (grad,)

def back_keep(v):
    return (v, None)

def back_low(kept, grad):
    return (low(grad),)
low.defvjp(low_keep, low_pass)
low_back.defvjp(back_keep, back_low)
exact_mode = lax.Precision.HIGHEST

def layer_norm(values, gain, bias):
    centered = values - lax.optimization_barrier(jnp.mean(values, -1, keepdims=True))
    factor = lax.rsqrt(lax.optimization_barrier(jnp.mean(centered * centered, -1, keepdims=True)) + 1e-05)
    return centered * factor * gain + bias

def unit_rows(values):
    return values * lax.rsqrt(lax.optimization_barrier(jnp.sum(values * values, -1, keepdims=True)) + 1e-06)

def block_group(group_rows, qkv_weight, out_weight, fc1_weight, fc1_bias, fc2_weight, ln1_gain, ln1_bias, ln2_gain, ln2_bias):
    group_size = group_rows.shape[0]
    normed_in = low(layer_norm(group_rows, ln1_gain, ln1_bias))
    packed = low_back(low(jnp.einsum('gpd,de->gpe', normed_in, qkv_weight, precision=exact_mode)))
    packed = packed.reshape(group_size, PATCH, 3, HEADS, HDIM)
    query, keys, values = (packed[:, :, 0], packed[:, :, 1], packed[:, :, 2])
    scores = low_back(0.125 * jnp.einsum('gqhd,gkhd->ghqk', query, keys, precision=exact_mode))
    attn_low = low(jax.nn.softmax(scores, -1))
    mixed = jnp.einsum('ghqk,gkhd->gqhd', attn_low, values, precision=exact_mode)
    mixed = low_back(low(mixed)).reshape(group_size, PATCH, D)
    middle = group_rows + low_back(jnp.einsum('gpd,de->gpe', mixed, out_weight, precision=exact_mode))
    normed_mid = low(layer_norm(middle, ln2_gain, ln2_bias))
    hidden = low_back(jnp.einsum('gpd,df->gpf', normed_mid, fc1_weight, precision=exact_mode) + fc1_bias)
    activation = low(hidden * jax.nn.sigmoid(1.702 * hidden))
    return middle + low_back(jnp.einsum('gpf,fd->gpd', activation, fc2_weight, precision=exact_mode))

def reference(images, qkv_weight, out_weight, fc1_weight, fc1_bias, fc2_weight, ln1_gain, ln1_bias, ln2_gain, ln2_bias, post_gain, post_bias, image_proj, text_feats, text_gain, text_bias, text_proj, log_scale, caption_counts, positives):
    floats = [item.astype(jnp.float32) for item in (images, qkv_weight, out_weight, fc1_weight, fc1_bias, fc2_weight, ln1_gain, ln1_bias, ln2_gain, ln2_bias, post_gain, post_bias, image_proj, text_feats, text_gain, text_bias, text_proj, log_scale)]
    counts = caption_counts.astype(jnp.float32)
    match = (positives[None, :] == jnp.arange(IMAGES, dtype=jnp.int32)[:, None]).astype(jnp.float32)
    text_ratio = IMAGES / CAPTIONS

    def forward(images, qkv_weight, out_weight, fc1_weight, fc1_bias, fc2_weight, ln1_gain, ln1_bias, ln2_gain, ln2_bias, post_gain, post_bias, image_proj, text_feats, text_gain, text_bias, text_proj, log_scale):
        group_size = math.gcd(IMAGES, 64)

        def run_group(group_rows):
            return block_group(group_rows, qkv_weight, out_weight, fc1_weight, fc1_bias, fc2_weight, ln1_gain, ln1_bias, ln2_gain, ln2_bias)
        grouped = images.reshape(IMAGES // group_size, group_size, PATCH, D)
        block = lax.map(jax.checkpoint(run_group), grouped).reshape(IMAGES, PATCH, D)
        class_norm = low(layer_norm(block[:, 0, :], post_gain, post_bias))
        image_embed = low_back(jnp.matmul(class_norm, image_proj, precision=exact_mode))
        image_low = low(unit_rows(image_embed))
        text_norm = low(layer_norm(text_feats, text_gain, text_bias))
        text_embed = low_back(jnp.matmul(text_norm, text_proj, precision=exact_mode))
        text_low = low(unit_rows(text_embed))
        cosines = jnp.matmul(image_low, text_low.T, precision=exact_mode)
        logit_scale = jnp.exp(log_scale[0])
        row_logits = low_back(logit_scale * cosines)
        col_logits = low_back(logit_scale * cosines)
        image_loss = jax.nn.logsumexp(row_logits, 1) - lax.optimization_barrier(jnp.sum(match * row_logits, 1)) / counts
        caption_loss = jax.nn.logsumexp(col_logits, 0) - lax.optimization_barrier(jnp.sum(match * col_logits, 0))
        total = 0.5 * jnp.sum(image_loss) + 0.5 * text_ratio * jnp.sum(caption_loss)
        return (total, (block, total / IMAGES))
    total, pullback, extras = jax.vjp(forward, *floats, has_aux=True)
    grads = pullback(jnp.ones((), jnp.float32))
    return (extras[0].astype(jnp.bfloat16), extras[1], grads[0], grads[1], grads[2], grads[3], grads[4], grads[5], grads[6], grads[7], grads[8], grads[9], grads[10], grads[11], grads[12], grads[13], grads[14], grads[15], grads[16], grads[17])
```

```python
import functools

import jax
import jax.numpy as jnp
from jax import lax
from jax.experimental import pallas as pl
from jax.experimental.pallas import tpu as pltpu
from jax.sharding import PartitionSpec as P

HEADS = 12
HDIM = 64


def matmul(left, right):
    return jnp.dot(left, right, preferred_element_type=jnp.float32)


def matmul_left(left, right):
    return lax.dot_general(
        left, right, (((0,), (0,)), ((), ())), preferred_element_type=jnp.float32
    )


def matmul_right(left, right):
    return lax.dot_general(
        left, right, (((1,), (1,)), ((), ())), preferred_element_type=jnp.float32
    )


def layer_norm(values, gain, bias):
    centered = values - jnp.mean(values, -1, keepdims=True)
    factor = lax.rsqrt(jnp.mean(centered * centered, -1, keepdims=True) + 1e-05)
    normed = centered * factor
    return (normed * gain + bias, normed, factor)


def norm_back(grad_out, normed, factor, gain):
    scaled = grad_out * gain
    grad_in = factor * (
        scaled
        - jnp.mean(scaled, -1, keepdims=True)
        - normed * jnp.mean(scaled * normed, -1, keepdims=True)
    )
    return (grad_in, jnp.sum(grad_out * normed, 0), jnp.sum(grad_out, 0))


def unit_rows(values):
    factor = lax.rsqrt(jnp.sum(values * values, -1, keepdims=True) + 1e-06)
    return (values * factor, factor)


def unit_back(grad_unit, unit, factor):
    return factor * (grad_unit - unit * jnp.sum(grad_unit * unit, -1, keepdims=True))


def row_logsumexp(values):
    top_value = jnp.max(values, 1, keepdims=True)
    return top_value[:, 0] + jnp.log(jnp.sum(jnp.exp(values - top_value), 1))


def shards(
    images,
    qkv_weight,
    out_weight,
    fc1_weight,
    fc1_bias,
    fc2_weight,
    ln1_gain,
    ln1_bias,
    ln2_gain,
    ln2_bias,
    post_gain,
    post_bias,
    image_proj,
    text_feats,
    text_gain,
    text_bias,
    text_proj,
    log_scale,
    caption_counts,
    positives,
):
    images_here, patches, model_width = images.shape
    row_count = images_here * patches
    resid = images.reshape(row_count, model_width).astype(jnp.float32)
    normed_one, unit_one, factor_one = layer_norm(resid, ln1_gain, ln1_bias)
    normed_in = normed_one.astype(jnp.bfloat16)
    packed = (
        matmul(normed_in, qkv_weight)
        .astype(jnp.bfloat16)
        .reshape(images_here, patches, 3, HEADS, HDIM)
    )
    query, keys, values = (packed[:, :, 0], packed[:, :, 1], packed[:, :, 2])
    scores = 0.125 * jnp.einsum("bqhd,bkhd->bhqk", query, keys, preferred_element_type=jnp.float32)
    score_peak = jnp.max(scores, -1, keepdims=True)
    score_lse = score_peak + jnp.log(jnp.sum(jnp.exp(scores - score_peak), -1, keepdims=True))
    attn_low = jnp.exp(scores - score_lse).astype(jnp.bfloat16)
    mixed = jnp.einsum("bhqk,bkhd->bqhd", attn_low, values, preferred_element_type=jnp.float32)
    mixed = mixed.reshape(row_count, model_width).astype(jnp.bfloat16)
    middle = resid + matmul(mixed, out_weight)
    normed_two, unit_two, factor_two = layer_norm(middle, ln2_gain, ln2_bias)
    normed_mid = normed_two.astype(jnp.bfloat16)
    hidden = matmul(normed_mid, fc1_weight) + fc1_bias
    gate_sig = jax.nn.sigmoid(1.702 * hidden)
    activation = (hidden * gate_sig).astype(jnp.bfloat16)
    block = middle + matmul(activation, fc2_weight)
    block_out = block.reshape(images_here, patches, model_width).astype(jnp.bfloat16)
    class_rows = block.reshape(images_here, patches, model_width)[:, 0, :]
    class_full, unit_post, factor_post = layer_norm(class_rows, post_gain, post_bias)
    class_norm = class_full.astype(jnp.bfloat16)
    image_unit, image_factor = unit_rows(matmul(class_norm, image_proj))
    image_low = image_unit.astype(jnp.bfloat16)
    text_full, unit_text, factor_text = layer_norm(
        text_feats.astype(jnp.float32), text_gain, text_bias
    )
    text_norm = text_full.astype(jnp.bfloat16)
    text_unit, text_factor = unit_rows(matmul(text_norm, text_proj))
    text_low = text_unit.astype(jnp.bfloat16)
    all_images, all_texts = (
        lax.all_gather(image_low, ("dp", "rep"), axis=0, tiled=True),
        lax.all_gather(text_low, ("dp", "rep"), axis=0, tiled=True),
    )
    all_positives = lax.all_gather(positives, ("dp", "rep"), axis=0, tiled=True)
    image_total = all_images.shape[0]
    caption_total = all_texts.shape[0]
    text_ratio = image_total / caption_total
    logit_scale = jnp.exp(log_scale[0])
    image_ids = lax.axis_index(("dp", "rep")) * images_here + jnp.arange(
        images_here, dtype=jnp.int32
    )
    counts = caption_counts.astype(jnp.float32)
    row_logits = logit_scale * matmul_right(image_low, all_texts)
    row_match = (all_positives[None, :] == image_ids[:, None]).astype(jnp.float32)
    row_lse = row_logsumexp(row_logits)
    image_loss = row_lse - jnp.sum(row_match * row_logits, 1) / counts
    col_logits = logit_scale * matmul_right(text_low, all_images)
    col_match = (positives[:, None] == jnp.arange(image_total, dtype=jnp.int32)[None, :]).astype(
        jnp.float32
    )
    col_lse = row_logsumexp(col_logits)
    caption_loss = col_lse - jnp.sum(col_match * col_logits, 1)
    grad_rows = (
        0.5 * (jnp.exp(row_logits - row_lse[:, None]) - row_match / counts[:, None])
    ).astype(jnp.bfloat16)
    grad_cols = (0.5 * text_ratio * (jnp.exp(col_logits - col_lse[:, None]) - col_match)).astype(
        jnp.bfloat16
    )
    total_part = 0.5 * jnp.sum(image_loss) + 0.5 * text_ratio * jnp.sum(caption_loss)
    scale_part = jnp.sum(grad_rows.astype(jnp.float32) * row_logits) + jnp.sum(
        grad_cols.astype(jnp.float32) * col_logits
    )
    total, scale_grad = lax.psum((total_part, scale_part), ("dp", "rep"))
    loss = total / image_total
    grad_log_scale = scale_grad.reshape(1)
    columns = grad_cols
    grad_image_unit = logit_scale * matmul(grad_rows, all_texts) + lax.psum_scatter(
        logit_scale * matmul_left(columns, text_low), ("dp", "rep"), scatter_dimension=0, tiled=True
    )
    columns = grad_rows
    grad_text_unit = logit_scale * matmul(grad_cols, all_images) + lax.psum_scatter(
        logit_scale * matmul_left(columns, image_low),
        ("dp", "rep"),
        scatter_dimension=0,
        tiled=True,
    )
    grad_image_embed = unit_back(grad_image_unit, image_unit, image_factor).astype(jnp.bfloat16)
    grad_image_proj = matmul_left(class_norm, grad_image_embed)
    grad_class, grad_post_gain, grad_post_bias = norm_back(
        matmul_right(grad_image_embed, image_proj), unit_post, factor_post, post_gain
    )
    grad_text_embed = unit_back(grad_text_unit, text_unit, text_factor).astype(jnp.bfloat16)
    grad_text_proj = matmul_left(text_norm, grad_text_embed)
    grad_text_feats, grad_text_gain, grad_text_bias = norm_back(
        matmul_right(grad_text_embed, text_proj), unit_text, factor_text, text_gain
    )
    grad_block = (
        jnp.zeros((images_here, patches, model_width), jnp.float32)
        .at[:, 0, :]
        .set(grad_class)
        .reshape(row_count, model_width)
    )
    grad_block_low = grad_block.astype(jnp.bfloat16)
    grad_activation = matmul_right(grad_block_low, fc2_weight)
    grad_hidden = (
        grad_activation * (gate_sig + 1.702 * hidden * gate_sig * (1.0 - gate_sig))
    ).astype(jnp.bfloat16)
    grad_fc1_bias = jnp.sum(grad_hidden.astype(jnp.float32), 0)
    grad_mid_norm, grad_ln2_gain, grad_ln2_bias = norm_back(
        matmul_right(grad_hidden, fc1_weight), unit_two, factor_two, ln2_gain
    )
    grad_middle = grad_block + grad_mid_norm
    grad_middle_low = grad_middle.astype(jnp.bfloat16)
    grad_out_weight = matmul_left(mixed, grad_middle_low)
    grad_mixed = (
        matmul_right(grad_middle_low, out_weight)
        .astype(jnp.bfloat16)
        .reshape(images_here, patches, HEADS, HDIM)
    )
    again_scores = 0.125 * jnp.einsum(
        "bqhd,bkhd->bhqk", query, keys, preferred_element_type=jnp.float32
    )
    attn_full = jnp.exp(again_scores - score_lse)
    grad_values = jnp.einsum(
        "bhqk,bqhd->bkhd", attn_low, grad_mixed, preferred_element_type=jnp.float32
    )
    grad_attn = jnp.einsum(
        "bqhd,bkhd->bhqk", grad_mixed, values, preferred_element_type=jnp.float32
    )
    grad_scores = (
        attn_full * (grad_attn - jnp.sum(grad_attn * attn_full, -1, keepdims=True))
    ).astype(jnp.bfloat16)
    grad_query = 0.125 * jnp.einsum(
        "bhqk,bkhd->bqhd", grad_scores, keys, preferred_element_type=jnp.float32
    )
    grad_keys = 0.125 * jnp.einsum(
        "bhqk,bqhd->bkhd", grad_scores, query, preferred_element_type=jnp.float32
    )
    grad_packed = (
        jnp.stack([grad_query, grad_keys, grad_values], 2)
        .reshape(row_count, 3 * model_width)
        .astype(jnp.bfloat16)
    )
    grad_qkv_weight = matmul_left(normed_in, grad_packed)
    grad_in_norm, grad_ln1_gain, grad_ln1_bias = norm_back(
        matmul_right(grad_packed, qkv_weight), unit_one, factor_one, ln1_gain
    )
    grad_images = (grad_middle + grad_in_norm).reshape(images_here, patches, model_width)
    grad_fc2_weight = matmul_left(activation, grad_block_low)
    grad_fc1_weight = matmul_left(normed_mid, grad_hidden)
    first_qkv, first_out, first_fc1, first_fc2, first_image, first_text = (
        lax.psum_scatter(grad_qkv_weight, "dp", scatter_dimension=1, tiled=True),
        lax.psum_scatter(grad_out_weight, "dp", scatter_dimension=1, tiled=True),
        lax.psum_scatter(grad_fc1_weight, "dp", scatter_dimension=1, tiled=True),
        lax.psum_scatter(grad_fc2_weight, "dp", scatter_dimension=1, tiled=True),
        lax.psum_scatter(grad_image_proj, "dp", scatter_dimension=1, tiled=True),
        lax.psum_scatter(grad_text_proj, "dp", scatter_dimension=1, tiled=True),
    )
    summed_qkv, summed_out, summed_fc1, summed_fc2, summed_image, summed_text = (
        lax.psum_scatter(first_qkv, "rep", scatter_dimension=0, tiled=True),
        lax.psum_scatter(first_out, "rep", scatter_dimension=0, tiled=True),
        lax.psum_scatter(first_fc1, "rep", scatter_dimension=0, tiled=True),
        lax.psum_scatter(first_fc2, "rep", scatter_dimension=0, tiled=True),
        lax.psum_scatter(first_image, "rep", scatter_dimension=0, tiled=True),
        lax.psum_scatter(first_text, "rep", scatter_dimension=0, tiled=True),
    )
    vector_sums = lax.psum(
        (
            grad_ln1_gain,
            grad_ln1_bias,
            grad_ln2_gain,
            grad_ln2_bias,
            grad_fc1_bias,
            grad_post_gain,
            grad_post_bias,
            grad_text_gain,
            grad_text_bias,
        ),
        ("dp", "rep"),
    )
    return (
        block_out,
        loss,
        grad_images,
        summed_qkv,
        summed_out,
        summed_fc1,
        vector_sums[4],
        summed_fc2,
        vector_sums[0],
        vector_sums[1],
        vector_sums[2],
        vector_sums[3],
        vector_sums[5],
        vector_sums[6],
        summed_image,
        grad_text_feats,
        vector_sums[7],
        vector_sums[8],
        summed_text,
        grad_log_scale,
    )


MESH = pl.DeviceIdType.MESH
F32 = jnp.float32
BF16 = jnp.bfloat16
PATCHES = 50
WIDTH = 768
HIDDEN = 3072
EMBED = 512
GROUP = 8
STEP = 160


def fits(dp_size, rep_size):
    return dp_size == 4 and rep_size == 8


def dot_rows(left, right):
    return lax.dot_general(left, right, (((1,), (1,)), ((), ())), preferred_element_type=F32)


def dot_cols(left, right):
    return lax.dot_general(left, right, (((0,), (0,)), ((), ())), preferred_element_type=F32)


def lane_shift(values, amount):
    width = values.shape[1]
    amount = amount % width
    return values if amount == 0 else pltpu.roll(values, width - amount, 1)


def pick_blocks(values, side, sides, block, count):
    lanes = block * count
    place = lax.broadcasted_iota(jnp.int32, (values.shape[0], lanes), 1) // block
    picked = lane_shift(values, side * block)[:, :lanes]
    for index in range(1, count):
        offset = (side + index * sides) * block - index * block
        picked = jnp.where(place == index, lane_shift(values, offset)[:, :lanes], picked)
    return picked


def head_spread(rows):
    count = rows.shape[0]
    lane_head = lax.broadcasted_iota(jnp.int32, (HEADS, count, WIDTH), 2) // HDIM
    head = lax.broadcasted_iota(jnp.int32, (HEADS, count, WIDTH), 0)
    spread = jnp.where(lane_head == head, rows[None], 0.0)
    return spread.reshape(HEADS * count, WIDTH)


def head_gather(stacked):
    count = stacked.shape[0] // HEADS
    stacked = stacked.reshape(HEADS, count, WIDTH)
    lane_head = lax.broadcasted_iota(jnp.int32, stacked.shape, 2) // HDIM
    head = lax.broadcasted_iota(jnp.int32, stacked.shape, 0)
    return jnp.sum(jnp.where(lane_head == head, stacked, 0.0), 0)


def fused_kernel(dims, counter, *refs):
    (
        x, qkv_hbm, out_hbm, fc1_hbm, fc2_hbm, ip_hbm, tp_hbm, fc1_bias,
        ln1_gain, ln1_bias, ln2_gain, ln2_bias, post_gain, post_bias,
        text_feats, text_gain, text_bias, log_scale, caption_counts, positives,
        block_out, grad_images, g_qkv, g_out, g_fc1, g_fc2, g_ip, g_text, g_tp, g_vec,
        qkv, w_out, fc1, fc2, ip, tp,
        ni, kv, qd, mixed, middle, nmd, ff_acc, gni,
        attn, attn_low, gsp, uu,
        hid_c, small,
        t_all, pos_all, i_all, cnt_all, row_sum, col_sum,
        gi_send, gi_recv, gt_send, gt_recv,
        nm_full, gb_full, rf_out, rf_in, ro_out, ro_in, tn_out, tn_in,
        co_out, co_in, te_out, te_in, ps_send, ps_recv, pt_send, pt_recv,
        vec_z, vec_p, hid_s, act_s, gh_s, nm_sel,
        local_sem, send_sem, recv_sem,
    ) = refs
    images_here, captions_here, planes, sides, dp_size = dims
    plane_size = dp_size * sides
    rep_size = planes * sides
    rows_all = images_here * PATCHES
    half = rows_all // 2
    dp = lax.axis_index("dp")
    rep = lax.axis_index("rep")
    z = rep // sides
    side = lax.rem(rep, sides)
    slot = dp * sides + side
    plane_images = plane_size * images_here
    line_captions = planes * captions_here
    image_total = plane_images * planes
    caption_total = line_captions * plane_size
    text_ratio = image_total / caption_total

    used = [0]

    def plane_peer(step):
        peer = lax.rem(slot + step, plane_size)
        return peer, (peer // sides, z * sides + lax.rem(peer, sides))

    def line_peer(step):
        peer = lax.rem(z + step, planes)
        return peer, (dp, peer * sides + side)

    def copy_to(source, target, device):
        index = used[0]
        used[0] += 1
        return pltpu.make_async_remote_copy(
            src_ref=source, dst_ref=target, send_sem=send_sem.at[index], recv_sem=recv_sem.at[index],
            device_id=device, device_id_type=MESH,
        )

    def to_plane(source_of, target):
        copies = []
        for step in range(1, plane_size):
            peer, device = plane_peer(step)
            copies.append(copy_to(source_of(peer), target, device))
        for copy in copies:
            copy.start()
        return copies

    def to_line(source_of, target):
        copies = []
        for step in range(1, planes):
            peer, device = line_peer(step)
            copies.append(copy_to(source_of(peer), target, device))
        for copy in copies:
            copy.start()
        return copies

    def finish(copies):
        for copy in copies:
            copy.wait()

    loads = []
    for index, (source, target) in enumerate(
        ((tp_hbm, tp), (qkv_hbm, qkv), (out_hbm, w_out), (fc1_hbm, fc1), (fc2_hbm, fc2), (ip_hbm, ip))
    ):
        load = pltpu.make_async_copy(source, target, local_sem.at[index])
        load.start()
        loads.append(load)

    barrier = pltpu.get_barrier_semaphore()
    for step in range(1, plane_size):
        pl.semaphore_signal(barrier, inc=1, device_id=plane_peer(step)[1], device_id_type=MESH)
    for step in range(1, planes):
        pl.semaphore_signal(barrier, inc=1, device_id=line_peer(step)[1], device_id_type=MESH)

    text_full, _, _ = layer_norm(text_feats[...].astype(F32), text_gain[...], text_bias[...])
    text_norm = text_full.astype(BF16)
    loads[0].wait()
    text_unit, text_factor = unit_rows(matmul(text_norm, tp[...]))
    t_all[z] = text_unit.astype(BF16)
    pos_rows = jnp.broadcast_to(positives[...].astype(F32), (128, captions_here))
    pos_all[z] = jnp.transpose(pos_rows)
    cnt_rows = jnp.broadcast_to(caption_counts[...].astype(F32), (128, images_here))
    cnt_all[slot] = jnp.transpose(cnt_rows)
    pl.semaphore_wait(barrier, plane_size - 1 + planes - 1)
    text_copies = to_line(lambda peer: t_all.at[z], t_all.at[z])
    pos_copies = to_line(lambda peer: pos_all.at[z], pos_all.at[z])
    cnt_copies = to_plane(lambda peer: cnt_all.at[slot], cnt_all.at[slot])

    def norm_in(step, _):
        rows = pl.ds(pl.multiple_of(step * STEP, STEP), STEP)
        full, _, _ = layer_norm(x[rows, :].astype(F32), ln1_gain[...], ln1_bias[...])
        full = full.reshape(STEP // 16, 2, GROUP, WIDTH)
        for part in range(2):
            to = pl.ds(pl.multiple_of(part * half + step * (STEP // 2), 16), STEP // 2)
            ni[to, :] = full[:, part].reshape(STEP // 2, WIDTH).astype(BF16)
        return 0

    lax.fori_loop(0, rows_all // STEP, norm_in, 0)

    loads[1].wait()

    def keys_values(step, _):
        source = pl.ds(pl.multiple_of(WIDTH + step * 256, 256), 256)
        to = pl.ds(pl.multiple_of(step * 256, 256), 256)
        kv[:, to] = matmul(ni[...], qkv[:, source]).astype(BF16)
        return 0

    lax.fori_loop(0, 2 * WIDTH // 256, keys_values, 0)

    resid_c = x[0:images_here, :].astype(F32)
    normed_c = layer_norm(resid_c, ln1_gain[...], ln1_bias[...])[0].astype(BF16)
    query_c = matmul(normed_c, qkv[:, 0:WIDTH]).astype(BF16)
    query_spread = head_spread(query_c.astype(F32)).astype(BF16)
    scores = 0.125 * dot_rows(query_spread, kv[:, 0:WIDTH])
    row_image = lax.rem(lax.broadcasted_iota(jnp.int32, scores.shape, 0), images_here)
    column = lax.broadcasted_iota(jnp.int32, scores.shape, 1)
    column_image = jnp.where(column < half, 0, GROUP) + lax.rem(column, GROUP)
    scores = jnp.where(row_image == column_image, scores, -1e30)
    weights = jnp.exp(scores - jnp.max(scores, 1, keepdims=True))
    weights = weights * (1.0 / jnp.sum(weights, 1, keepdims=True))
    attn[...] = weights
    attn_low[...] = weights.astype(BF16)
    mixed_c = head_gather(matmul(attn_low[...], kv[:, WIDTH:]))
    loads[2].wait()
    middle_c = resid_c + matmul(mixed_c.astype(BF16), w_out[...])
    full, unit_two, factor_two = layer_norm(middle_c, ln2_gain[...], ln2_bias[...])
    nm_full[z, slot] = full.astype(BF16)
    nm_line = to_line(lambda peer: nm_full.at[z, slot], nm_full.at[z, slot])
    loads[3].wait()
    hid_c[...] = matmul(full.astype(BF16), fc1[...]) + fc1_bias[...]
    act_c = (hid_c[...] * jax.nn.sigmoid(1.702 * hid_c[...])).astype(BF16)
    loads[4].wait()
    block_c = middle_c + matmul(act_c, fc2[...])
    full, unit_post, factor_post = layer_norm(block_c, post_gain[...], post_bias[...])
    class_norm = full.astype(BF16)
    loads[5].wait()
    image_unit, image_factor = unit_rows(matmul(class_norm, ip[...]))
    i_all[slot] = image_unit.astype(BF16)
    image_copies = to_plane(lambda peer: i_all.at[slot], i_all.at[slot])
    small[0] = unit_two
    small[1] = unit_post

    value_rows = matmul(attn_low[...], ni[...])
    normed_cf = normed_c.astype(F32)
    block_lanes = WIDTH // rep_size
    text_lanes = EMBED // rep_size
    for to_side in range(sides):
        picked = pick_blocks(value_rows, to_side, sides, block_lanes, planes).astype(BF16)
        rf_out[to_side, 2 * HEADS : 3 * HEADS] = picked.reshape(HEADS, images_here, planes * block_lanes)
        picked = pick_blocks(normed_cf, to_side, sides, block_lanes, planes).astype(BF16)
        rf_out[to_side, 0:HEADS] = jnp.broadcast_to(picked[None], (HEADS, images_here, planes * block_lanes))
        ro_out[to_side, 0] = pick_blocks(mixed_c, to_side, sides, block_lanes, planes).astype(BF16)
        ro_out[to_side, 1] = pick_blocks(full, to_side, sides, block_lanes, planes).astype(BF16)
        tn_out[to_side] = pick_blocks(text_full, to_side, sides, text_lanes, planes).astype(BF16)

    heads_here = 3 * HEADS // dp_size
    bundle = heads_here // 3
    rf_copies = []
    for step in range(1, plane_size):
        peer, device = plane_peer(step)
        for part in range(3):
            first = (peer // sides) * heads_here + part * bundle
            mine = dp * heads_here + part * bundle
            copy = copy_to(
                rf_out.at[lax.rem(peer, sides), pl.ds(first, bundle)],
                rf_in.at[pl.ds(part * bundle, bundle), slot], device,
            )
            is_keys = (first >= HEADS) & (first < 2 * HEADS)
            mine_keys = (mine >= HEADS) & (mine < 2 * HEADS)
            rf_copies.append((copy, is_keys, mine_keys))

    for copy, is_keys, _ in rf_copies:
        pl.when(jnp.logical_not(is_keys))(copy.start)
    ro_copies = to_plane(lambda peer: ro_out.at[lax.rem(peer, sides)], ro_in.at[:, slot])
    tn_copies = to_plane(lambda peer: tn_out.at[lax.rem(peer, sides)], tn_in.at[slot])

    def dense_query():
        def piece(step, _):
            columns = pl.ds(pl.multiple_of(step * 256, 256), 256)
            qd[:, columns] = (0.125 * matmul(ni[...], qkv[:, columns]).astype(BF16).astype(F32)).astype(BF16)
            return 0

        lax.fori_loop(0, WIDTH // 256, piece, 0)

    def dense_attention(first, last):
        def piece(index, _):
            part = index // (HEADS // 2)
            pair = lax.rem(index, HEADS // 2)
            rows = pl.ds(pl.multiple_of(part * half, 16), half)
            lanes = pl.ds(pl.multiple_of(pair * 128, 128), 128)
            value_lanes = pl.ds(pl.multiple_of(WIDTH + pair * 128, 128), 128)
            query = qd[rows, lanes]
            keys = kv[rows, lanes]
            values = kv[rows, value_lanes]
            lane = lax.broadcasted_iota(jnp.int32, (half, 128), 1)
            row_of = lax.rem(lax.broadcasted_iota(jnp.int32, (half, half), 0), GROUP)
            col_of = lax.rem(lax.broadcasted_iota(jnp.int32, (half, half), 1), GROUP)
            same = row_of == col_of
            result = None
            for which in range(2):
                own = (lane < HDIM) if which == 0 else (lane >= HDIM)
                logits = dot_rows(jnp.where(own, query, jnp.zeros_like(query)), keys)
                logits = jnp.where(same, logits, -1e30)
                top = jnp.exp(logits - jnp.max(logits, 1, keepdims=True))
                top = top * (1.0 / jnp.sum(top, 1, keepdims=True))
                got = matmul(top.astype(BF16), values)
                result = got if which == 0 else jnp.where(own, got, result)
            mixed[rows, lanes] = result.astype(BF16)
            return 0

        lax.fori_loop(first, last, piece, 0)

    def dense_out():
        def piece(step, _):
            parts = []
            for part in range(2):
                rows = pl.ds(pl.multiple_of(part * half + step * (STEP // 2), 16), STEP // 2)
                parts.append(matmul(mixed[rows, :], w_out[...]).reshape(STEP // 16, GROUP, WIDTH))
            joined = jnp.stack(parts, 1).reshape(STEP, WIDTH)
            rows = pl.ds(pl.multiple_of(step * STEP, STEP), STEP)
            value = x[rows, :].astype(F32) + joined
            middle[rows, :] = value
            nmd[rows, :] = layer_norm(value, ln2_gain[...], ln2_bias[...])[0].astype(BF16)
            return 0

        lax.fori_loop(0, rows_all // STEP, piece, 0)

    def dense_ff():
        def outer(part, _):
            rows = pl.ds(pl.multiple_of(part * half, 16), half)
            ff_acc[...] = middle[rows, :]

            def inner(step, _):
                columns = pl.ds(pl.multiple_of(step * 768, 768), 768)
                hidden = matmul(nmd[rows, :], fc1[:, columns]) + fc1_bias[:, columns]
                act = (hidden * jax.nn.sigmoid(1.702 * hidden)).astype(BF16)
                ff_acc[...] += matmul(act, fc2[columns, :])
                return 0

            lax.fori_loop(0, HIDDEN // 768, inner, 0)
            block_out[rows, :] = ff_acc[...].astype(BF16)
            return 0

        lax.fori_loop(0, 2, outer, 0)

    dense_query()

    finish(text_copies)
    finish(pos_copies)
    finish(cnt_copies)
    finish(image_copies)
    scale = jnp.exp(log_scale[...])
    images_low = i_all[...].reshape(plane_images, EMBED)
    texts_low = t_all[...].reshape(line_captions, EMBED)
    logits = scale * dot_rows(images_low, texts_low)
    logits_t = scale * dot_rows(texts_low, images_low)

    def image_ids(dim, shape):
        index = lax.broadcasted_iota(jnp.int32, shape, dim)
        holder = index // images_here
        owner = (holder // sides) * rep_size + z * sides + lax.rem(holder, sides)
        return (owner * images_here + lax.rem(index, images_here)).astype(F32)

    pos_col = pos_all[...].reshape(line_captions, 128)
    match_t = (pos_col[:, 0:1] == image_ids(1, logits_t.shape)).astype(F32)
    match = (jnp.transpose(pos_col) == image_ids(0, logits.shape)).astype(F32)
    counts = jnp.transpose(cnt_all[...].reshape(plane_images, 128))[0:1, :]
    row_sum[slot] = jnp.broadcast_to(jnp.sum(jnp.exp(logits_t), 0, keepdims=True), (8, plane_images))
    col_sum[z] = jnp.broadcast_to(jnp.sum(jnp.exp(logits), 0, keepdims=True), (8, line_captions))
    sum_copies = to_plane(lambda peer: row_sum.at[slot], row_sum.at[slot])
    sum_copies += to_line(lambda peer: col_sum.at[z], col_sum.at[z])

    finish(nm_line)
    nm_plane = to_plane(lambda peer: nm_full.at[:, slot], nm_full.at[:, slot])
    dense_attention(0, 3)

    finish(sum_copies)
    row_lse = jnp.log(jnp.sum(row_sum[...], 0)[0:1])
    col_lse = jnp.log(jnp.sum(col_sum[...], 0)[0:1])
    grad_cols = (0.5 * text_ratio * (jnp.exp(logits - col_lse) - match)).astype(BF16)
    grad_rows_t = (0.5 * (jnp.exp(logits_t - row_lse) - match_t / counts)).astype(BF16)
    loss_part = 0.5 * (jnp.sum(row_lse) / plane_size - jnp.sum(match_t * logits_t / counts)) + (
        0.5 * text_ratio
    ) * (jnp.sum(col_lse) / planes - jnp.sum(match * logits))
    scale_part = jnp.sum(grad_cols.astype(F32) * logits) + jnp.sum(grad_rows_t.astype(F32) * logits_t)
    gi_send[...] = (scale * (dot_cols(grad_rows_t, texts_low) + matmul(grad_cols, texts_low))).reshape(
        plane_size, images_here, EMBED
    )
    gi_copies = to_plane(lambda peer: gi_send.at[peer], gi_recv.at[slot])
    gi_recv[slot] = gi_send[slot]
    gt_send[...] = (scale * (dot_cols(grad_cols, images_low) + matmul(grad_rows_t, images_low))).reshape(
        planes, captions_here, EMBED
    )
    gt_copies = to_line(lambda peer: gt_send.at[peer], gt_recv.at[z])
    gt_recv[z] = gt_send[z]

    dense_attention(3, 6)

    finish(gi_copies)
    grad_embed = unit_back(jnp.sum(gi_recv[...], 0), image_unit, image_factor).astype(BF16)
    grad_class, g_post_gain, g_post_bias = norm_back(
        dot_rows(grad_embed, ip[...]), small[1], factor_post, post_gain[...]
    )
    gb_low = grad_class.astype(BF16)
    gb_full[z, slot] = gb_low
    gb_line = to_line(lambda peer: gb_full.at[z, slot], gb_full.at[z, slot])
    gate = jax.nn.sigmoid(1.702 * hid_c[...])
    grad_hidden = (
        dot_rows(gb_low, fc2[...]) * (gate + 1.702 * hid_c[...] * gate * (1.0 - gate))
    ).astype(BF16)
    g_fc1_bias = jnp.sum(grad_hidden.astype(F32), 0, keepdims=True)
    grad_two, g_ln2_gain, g_ln2_bias = norm_back(
        dot_rows(grad_hidden, fc1[...]), small[0], factor_two, ln2_gain[...]
    )
    grad_middle = grad_class + grad_two
    grad_middle_low = grad_middle.astype(BF16)
    grad_mixed = dot_rows(grad_middle_low, w_out[...]).astype(BF16)
    mixed_spread = head_spread(grad_mixed.astype(F32)).astype(BF16)
    grad_attn = dot_rows(mixed_spread, kv[:, WIDTH:])
    weights = attn[...]
    grad_scores = weights * (grad_attn - jnp.sum(grad_attn * weights, 1, keepdims=True))
    grad_scores = 0.125 * grad_scores.astype(BF16).astype(F32)
    gsp[0 : HEADS * images_here] = grad_scores.astype(BF16)
    gsp[HEADS * images_here :] = attn_low[...]
    score_low = gsp[0 : HEADS * images_here]
    grad_query = head_gather(matmul(score_low, kv[:, 0:WIDTH])).astype(BF16)
    key_rows = matmul(score_low, ni[...])
    for to_side in range(sides):
        picked = pick_blocks(key_rows, to_side, sides, block_lanes, planes).astype(BF16)
        rf_out[to_side, HEADS : 2 * HEADS] = picked.reshape(HEADS, images_here, planes * block_lanes)

    grad_q = grad_query.astype(F32)
    query_f = query_c.astype(F32)
    grad_v = grad_mixed.astype(F32)
    lane = lax.broadcasted_iota(jnp.int32, (images_here, 128), 1)
    q_shift, k_shift, v_shift = lane_shift(grad_q, 64), lane_shift(query_f, -64), lane_shift(grad_v, 64)
    m_shift = lane_shift(grad_middle_low.astype(F32), 64)
    m_plain = grad_middle_low.astype(F32)
    co_out[0, :, 0:576] = grad_q[:, 0:576].astype(BF16)
    co_out[1, :, 0:128] = q_shift[:, 512:640].astype(BF16)
    co_out[1, :, 128:256] = jnp.where(lane < 64, q_shift[:, 640:768], k_shift[:, 0:128]).astype(BF16)
    co_out[1, :, 256:576] = k_shift[:, 128:448].astype(BF16)
    co_out[2, :, 0:384] = query_f[:, 384:768].astype(BF16)
    co_out[2, :, 384:576] = grad_v[:, 0:192].astype(BF16)
    co_out[3, :, 0:576] = v_shift[:, 128:704].astype(BF16)
    for to_dp, source in enumerate((m_plain[:, 0:192], m_shift[:, 128:320], m_plain[:, 384:576], m_shift[:, 512:704])):
        co_out[to_dp, :, 640:832] = source.astype(BF16)
        co_out[to_dp, :, 896:1024] = grad_embed[:, to_dp * 128 : to_dp * 128 + 128]
    co_copies = to_plane(lambda peer: co_out.at[peer // sides], co_in.at[slot])
    for copy, is_keys, _ in rf_copies:
        pl.when(is_keys)(copy.start)
    own_rf = pltpu.make_async_copy(
        rf_out.at[side, pl.ds(dp * heads_here, heads_here)], rf_in.at[:, slot], local_sem.at[6]
    )
    own_rf.start()
    co_in[slot] = co_out[dp]
    ro_in[:, slot] = ro_out[side]
    tn_in[slot] = tn_out[side]

    finish(gt_copies)
    grad_text = unit_back(jnp.sum(gt_recv[...], 0), text_unit, text_factor).astype(BF16)
    for to_dp in range(dp_size):
        te_out[to_dp] = grad_text[:, to_dp * 128 : to_dp * 128 + 128]
    te_copies = to_plane(lambda peer: te_out.at[peer // sides], te_in.at[slot])
    te_in[slot] = te_out[dp]
    _, unit_text, factor_text = layer_norm(text_feats[...].astype(F32), text_gain[...], text_bias[...])
    g_feats, g_text_gain, g_text_bias = norm_back(
        dot_rows(grad_text, tp[...]), unit_text, factor_text, text_gain[...]
    )
    g_text[...] = g_feats

    finish(gb_line)
    gb_plane = to_plane(lambda peer: gb_full.at[:, slot], gb_full.at[:, slot])

    uu[0 : HEADS * images_here] = dot_rows(query_spread, qkv[:, WIDTH : 2 * WIDTH]).astype(BF16)
    uu[HEADS * images_here :] = dot_rows(mixed_spread, qkv[:, 2 * WIDTH :]).astype(BF16)
    class_in = dot_rows(grad_query, qkv[:, 0:WIDTH])

    def spread_back(step, _):
        columns = pl.ds(pl.multiple_of(step * 256, 256), 256)
        gni[:, columns] = dot_cols(gsp[...], uu[:, columns])
        return 0

    lax.fori_loop(0, WIDTH // 256, spread_back, 0)
    gni[0:GROUP] += class_in[0:GROUP]
    gni[half : half + GROUP] += class_in[GROUP:]

    def norm_one_back(step, sums):
        rows = pl.ds(pl.multiple_of(step * STEP, STEP), STEP)
        _, unit, factor = layer_norm(x[rows, :].astype(F32), ln1_gain[...], ln1_bias[...])
        parts = []
        for part in range(2):
            source = pl.ds(pl.multiple_of(part * half + step * (STEP // 2), 16), STEP // 2)
            parts.append(gni[source, :].reshape(STEP // 16, GROUP, WIDTH))
        grad_out = jnp.stack(parts, 1).reshape(STEP, WIDTH)
        grad_in, gain_part, bias_part = norm_back(grad_out, unit, factor, ln1_gain[...])
        grad_images[rows, :] = grad_in
        return (sums[0] + gain_part[None], sums[1] + bias_part[None])

    zero = jnp.zeros((1, WIDTH), F32)
    g_ln1_gain, g_ln1_bias = lax.fori_loop(0, rows_all // STEP, norm_one_back, (zero, zero))
    grad_images[0:images_here] += grad_middle

    vectors = (
        g_ln1_gain, g_ln1_bias, g_ln2_gain[None], g_ln2_bias[None], g_post_gain[None], g_post_bias[None],
        g_text_gain[None], g_text_bias[None],
    )
    for index, vector in enumerate(vectors):
        vec_z[z, index : index + 1, 0 : vector.shape[1]] = vector
        vec_z[z, index : index + 1, WIDTH:] = g_fc1_bias[:, index * 384 : index * 384 + 384]
    lane = lax.broadcasted_iota(jnp.int32, (2, 256), 1)
    row = lax.broadcasted_iota(jnp.int32, (2, 256), 0)
    vec_z[z, 6:8, EMBED:WIDTH] = jnp.where((lane == 0) & (row == 0), loss_part, 0.0) + jnp.where(
        (lane == 0) & (row == 1), scale_part, 0.0
    )
    vec_line = to_line(lambda peer: vec_z.at[z], vec_z.at[z])

    own_rf.wait()
    for copy, is_keys, mine_keys in rf_copies:
        copy.wait()
    finish(co_copies)
    columns_in = co_in[...].reshape(plane_images, 1024)
    lane = lax.broadcasted_iota(jnp.int32, (planes * block_lanes, 128), 1)
    for tile in range(5):
        right = columns_in[:, tile * 128 : tile * 128 + 128]
        got = dot_cols(rf_in[2 * tile].reshape(plane_images, planes * block_lanes), right)
        if 2 * tile + 1 < heads_here:
            other = dot_cols(rf_in[2 * tile + 1].reshape(plane_images, planes * block_lanes), right)
            got = jnp.where(lane < HDIM, got, other)
        ps_send[:, :, tile * 128 : tile * 128 + 128] = got.astype(BF16).reshape(planes, block_lanes, 128)
    finish(ro_copies)
    got = dot_cols(ro_in[0].reshape(plane_images, planes * block_lanes), columns_in[:, 640:896])
    ps_send[:, :, 640:896] = got.astype(BF16).reshape(planes, block_lanes, 256)
    got = dot_cols(ro_in[1].reshape(plane_images, planes * block_lanes), columns_in[:, 896:1024])
    ps_send[:, :, 896:1024] = got.astype(BF16).reshape(planes, block_lanes, 128)
    ps_copies = to_line(lambda peer: ps_send.at[peer], ps_recv.at[z])
    ps_recv[z] = ps_send[z]
    finish(tn_copies)
    finish(te_copies)
    got = dot_cols(
        tn_in[...].reshape(plane_size * captions_here, planes * text_lanes),
        te_in[...].reshape(plane_size * captions_here, 128),
    )
    pt_send[...] = got.astype(BF16).reshape(planes, text_lanes, 128)
    pt_copies = to_line(lambda peer: pt_send.at[peer], pt_recv.at[z])
    pt_recv[z] = pt_send[z]

    finish(vec_line)
    vec_p[slot] = jnp.sum(vec_z[...], 0)
    vec_plane = to_plane(lambda peer: vec_p.at[slot], vec_p.at[slot])

    finish(nm_plane)
    all_rows = plane_images * planes
    nm_rows = nm_full[...].reshape(all_rows, WIDTH)
    my_columns = pl.ds(pl.multiple_of(dp * (HIDDEN // dp_size), 128), HIDDEN // dp_size)
    my_rows = pl.ds(pl.multiple_of(rep * (HIDDEN // rep_size), 128), HIDDEN // rep_size)
    hid_s[...] = matmul(nm_rows, fc1[:, my_columns]) + fc1_bias[:, my_columns]
    hidden = matmul(nm_rows, fc1[:, my_rows]) + fc1_bias[:, my_rows]
    act_s[...] = (hidden * jax.nn.sigmoid(1.702 * hidden)).astype(BF16)
    source = lax.broadcasted_iota(jnp.int32, (WIDTH, 128), 0)
    place = lax.broadcasted_iota(jnp.int32, (WIDTH, 128), 1)
    chosen = jnp.where((source == place + rep * block_lanes) & (place < block_lanes), 1.0, 0.0).astype(BF16)
    nm_sel[...] = matmul(nm_rows, chosen).astype(BF16)
    finish(gb_plane)
    gb_rows = gb_full[...].reshape(all_rows, WIDTH)
    gate = jax.nn.sigmoid(1.702 * hid_s[...])
    gh_s[...] = (
        dot_rows(gb_rows, fc2[my_columns, :]) * (gate + 1.702 * hid_s[...] * gate * (1.0 - gate))
    ).astype(BF16)
    g_fc1[...] = dot_cols(nm_sel[...], gh_s[...])[0:block_lanes]
    out_lanes = WIDTH // dp_size
    source = lax.broadcasted_iota(jnp.int32, (WIDTH, 256), 0)
    place = lax.broadcasted_iota(jnp.int32, (WIDTH, 256), 1)
    chosen = jnp.where((source == place + dp * out_lanes) & (place < out_lanes), 1.0, 0.0).astype(BF16)
    g_fc2[...] = dot_cols(matmul(gb_rows, chosen).astype(BF16), act_s[...])[0:out_lanes]

    dense_attention(6, 12)
    dense_out()
    dense_ff()

    finish(vec_plane)
    g_vec[...] = jnp.sum(vec_p[...], 0)
    finish(ps_copies)
    summed = jnp.sum(ps_recv[...].astype(F32), 0)
    g_qkv[...] = summed[:, 0:576]
    g_out[...] = summed[:, 640:832]
    g_ip[...] = summed[:, 896:1024]
    finish(pt_copies)
    g_tp[...] = jnp.sum(pt_recv[...].astype(F32), 0)
    assert used[0] <= counter


def fused_shards(
    dp_size,
    rep_size,
    images,
    qkv_weight,
    out_weight,
    fc1_weight,
    fc1_bias,
    fc2_weight,
    ln1_gain,
    ln1_bias,
    ln2_gain,
    ln2_bias,
    post_gain,
    post_bias,
    image_proj,
    text_feats,
    text_gain,
    text_bias,
    text_proj,
    log_scale,
    caption_counts,
    positives,
):
    images_here, patches, width = images.shape
    captions_here = text_feats.shape[0]
    sides = 2
    planes = rep_size // sides
    plane_size = dp_size * sides
    rows_all = images_here * patches
    heads_here = 3 * HEADS // dp_size
    block = WIDTH // rep_size
    text_block = EMBED // rep_size
    spread = HEADS * images_here
    line = planes * captions_here
    total_images = plane_size * planes * images_here
    copies = 192
    vmem = pl.BlockSpec(memory_space=pltpu.VMEM)
    hbm = pl.BlockSpec(memory_space=pl.ANY)

    def f32(*shape):
        return pltpu.VMEM(shape, F32)

    def b16(*shape):
        return pltpu.VMEM(shape, BF16)

    out_shapes = (
        ((rows_all, WIDTH), BF16),
        ((rows_all, WIDTH), F32),
        ((block, 3 * WIDTH // dp_size), F32),
        ((block, WIDTH // dp_size), F32),
        ((block, HIDDEN // dp_size), F32),
        ((WIDTH // dp_size, HIDDEN // rep_size), F32),
        ((block, EMBED // dp_size), F32),
        ((captions_here, EMBED), F32),
        ((text_block, EMBED // dp_size), F32),
        ((8, 1152), F32),
    )
    scratch = [
        b16(WIDTH, 3 * WIDTH), b16(WIDTH, WIDTH), b16(WIDTH, HIDDEN), b16(HIDDEN, WIDTH),
        b16(WIDTH, EMBED), b16(EMBED, EMBED),
        b16(rows_all, WIDTH), b16(rows_all, 2 * WIDTH), b16(rows_all, WIDTH), b16(rows_all, WIDTH),
        f32(rows_all, WIDTH), b16(rows_all, WIDTH), f32(rows_all // 2, WIDTH), f32(rows_all, WIDTH),
        f32(spread, rows_all), b16(spread, rows_all), b16(2 * spread, rows_all), b16(2 * spread, WIDTH),
        f32(images_here, HIDDEN), f32(2, images_here, WIDTH),
        b16(planes, captions_here, EMBED), f32(planes, captions_here, 128),
        b16(plane_size, images_here, EMBED), f32(plane_size, images_here, 128),
        f32(plane_size, 8, plane_size * images_here), f32(planes, 8, line),
        f32(plane_size, images_here, EMBED), f32(plane_size, images_here, EMBED),
        f32(planes, captions_here, EMBED), f32(planes, captions_here, EMBED),
        b16(planes, plane_size, images_here, WIDTH), b16(planes, plane_size, images_here, WIDTH),
        b16(sides, 3 * HEADS, images_here, planes * block),
        b16(heads_here, plane_size, images_here, planes * block),
        b16(sides, 2, images_here, planes * block), b16(2, plane_size, images_here, planes * block),
        b16(sides, captions_here, planes * text_block), b16(plane_size, captions_here, planes * text_block),
        b16(dp_size, images_here, 1024), b16(plane_size, images_here, 1024),
        b16(dp_size, captions_here, 128), b16(plane_size, captions_here, 128),
        b16(planes, block, 1024), b16(planes, block, 1024),
        b16(planes, text_block, 128), b16(planes, text_block, 128),
        f32(planes, 8, 1152), f32(plane_size, 8, 1152),
        f32(total_images, HIDDEN // dp_size), b16(total_images, HIDDEN // rep_size),
        b16(total_images, HIDDEN // dp_size), b16(total_images, 128),
        pltpu.SemaphoreType.DMA((8,)), pltpu.SemaphoreType.DMA((copies,)), pltpu.SemaphoreType.DMA((copies,)),
    ]
    rows = images.transpose(1, 0, 2).reshape(rows_all, width)
    results = pl.pallas_call(
        functools.partial(
            fused_kernel, (images_here, captions_here, planes, sides, dp_size), copies
        ),
        out_shape=tuple(jax.ShapeDtypeStruct(shape, kind) for shape, kind in out_shapes),
        in_specs=[vmem] + [hbm] * 6 + [vmem] * 13,
        out_specs=tuple(vmem for _ in out_shapes),
        scratch_shapes=scratch,
        compiler_params=pltpu.CompilerParams(
            collective_id=1, has_side_effects=True, vmem_limit_bytes=60 * 2**20
        ),
        name="fused_block",
    )(
        rows, qkv_weight, out_weight, fc1_weight, fc2_weight, image_proj, text_proj,
        fc1_bias.reshape(1, -1), ln1_gain.reshape(1, -1), ln1_bias.reshape(1, -1),
        ln2_gain.reshape(1, -1), ln2_bias.reshape(1, -1), post_gain.reshape(1, -1),
        post_bias.reshape(1, -1), text_feats, text_gain.reshape(1, -1), text_bias.reshape(1, -1),
        log_scale.reshape(1, 1), caption_counts.reshape(1, -1), positives.reshape(1, -1),
    )
    block_out, grad_images, g_qkv, g_out, g_fc1, g_fc2, g_ip, g_text, g_tp, g_vec = results

    def restore(values):
        return values.reshape(patches, images_here, width).transpose(1, 0, 2)

    image_total = images_here * dp_size * rep_size
    return (
        restore(block_out),
        g_vec[6, EMBED] / image_total,
        restore(grad_images),
        g_qkv,
        g_out,
        g_fc1,
        g_vec[:, WIDTH:].reshape(-1),
        g_fc2.T,
        g_vec[0, 0:WIDTH],
        g_vec[1, 0:WIDTH],
        g_vec[2, 0:WIDTH],
        g_vec[3, 0:WIDTH],
        g_vec[4, 0:WIDTH],
        g_vec[5, 0:WIDTH],
        g_ip,
        g_text,
        g_vec[6, 0:EMBED],
        g_vec[7, 0:EMBED],
        g_tp,
        g_vec[7, EMBED : EMBED + 1],
    )


def solution(mesh):
    dp_size, rep_size = mesh.shape["dp"], mesh.shape["rep"]
    body = functools.partial(fused_shards, dp_size, rep_size) if fits(dp_size, rep_size) else shards

    return jax.shard_map(
        body,
        mesh=mesh,
        in_specs=(
            P(("dp", "rep"), None, None),
            P(),
            P(),
            P(),
            P(),
            P(),
            P(),
            P(),
            P(),
            P(),
            P(),
            P(),
            P(),
            P(("dp", "rep"), None),
            P(),
            P(),
            P(),
            P(),
            P(("dp", "rep")),
            P(("dp", "rep")),
        ),
        out_specs=(
            P(("dp", "rep"), None, None),
            P(),
            P(("dp", "rep"), None, None),
            P("rep", "dp"),
            P("rep", "dp"),
            P("rep", "dp"),
            P(),
            P("rep", "dp"),
            P(),
            P(),
            P(),
            P(),
            P(),
            P(),
            P("rep", "dp"),
            P(("dp", "rep"), None),
            P(),
            P(),
            P("rep", "dp"),
            P(),
        ),
        check_vma=False,
    )
```

```python
import functools

import jax
import jax.numpy as jnp
from jax import lax
from jax.experimental import pallas as pl
from jax.experimental.pallas import tpu as pltpu
from jax.sharding import PartitionSpec as P

HEADS = 12
HDIM = 64


def matmul(left, right):
    return jnp.dot(left, right, preferred_element_type=jnp.float32)


def matmul_left(left, right):
    return lax.dot_general(
        left, right, (((0,), (0,)), ((), ())), preferred_element_type=jnp.float32
    )


def matmul_right(left, right):
    return lax.dot_general(
        left, right, (((1,), (1,)), ((), ())), preferred_element_type=jnp.float32
    )


def layer_norm(values, gain, bias):
    centered = values - jnp.mean(values, -1, keepdims=True)
    factor = lax.rsqrt(jnp.mean(centered * centered, -1, keepdims=True) + 1e-05)
    normed = centered * factor
    return (normed * gain + bias, normed, factor)


def norm_back(grad_out, normed, factor, gain):
    scaled = grad_out * gain
    grad_in = factor * (
        scaled
        - jnp.mean(scaled, -1, keepdims=True)
        - normed * jnp.mean(scaled * normed, -1, keepdims=True)
    )
    return (grad_in, jnp.sum(grad_out * normed, 0), jnp.sum(grad_out, 0))


def unit_rows(values):
    factor = lax.rsqrt(jnp.sum(values * values, -1, keepdims=True) + 1e-06)
    return (values * factor, factor)


def unit_back(grad_unit, unit, factor):
    return factor * (grad_unit - unit * jnp.sum(grad_unit * unit, -1, keepdims=True))


def row_logsumexp(values):
    top_value = jnp.max(values, 1, keepdims=True)
    return top_value[:, 0] + jnp.log(jnp.sum(jnp.exp(values - top_value), 1))


def shards(
    images,
    qkv_weight,
    out_weight,
    fc1_weight,
    fc1_bias,
    fc2_weight,
    ln1_gain,
    ln1_bias,
    ln2_gain,
    ln2_bias,
    post_gain,
    post_bias,
    image_proj,
    text_feats,
    text_gain,
    text_bias,
    text_proj,
    log_scale,
    caption_counts,
    positives,
):
    images_here, patches, model_width = images.shape
    row_count = images_here * patches
    resid = images.reshape(row_count, model_width).astype(jnp.float32)
    normed_one, unit_one, factor_one = layer_norm(resid, ln1_gain, ln1_bias)
    normed_in = normed_one.astype(jnp.bfloat16)
    packed = (
        matmul(normed_in, qkv_weight)
        .astype(jnp.bfloat16)
        .reshape(images_here, patches, 3, HEADS, HDIM)
    )
    query, keys, values = (packed[:, :, 0], packed[:, :, 1], packed[:, :, 2])
    scores = 0.125 * jnp.einsum("bqhd,bkhd->bhqk", query, keys, preferred_element_type=jnp.float32)
    score_peak = jnp.max(scores, -1, keepdims=True)
    score_lse = score_peak + jnp.log(jnp.sum(jnp.exp(scores - score_peak), -1, keepdims=True))
    attn_low = jnp.exp(scores - score_lse).astype(jnp.bfloat16)
    mixed = jnp.einsum("bhqk,bkhd->bqhd", attn_low, values, preferred_element_type=jnp.float32)
    mixed = mixed.reshape(row_count, model_width).astype(jnp.bfloat16)
    middle = resid + matmul(mixed, out_weight)
    normed_two, unit_two, factor_two = layer_norm(middle, ln2_gain, ln2_bias)
    normed_mid = normed_two.astype(jnp.bfloat16)
    hidden = matmul(normed_mid, fc1_weight) + fc1_bias
    gate_sig = jax.nn.sigmoid(1.702 * hidden)
    activation = (hidden * gate_sig).astype(jnp.bfloat16)
    block = middle + matmul(activation, fc2_weight)
    block_out = block.reshape(images_here, patches, model_width).astype(jnp.bfloat16)
    class_rows = block.reshape(images_here, patches, model_width)[:, 0, :]
    class_full, unit_post, factor_post = layer_norm(class_rows, post_gain, post_bias)
    class_norm = class_full.astype(jnp.bfloat16)
    image_unit, image_factor = unit_rows(matmul(class_norm, image_proj))
    image_low = image_unit.astype(jnp.bfloat16)
    text_full, unit_text, factor_text = layer_norm(
        text_feats.astype(jnp.float32), text_gain, text_bias
    )
    text_norm = text_full.astype(jnp.bfloat16)
    text_unit, text_factor = unit_rows(matmul(text_norm, text_proj))
    text_low = text_unit.astype(jnp.bfloat16)
    all_images, all_texts = (
        lax.all_gather(image_low, ("dp", "rep"), axis=0, tiled=True),
        lax.all_gather(text_low, ("dp", "rep"), axis=0, tiled=True),
    )
    all_positives = lax.all_gather(positives, ("dp", "rep"), axis=0, tiled=True)
    image_total = all_images.shape[0]
    caption_total = all_texts.shape[0]
    text_ratio = image_total / caption_total
    logit_scale = jnp.exp(log_scale[0])
    image_ids = lax.axis_index(("dp", "rep")) * images_here + jnp.arange(
        images_here, dtype=jnp.int32
    )
    counts = caption_counts.astype(jnp.float32)
    row_logits = logit_scale * matmul_right(image_low, all_texts)
    row_match = (all_positives[None, :] == image_ids[:, None]).astype(jnp.float32)
    row_lse = row_logsumexp(row_logits)
    image_loss = row_lse - jnp.sum(row_match * row_logits, 1) / counts
    col_logits = logit_scale * matmul_right(text_low, all_images)
    col_match = (positives[:, None] == jnp.arange(image_total, dtype=jnp.int32)[None, :]).astype(
        jnp.float32
    )
    col_lse = row_logsumexp(col_logits)
    caption_loss = col_lse - jnp.sum(col_match * col_logits, 1)
    grad_rows = (
        0.5 * (jnp.exp(row_logits - row_lse[:, None]) - row_match / counts[:, None])
    ).astype(jnp.bfloat16)
    grad_cols = (0.5 * text_ratio * (jnp.exp(col_logits - col_lse[:, None]) - col_match)).astype(
        jnp.bfloat16
    )
    total_part = 0.5 * jnp.sum(image_loss) + 0.5 * text_ratio * jnp.sum(caption_loss)
    scale_part = jnp.sum(grad_rows.astype(jnp.float32) * row_logits) + jnp.sum(
        grad_cols.astype(jnp.float32) * col_logits
    )
    total, scale_grad = lax.psum((total_part, scale_part), ("dp", "rep"))
    loss = total / image_total
    grad_log_scale = scale_grad.reshape(1)
    columns = grad_cols
    grad_image_unit = logit_scale * matmul(grad_rows, all_texts) + lax.psum_scatter(
        logit_scale * matmul_left(columns, text_low), ("dp", "rep"), scatter_dimension=0, tiled=True
    )
    columns = grad_rows
    grad_text_unit = logit_scale * matmul(grad_cols, all_images) + lax.psum_scatter(
        logit_scale * matmul_left(columns, image_low),
        ("dp", "rep"),
        scatter_dimension=0,
        tiled=True,
    )
    grad_image_embed = unit_back(grad_image_unit, image_unit, image_factor).astype(jnp.bfloat16)
    grad_image_proj = matmul_left(class_norm, grad_image_embed)
    grad_class, grad_post_gain, grad_post_bias = norm_back(
        matmul_right(grad_image_embed, image_proj), unit_post, factor_post, post_gain
    )
    grad_text_embed = unit_back(grad_text_unit, text_unit, text_factor).astype(jnp.bfloat16)
    grad_text_proj = matmul_left(text_norm, grad_text_embed)
    grad_text_feats, grad_text_gain, grad_text_bias = norm_back(
        matmul_right(grad_text_embed, text_proj), unit_text, factor_text, text_gain
    )
    grad_block = (
        jnp.zeros((images_here, patches, model_width), jnp.float32)
        .at[:, 0, :]
        .set(grad_class)
        .reshape(row_count, model_width)
    )
    grad_block_low = grad_block.astype(jnp.bfloat16)
    grad_activation = matmul_right(grad_block_low, fc2_weight)
    grad_hidden = (
        grad_activation * (gate_sig + 1.702 * hidden * gate_sig * (1.0 - gate_sig))
    ).astype(jnp.bfloat16)
    grad_fc1_bias = jnp.sum(grad_hidden.astype(jnp.float32), 0)
    grad_mid_norm, grad_ln2_gain, grad_ln2_bias = norm_back(
        matmul_right(grad_hidden, fc1_weight), unit_two, factor_two, ln2_gain
    )
    grad_middle = grad_block + grad_mid_norm
    grad_middle_low = grad_middle.astype(jnp.bfloat16)
    grad_out_weight = matmul_left(mixed, grad_middle_low)
    grad_mixed = (
        matmul_right(grad_middle_low, out_weight)
        .astype(jnp.bfloat16)
        .reshape(images_here, patches, HEADS, HDIM)
    )
    again_scores = 0.125 * jnp.einsum(
        "bqhd,bkhd->bhqk", query, keys, preferred_element_type=jnp.float32
    )
    attn_full = jnp.exp(again_scores - score_lse)
    grad_values = jnp.einsum(
        "bhqk,bqhd->bkhd", attn_low, grad_mixed, preferred_element_type=jnp.float32
    )
    grad_attn = jnp.einsum(
        "bqhd,bkhd->bhqk", grad_mixed, values, preferred_element_type=jnp.float32
    )
    grad_scores = (
        attn_full * (grad_attn - jnp.sum(grad_attn * attn_full, -1, keepdims=True))
    ).astype(jnp.bfloat16)
    grad_query = 0.125 * jnp.einsum(
        "bhqk,bkhd->bqhd", grad_scores, keys, preferred_element_type=jnp.float32
    )
    grad_keys = 0.125 * jnp.einsum(
        "bhqk,bqhd->bkhd", grad_scores, query, preferred_element_type=jnp.float32
    )
    grad_packed = (
        jnp.stack([grad_query, grad_keys, grad_values], 2)
        .reshape(row_count, 3 * model_width)
        .astype(jnp.bfloat16)
    )
    grad_qkv_weight = matmul_left(normed_in, grad_packed)
    grad_in_norm, grad_ln1_gain, grad_ln1_bias = norm_back(
        matmul_right(grad_packed, qkv_weight), unit_one, factor_one, ln1_gain
    )
    grad_images = (grad_middle + grad_in_norm).reshape(images_here, patches, model_width)
    grad_fc2_weight = matmul_left(activation, grad_block_low)
    grad_fc1_weight = matmul_left(normed_mid, grad_hidden)
    first_qkv, first_out, first_fc1, first_fc2, first_image, first_text = (
        lax.psum_scatter(grad_qkv_weight, "dp", scatter_dimension=1, tiled=True),
        lax.psum_scatter(grad_out_weight, "dp", scatter_dimension=1, tiled=True),
        lax.psum_scatter(grad_fc1_weight, "dp", scatter_dimension=1, tiled=True),
        lax.psum_scatter(grad_fc2_weight, "dp", scatter_dimension=1, tiled=True),
        lax.psum_scatter(grad_image_proj, "dp", scatter_dimension=1, tiled=True),
        lax.psum_scatter(grad_text_proj, "dp", scatter_dimension=1, tiled=True),
    )
    summed_qkv, summed_out, summed_fc1, summed_fc2, summed_image, summed_text = (
        lax.psum_scatter(first_qkv, "rep", scatter_dimension=0, tiled=True),
        lax.psum_scatter(first_out, "rep", scatter_dimension=0, tiled=True),
        lax.psum_scatter(first_fc1, "rep", scatter_dimension=0, tiled=True),
        lax.psum_scatter(first_fc2, "rep", scatter_dimension=0, tiled=True),
        lax.psum_scatter(first_image, "rep", scatter_dimension=0, tiled=True),
        lax.psum_scatter(first_text, "rep", scatter_dimension=0, tiled=True),
    )
    vector_sums = lax.psum(
        (
            grad_ln1_gain,
            grad_ln1_bias,
            grad_ln2_gain,
            grad_ln2_bias,
            grad_fc1_bias,
            grad_post_gain,
            grad_post_bias,
            grad_text_gain,
            grad_text_bias,
        ),
        ("dp", "rep"),
    )
    return (
        block_out,
        loss,
        grad_images,
        summed_qkv,
        summed_out,
        summed_fc1,
        vector_sums[4],
        summed_fc2,
        vector_sums[0],
        vector_sums[1],
        vector_sums[2],
        vector_sums[3],
        vector_sums[5],
        vector_sums[6],
        summed_image,
        grad_text_feats,
        vector_sums[7],
        vector_sums[8],
        summed_text,
        grad_log_scale,
    )


MESH = pl.DeviceIdType.MESH
F32 = jnp.float32
BF16 = jnp.bfloat16
PATCHES = 50
WIDTH = 768
HIDDEN = 3072
EMBED = 512
GROUP = 8
STEP = 160


def fits(dp_size, rep_size):
    return dp_size == 4 and rep_size == 8


def dot_rows(left, right):
    return lax.dot_general(left, right, (((1,), (1,)), ((), ())), preferred_element_type=F32)


def dot_cols(left, right):
    return lax.dot_general(left, right, (((0,), (0,)), ((), ())), preferred_element_type=F32)


def lane_shift(values, amount):
    width = values.shape[1]
    amount = amount % width
    return values if amount == 0 else pltpu.roll(values, width - amount, 1)


def pick_blocks(values, side, sides, block, count):
    lanes = block * count
    place = lax.broadcasted_iota(jnp.int32, (values.shape[0], lanes), 1) // block
    picked = lane_shift(values, side * block)[:, :lanes]
    for index in range(1, count):
        offset = (side + index * sides) * block - index * block
        picked = jnp.where(place == index, lane_shift(values, offset)[:, :lanes], picked)
    return picked


def head_spread(rows):
    count = rows.shape[0]
    lane_head = lax.broadcasted_iota(jnp.int32, (HEADS, count, WIDTH), 2) // HDIM
    head = lax.broadcasted_iota(jnp.int32, (HEADS, count, WIDTH), 0)
    spread = jnp.where(lane_head == head, rows[None], 0.0)
    return spread.reshape(HEADS * count, WIDTH)


def head_gather(stacked):
    count = stacked.shape[0] // HEADS
    stacked = stacked.reshape(HEADS, count, WIDTH)
    lane_head = lax.broadcasted_iota(jnp.int32, stacked.shape, 2) // HDIM
    head = lax.broadcasted_iota(jnp.int32, stacked.shape, 0)
    return jnp.sum(jnp.where(lane_head == head, stacked, 0.0), 0)


def fused_kernel(dims, counter, *refs):
    (
        x_hbm, qkv_hbm, out_hbm, fc1_hbm, fc2_hbm, ip_hbm, tp_hbm, fc1_bias_in,
        ln1_gain_in, ln1_bias_in, ln2_gain_in, ln2_bias_in, post_gain_in, post_bias_in,
        text_feats, text_gain_in, text_bias_in, log_scale_in, caption_counts, positives,
        block_hbm, images_hbm, qkv_out, w_out_out, fc1_out, fc2_out, ip_out, text_out, tp_out, g_vec,
        x, qkv, w_out, fc1, fc2, ip, tp,
        ni, kv, qd, mixed, middle, nmd, block_out, grad_images,
        g_qkv, g_out, g_fc1, g_fc2, g_ip, g_text, g_tp,
        attn, attn_low, gsp, uu,
        hid_c, small,
        t_all, pos_all, i_all, cnt_all, row_sum, col_sum,
        gi_send, gi_recv, gt_send, gt_recv,
        nm_full, gb_full, rf_out, rf_in, ro_out, ro_in, cn_out, cn_in, tn_out, tn_in,
        ca_out, ca_in, co_out, co_in, te_out, te_in, pa_send, pa_recv, ps_send, ps_recv, pt_send, pt_recv,
        vec_out, vec_in, vec_z, vec_all, hid_s, act_s, gh_s, nm_sel,
        local_sem, send_sem, recv_sem,
    ) = refs
    images_here, captions_here, planes, sides, dp_size = dims
    plane_size = dp_size * sides
    rep_size = planes * sides
    rows_all = images_here * PATCHES
    half = rows_all // 2
    dp = lax.axis_index("dp")
    rep = lax.axis_index("rep")
    z = rep // sides
    side = lax.rem(rep, sides)
    slot = dp * sides + side
    row_y = dp // 2
    core = lax.rem(dp, 2)
    plane_images = plane_size * images_here
    line_captions = planes * captions_here
    image_total = plane_images * planes
    caption_total = line_captions * plane_size
    text_ratio = image_total / caption_total

    used = [0]
    fc1_bias = fc1_bias_in[...].reshape(1, HIDDEN)
    ln1_gain, ln1_bias, ln2_gain, ln2_bias, post_gain, post_bias = (
        ref[...].reshape(1, WIDTH)
        for ref in (ln1_gain_in, ln1_bias_in, ln2_gain_in, ln2_bias_in, post_gain_in, post_bias_in)
    )
    text_gain, text_bias = (ref[...].reshape(1, EMBED) for ref in (text_gain_in, text_bias_in))

    def plane_peer(step):
        peer = lax.rem(slot + step, plane_size)
        return peer, (peer // sides, z * sides + lax.rem(peer, sides))

    def line_peer(step):
        peer = lax.rem(z + step, planes)
        return peer, (dp, peer * sides + side)

    def copy_to(source, target, device, sends, arrivals):
        return pltpu.make_async_remote_copy(
            src_ref=source, dst_ref=target, send_sem=send_sem.at[sends], recv_sem=recv_sem.at[arrivals],
            device_id=device, device_id_type=MESH,
        )

    def take(count=1):
        used[0] += count
        return used[0] - count

    def exchange(peers, source_of, target, whole):
        index = take()
        for peer, device in peers:
            copy_to(source_of(peer), target, device, index, index).start()
        return (whole, index)

    def to_plane(source_of, target, whole):
        return exchange([plane_peer(step) for step in range(1, plane_size)], source_of, target, whole)

    def to_line(source_of, target, whole):
        return exchange([line_peer(step) for step in range(1, planes)], source_of, target, whole)

    def to_chips(buffer):
        peers = []
        for step in range(1, 2 * sides):
            peer = lax.rem(row_y * sides + side + step, 2 * sides)
            peers.append((peer, ((peer // sides) * 2 + core, z * sides + lax.rem(peer, sides))))
        mine = buffer.at[:, row_y, core, side]
        return exchange(peers, lambda peer: mine, mine, buffer.at[0 : planes - 1, 0])

    def to_partner(buffer):
        device = (row_y * 2 + 1 - core, rep)
        mine = buffer.at[:, :, core]
        return exchange([(0, device)], lambda peer: mine, mine, mine)

    def finish(sent):
        whole, index = sent
        pltpu.make_async_copy(whole, whole, recv_sem.at[index]).wait()
        pltpu.make_async_copy(whole, whole, send_sem.at[index]).wait()

    others = plane_size - 1
    lines = planes - 1

    loads = []

    def put_out(source, target):
        copy = pltpu.make_async_copy(source, target, local_sem.at[len(loads)])
        loads.append(copy)
        copy.start()
        return copy

    for index, (source, target) in enumerate(
        (
            (tp_hbm, tp), (x_hbm, x), (qkv_hbm, qkv), (out_hbm, w_out), (fc1_hbm, fc1), (fc2_hbm, fc2),
            (ip_hbm, ip),
        )
    ):
        load = pltpu.make_async_copy(source, target, local_sem.at[index])
        load.start()
        loads.append(load)

    barrier = pltpu.get_barrier_semaphore()
    for step in range(1, plane_size):
        pl.semaphore_signal(barrier, inc=1, device_id=plane_peer(step)[1], device_id_type=MESH)
    for step in range(1, planes):
        pl.semaphore_signal(barrier, inc=1, device_id=line_peer(step)[1], device_id_type=MESH)

    text_full, _, _ = layer_norm(text_feats[...].astype(F32), text_gain, text_bias)
    text_norm = text_full.astype(BF16)
    loads[0].wait()
    text_unit, text_factor = unit_rows(matmul(text_norm, tp[...]))
    t_all[z] = text_unit.astype(BF16)
    pos_rows = jnp.broadcast_to(positives[...].reshape(1, captions_here).astype(F32), (128, captions_here))
    pos_all[z] = jnp.transpose(pos_rows)
    cnt_rows = jnp.broadcast_to(caption_counts[...].reshape(1, images_here).astype(F32), (128, images_here))
    cnt_all[slot] = jnp.transpose(cnt_rows)
    pl.semaphore_wait(barrier, plane_size - 1 + planes - 1)
    text_copies = to_line(lambda peer: t_all.at[z], t_all.at[z], t_all.at[0:lines])
    pos_copies = to_line(lambda peer: pos_all.at[z], pos_all.at[z], pos_all.at[0:lines])
    cnt_copies = to_plane(lambda peer: cnt_all.at[slot], cnt_all.at[slot], cnt_all.at[0:others])
    text_lanes = EMBED // rep_size
    for to_side in range(sides):
        tn_out[to_side] = pick_blocks(text_full, to_side, sides, text_lanes, planes).astype(BF16)
    tn_copies = to_plane(lambda peer: tn_out.at[lax.rem(peer, sides)], tn_in.at[slot], tn_in.at[0:others])
    tn_in[slot] = tn_out[side]

    loads[1].wait()
    for first in range(0, rows_all, STEP):
        full = layer_norm(x[first : first + STEP, :].astype(F32), ln1_gain, ln1_bias)[0]
        full = full.reshape(STEP // 16, 2, GROUP, WIDTH)
        for part in range(2):
            to = part * half + first // 2
            ni[to : to + STEP // 2, :] = full[:, part].reshape(STEP // 2, WIDTH).astype(BF16)

    loads[2].wait()
    for first in range(0, 2 * WIDTH, WIDTH):
        kv[:, first : first + WIDTH] = matmul(ni[...], qkv[:, WIDTH + first : 2 * WIDTH + first]).astype(BF16)

    resid_c = x[0:images_here, :].astype(F32)
    normed_c = layer_norm(resid_c, ln1_gain, ln1_bias)[0].astype(BF16)
    query_c = matmul(normed_c, qkv[:, 0:WIDTH]).astype(BF16)
    query_spread = head_spread(query_c.astype(F32)).astype(BF16)
    scores = 0.125 * dot_rows(query_spread, kv[:, 0:WIDTH])
    row_image = lax.broadcasted_iota(jnp.int32, scores.shape, 0) & (images_here - 1)
    column = lax.broadcasted_iota(jnp.int32, scores.shape, 1)
    column_image = jnp.where(column < half, 0, GROUP) + (column & (GROUP - 1))
    scores = jnp.where(row_image == column_image, scores, -1e30)
    weights = jnp.exp(scores - jnp.max(scores, 1, keepdims=True))
    weights = weights * (1.0 / jnp.sum(weights, 1, keepdims=True))
    attn[...] = weights
    attn_low[...] = weights.astype(BF16)
    mixed_c = head_gather(matmul(attn_low[...], kv[:, WIDTH:]))
    block_lanes = WIDTH // rep_size
    mixed_f, normed_f = mixed_c.astype(BF16).astype(F32), normed_c.astype(F32)
    for to_side in range(sides):
        ro_out[to_side, 0] = pick_blocks(mixed_f, to_side, sides, block_lanes, planes).astype(BF16)
        ro_out[to_side, 1] = pick_blocks(normed_f, to_side, sides, block_lanes, planes).astype(BF16)
    ro_copies = to_plane(
        lambda peer: ro_out.at[lax.rem(peer, sides)], ro_in.at[:, slot], ro_in.at[:, 0:others]
    )
    ro_in[:, slot] = ro_out[side]
    loads[3].wait()
    middle_c = resid_c + matmul(mixed_c.astype(BF16), w_out[...])
    full, unit_two, factor_two = layer_norm(middle_c, ln2_gain, ln2_bias)
    nm_full[z, row_y, core, side] = full.astype(BF16)
    nm_line = to_line(
        lambda peer: nm_full.at[z, row_y, core, side], nm_full.at[z, row_y, core, side], nm_full.at[0:lines, 0, 0, 0]
    )
    loads[4].wait()
    hid_c[...] = matmul(full.astype(BF16), fc1[...]) + fc1_bias
    act_c = (hid_c[...] * jax.nn.sigmoid(1.702 * hid_c[...])).astype(BF16)
    loads[5].wait()
    block_c = middle_c + matmul(act_c, fc2[...])
    full, unit_post, factor_post = layer_norm(block_c, post_gain, post_bias)
    class_norm = full.astype(BF16)
    loads[6].wait()
    image_unit, image_factor = unit_rows(matmul(class_norm, ip[...]))
    i_all[slot] = image_unit.astype(BF16)
    image_copies = to_plane(lambda peer: i_all.at[slot], i_all.at[slot], i_all.at[0:others])
    small[0] = unit_two
    small[1] = unit_post

    value_rows = matmul(attn_low[...], ni[...])
    for to_side in range(sides):
        picked = pick_blocks(value_rows, to_side, sides, block_lanes, planes).astype(BF16)
        rf_out[to_side, HEADS:] = picked.reshape(HEADS, images_here, planes * block_lanes)
        cn_out[to_side] = pick_blocks(full, to_side, sides, block_lanes, planes).astype(BF16)
    cn_in[slot] = cn_out[side]

    heads_here = 3 * HEADS // dp_size
    bundle = heads_here // 3
    rf_copies = []
    arrivals = take(3)
    for step in range(1, plane_size):
        peer, device = plane_peer(step)
        for part in range(3):
            first = (peer // sides) * heads_here + part * bundle
            copy = copy_to(
                rf_out.at[lax.rem(peer, sides), pl.ds(lax.rem(first + HEADS, 2 * HEADS), bundle)],
                rf_in.at[pl.ds(part * bundle, bundle), slot], device, take(), arrivals + part,
            )
            rf_copies.append((copy, first))

    def head_kind(first):
        return first // HEADS

    def dense_query():
        qd[...] = (0.125 * matmul(ni[...], qkv[:, 0:WIDTH]).astype(BF16).astype(F32)).astype(BF16)

    def dense_attention(first, last):
        lane = lax.broadcasted_iota(jnp.int32, (half, 128), 1)
        apart = lax.broadcasted_iota(jnp.int32, (GROUP, half), 0) != (
            lax.broadcasted_iota(jnp.int32, (GROUP, half), 1) & (GROUP - 1)
        )
        bias = jnp.where(apart, -1e30, 0.0)[None]
        for index in range(first, last):
            rows = slice((index % 2) * half, (index % 2) * half + half)
            lanes = slice((index // 2) * 128, (index // 2) * 128 + 128)
            query = qd[rows, lanes]
            keys = kv[rows, lanes]
            values = kv[rows, WIDTH + lanes.start : WIDTH + lanes.stop]
            result = None
            for which in range(2):
                own = (lane < HDIM) if which == 0 else (lane >= HDIM)
                logits = dot_rows(jnp.where(own, query, jnp.zeros_like(query)), keys)
                logits = (logits.reshape(half // GROUP, GROUP, half) + bias).reshape(half, half)
                top = jnp.exp(logits - jnp.max(logits, 1, keepdims=True))
                got = matmul(top.astype(BF16), values) * (1.0 / jnp.sum(top, 1, keepdims=True))
                result = got if which == 0 else jnp.where(own, got, result)
            mixed[rows, lanes] = result.astype(BF16)

    def join_groups(values, first):
        parts = [
            values[part * half + first // 2 : part * half + (first + STEP) // 2].reshape(STEP // 16, GROUP, WIDTH)
            for part in range(2)
        ]
        return jnp.stack(parts, 1).reshape(STEP, WIDTH)

    def dense_out():
        added = matmul(mixed[...], w_out[...])
        for first in range(0, rows_all, STEP):
            rows = slice(first, first + STEP)
            value = x[rows, :].astype(F32) + join_groups(added, first)
            middle[rows, :] = value
            nmd[rows, :] = layer_norm(value, ln2_gain, ln2_bias)[0].astype(BF16)

    def dense_ff(part):
        rows = slice(part * half, (part + 1) * half)
        hidden = matmul(nmd[rows, :], fc1[...]) + fc1_bias
        act = (hidden * jax.nn.sigmoid(1.702 * hidden)).astype(BF16)
        block_out[rows, :] = (middle[rows, :] + matmul(act, fc2[...])).astype(BF16)
        return put_out(block_out.at[rows], block_hbm.at[rows])

    dense_query()

    finish(text_copies)
    finish(pos_copies)
    finish(cnt_copies)
    finish(image_copies)
    scale = jnp.exp(log_scale_in[...].reshape(1, 1))
    images_low = i_all[...].reshape(plane_images, EMBED)
    texts_low = t_all[...].reshape(line_captions, EMBED)
    logits = scale * dot_rows(images_low, texts_low)
    logits_t = scale * dot_rows(texts_low, images_low)

    def image_ids(dim, shape):
        index = lax.broadcasted_iota(jnp.int32, shape, dim)
        holder = index // images_here
        owner = (holder // sides) * rep_size + z * sides + lax.rem(holder, sides)
        return (owner * images_here + lax.rem(index, images_here)).astype(F32)

    pos_col = pos_all[...].reshape(line_captions, 128)
    match_t = (pos_col[:, 0:1] == image_ids(1, logits_t.shape)).astype(F32)
    match = (jnp.transpose(pos_col) == image_ids(0, logits.shape)).astype(F32)
    counts = jnp.transpose(cnt_all[...].reshape(plane_images, 128))[0:1, :]
    row_sum[slot] = jnp.broadcast_to(jnp.sum(jnp.exp(logits_t), 0, keepdims=True), (8, plane_images))
    col_sum[z] = jnp.broadcast_to(jnp.sum(jnp.exp(logits), 0, keepdims=True), (8, line_captions))
    row_copies = to_plane(lambda peer: row_sum.at[slot], row_sum.at[slot], row_sum.at[0:others])
    col_copies = to_line(lambda peer: col_sum.at[z], col_sum.at[z], col_sum.at[0:lines])

    dense_attention(0, 6)

    finish(row_copies)
    finish(col_copies)
    row_lse = jnp.log(jnp.sum(row_sum[...], 0)[0:1])
    col_lse = jnp.log(jnp.sum(col_sum[...], 0)[0:1])
    grad_cols = (0.5 * text_ratio * (jnp.exp(logits - col_lse) - match)).astype(BF16)
    grad_rows_t = (0.5 * (jnp.exp(logits_t - row_lse) - match_t / counts)).astype(BF16)
    loss_part = 0.5 * (jnp.sum(row_lse) / plane_size - jnp.sum(match_t * logits_t / counts)) + (
        0.5 * text_ratio
    ) * (jnp.sum(col_lse) / planes - jnp.sum(match * logits))
    scale_part = jnp.sum(grad_cols.astype(F32) * logits) + jnp.sum(grad_rows_t.astype(F32) * logits_t)
    gi_send[...] = (
        (scale * (dot_cols(grad_rows_t, texts_low) + matmul(grad_cols, texts_low)))
        .astype(BF16)
        .reshape(plane_size, images_here, EMBED)
    )
    gi_copies = to_plane(lambda peer: gi_send.at[peer], gi_recv.at[slot], gi_recv.at[0:others])
    gi_recv[slot] = gi_send[slot]
    gt_send[...] = (
        (scale * (dot_cols(grad_cols, images_low) + matmul(grad_rows_t, images_low)))
        .astype(BF16)
        .reshape(planes, captions_here, EMBED)
    )
    gt_copies = to_line(lambda peer: gt_send.at[peer], gt_recv.at[z], gt_recv.at[0:lines])
    gt_recv[z] = gt_send[z]

    dense_attention(6, 12)

    finish(gi_copies)
    cn_copies = to_plane(lambda peer: cn_out.at[lax.rem(peer, sides)], cn_in.at[slot], cn_in.at[0:others])
    for copy, first in rf_copies:
        pl.when(head_kind(first) == 2)(copy.start)
    grad_embed = unit_back(jnp.sum(gi_recv[...].astype(F32), 0), image_unit, image_factor).astype(BF16)
    grad_class, g_post_gain, g_post_bias = norm_back(
        dot_rows(grad_embed, ip[...]), small[1], factor_post, post_gain
    )
    gb_low = grad_class.astype(BF16)
    gb_full[z, row_y, core, side] = gb_low
    gb_line = to_line(
        lambda peer: gb_full.at[z, row_y, core, side], gb_full.at[z, row_y, core, side], gb_full.at[0:lines, 0, 0, 0]
    )
    gate = jax.nn.sigmoid(1.702 * hid_c[...])
    grad_hidden = (
        dot_rows(gb_low, fc2[...]) * (gate + 1.702 * hid_c[...] * gate * (1.0 - gate))
    ).astype(BF16)
    g_fc1_bias = jnp.sum(grad_hidden.astype(F32), 0, keepdims=True)
    grad_two, g_ln2_gain, g_ln2_bias = norm_back(
        dot_rows(grad_hidden, fc1[...]), small[0], factor_two, ln2_gain
    )
    grad_middle = grad_class + grad_two
    grad_middle_low = grad_middle.astype(BF16)
    m_plain = grad_middle_low.astype(F32)
    m_shift = lane_shift(m_plain, 64)
    cuts = (m_plain[:, 0:192], m_shift[:, 128:320], m_plain[:, 384:576], m_shift[:, 512:704])
    for to_dp, source in enumerate(cuts):
        ca_out[to_dp, :, 0:192] = source.astype(BF16)
        ca_out[to_dp, :, 256:384] = grad_embed[:, to_dp * 128 : to_dp * 128 + 128]
    ca_copies = to_plane(lambda peer: ca_out.at[peer // sides], ca_in.at[slot], ca_in.at[0:others])
    ca_in[slot] = ca_out[dp]
    grad_mixed = dot_rows(grad_middle_low, w_out[...]).astype(BF16)
    mixed_spread = head_spread(grad_mixed.astype(F32)).astype(BF16)
    grad_attn = dot_rows(mixed_spread, kv[:, WIDTH:])
    weights = attn[...]
    grad_scores = weights * (grad_attn - jnp.sum(grad_attn * weights, 1, keepdims=True))
    grad_scores = 0.125 * grad_scores.astype(BF16).astype(F32)
    gsp[0 : HEADS * images_here] = grad_scores.astype(BF16)
    gsp[HEADS * images_here :] = attn_low[...]
    score_low = gsp[0 : HEADS * images_here]
    grad_query = head_gather(matmul(score_low, kv[:, 0:WIDTH])).astype(BF16)
    key_rows = matmul(score_low, ni[...])
    for to_side in range(sides):
        picked = pick_blocks(key_rows, to_side, sides, block_lanes, planes).astype(BF16)
        rf_out[to_side, 0:HEADS] = picked.reshape(HEADS, images_here, planes * block_lanes)

    grad_q = grad_query.astype(F32)
    query_f = query_c.astype(F32)
    grad_v = grad_mixed.astype(F32)
    lane = lax.broadcasted_iota(jnp.int32, (images_here, 128), 1)
    q_shift, k_shift, v_shift = lane_shift(grad_q, 64), lane_shift(query_f, -64), lane_shift(grad_v, 64)
    co_out[0, :, 0:576] = grad_q[:, 0:576].astype(BF16)
    co_out[1, :, 0:128] = q_shift[:, 512:640].astype(BF16)
    co_out[1, :, 128:256] = jnp.where(lane < 64, q_shift[:, 640:768], k_shift[:, 0:128]).astype(BF16)
    co_out[1, :, 256:576] = k_shift[:, 128:448].astype(BF16)
    co_out[2, :, 0:384] = query_f[:, 384:768].astype(BF16)
    co_out[2, :, 384:576] = grad_v[:, 0:192].astype(BF16)
    co_out[3, :, 0:576] = v_shift[:, 128:704].astype(BF16)
    co_copies = to_plane(lambda peer: co_out.at[peer // sides], co_in.at[slot], co_in.at[0:others])
    for copy, first in rf_copies:
        pl.when(head_kind(first) == 1)(copy.start)
    co_in[slot] = co_out[dp]
    for part in range(3):
        mine = dp * heads_here + part * bundle

        def keep(part=part, mine=mine):
            own = rf_out[side, pl.ds(lax.rem(mine + HEADS, 2 * HEADS), bundle)]
            rf_in[part * bundle : (part + 1) * bundle, slot] = own

        pl.when(head_kind(mine) > 0)(keep)

    rows_here = planes * block_lanes
    finish(ro_copies)
    finish(cn_copies)
    finish(ca_copies)
    columns_in = ca_in[...].reshape(plane_images, 384)
    got = dot_cols(ro_in[0].reshape(plane_images, rows_here), columns_in[:, 0:256])
    pa_send[:, :, 0:256] = got.astype(BF16).reshape(planes, block_lanes, 256)
    got = dot_cols(cn_in[...].reshape(plane_images, rows_here), columns_in[:, 256:384])
    pa_send[:, :, 256:384] = got.astype(BF16).reshape(planes, block_lanes, 128)
    pa_copies = to_line(lambda peer: pa_send.at[peer], pa_recv.at[z], pa_recv.at[0:lines])
    pa_recv[z] = pa_send[z]

    finish(gt_copies)
    grad_text = unit_back(jnp.sum(gt_recv[...].astype(F32), 0), text_unit, text_factor).astype(BF16)
    for to_dp in range(dp_size):
        te_out[to_dp] = grad_text[:, to_dp * 128 : to_dp * 128 + 128]
    te_copies = to_plane(lambda peer: te_out.at[peer // sides], te_in.at[slot], te_in.at[0:others])
    te_in[slot] = te_out[dp]
    _, unit_text, factor_text = layer_norm(text_feats[...].astype(F32), text_gain, text_bias)
    g_feats, g_text_gain, g_text_bias = norm_back(
        dot_rows(grad_text, tp[...]), unit_text, factor_text, text_gain
    )
    g_text[...] = g_feats

    finish(nm_line)
    nm_chips = to_chips(nm_full)
    finish(gb_line)
    gb_chips = to_chips(gb_full)

    uu[0 : HEADS * images_here] = dot_rows(query_spread, qkv[:, WIDTH : 2 * WIDTH]).astype(BF16)
    uu[HEADS * images_here :] = dot_rows(mixed_spread, qkv[:, 2 * WIDTH :]).astype(BF16)
    class_in = dot_rows(grad_query, qkv[:, 0:WIDTH])

    spread = dot_cols(gsp[...], uu[...])
    g_ln1_gain = jnp.zeros((1, WIDTH), F32)
    g_ln1_bias = jnp.zeros((1, WIDTH), F32)
    for first in range(0, rows_all, STEP):
        rows = slice(first, first + STEP)
        _, unit, factor = layer_norm(x[rows, :].astype(F32), ln1_gain, ln1_bias)
        grad_out = join_groups(spread, first)
        if first == 0:
            grad_out = jnp.concatenate([grad_out[0:images_here] + class_in, grad_out[images_here:]], 0)
        grad_in, gain_part, bias_part = norm_back(grad_out, unit, factor, ln1_gain)
        grad_images[rows, :] = grad_in
        g_ln1_gain += gain_part[None]
        g_ln1_bias += bias_part[None]
    grad_images[0:images_here] += grad_middle
    outs = [put_out(grad_images, images_hbm), put_out(g_text, text_out)]

    vectors = (
        g_ln1_gain, g_ln1_bias, g_ln2_gain[None], g_ln2_bias[None], g_post_gain[None], g_post_bias[None],
        g_text_gain[None], g_text_bias[None],
    )
    for index, vector in enumerate(vectors):
        vec_out[index, :, 0 : vector.shape[1]] = vector
        vec_out[index, :, WIDTH:] = g_fc1_bias[:, index * 384 : index * 384 + 384]
    first_lane = lax.broadcasted_iota(jnp.int32, (1, 256), 1) == 0
    vec_out[6, :, EMBED:WIDTH] = jnp.where(first_lane, loss_part, 0.0)
    vec_out[7, :, EMBED:WIDTH] = jnp.where(first_lane, scale_part, 0.0)
    vec_plane = to_plane(lambda peer: vec_out.at[peer], vec_in.at[slot], vec_in.at[0:others])
    vec_in[slot] = vec_out[slot]

    for part in range(3):
        mine = dp * heads_here + part * bundle
        here = rf_in.at[part * bundle : (part + 1) * bundle, 0:others]
        pl.when(head_kind(mine) > 0)(pltpu.make_async_copy(here, here, recv_sem.at[arrivals + part]).wait)

        def repeat(part=part):
            rf_in[part * bundle : (part + 1) * bundle] = jnp.broadcast_to(
                ro_in[1][None], (bundle, plane_size, images_here, rows_here)
            )

        pl.when(head_kind(mine) == 0)(repeat)
    finish(co_copies)
    columns_in = co_in[...].reshape(plane_images, 640)
    lane = lax.broadcasted_iota(jnp.int32, (rows_here, 128), 1)
    for tile in range(5):
        right = columns_in[:, tile * 128 : tile * 128 + 128]
        got = dot_cols(rf_in[2 * tile].reshape(plane_images, rows_here), right)
        if 2 * tile + 1 < heads_here:
            other = dot_cols(rf_in[2 * tile + 1].reshape(plane_images, rows_here), right)
            got = jnp.where(lane < HDIM, got, other)
        width = min(128, 576 - tile * 128)
        ps_send[:, :, tile * 128 : tile * 128 + width] = (
            got[:, 0:width].astype(BF16).reshape(planes, block_lanes, width)
        )
    ps_copies = to_line(lambda peer: ps_send.at[peer], ps_recv.at[z], ps_recv.at[0:lines])
    ps_recv[z] = ps_send[z]
    for copy, first in rf_copies:
        pl.when(head_kind(first) > 0)(copy.wait_send)
    finish(tn_copies)
    finish(te_copies)
    got = dot_cols(
        tn_in[...].reshape(plane_size * captions_here, planes * text_lanes),
        te_in[...].reshape(plane_size * captions_here, 128),
    )
    pt_send[...] = got.astype(BF16).reshape(planes, text_lanes, 128)
    pt_copies = to_line(lambda peer: pt_send.at[peer], pt_recv.at[z], pt_recv.at[0:lines])
    pt_recv[z] = pt_send[z]

    finish(vec_plane)
    vec_z[z] = jnp.sum(vec_in[...], 0)
    vec_line = to_line(lambda peer: vec_z.at[z], vec_z.at[z], vec_z.at[0:lines])
    finish(nm_chips)
    nm_partner = to_partner(nm_full)

    finish(gb_chips)
    gb_partner = to_partner(gb_full)
    finish(nm_partner)
    all_rows = plane_images * planes
    nm_rows = nm_full[...].reshape(all_rows, WIDTH)
    my_columns = pl.ds(pl.multiple_of(dp * (HIDDEN // dp_size), 128), HIDDEN // dp_size)
    my_rows = pl.ds(pl.multiple_of(rep * (HIDDEN // rep_size), 128), HIDDEN // rep_size)
    hid_s[...] = matmul(nm_rows, fc1[:, my_columns]) + fc1_bias_in[my_columns].reshape(1, HIDDEN // dp_size)
    hidden = matmul(nm_rows, fc1[:, my_rows]) + fc1_bias_in[my_rows].reshape(1, HIDDEN // rep_size)
    act_s[...] = (hidden * jax.nn.sigmoid(1.702 * hidden)).astype(BF16)
    source = lax.broadcasted_iota(jnp.int32, (WIDTH, 128), 0)
    place = lax.broadcasted_iota(jnp.int32, (WIDTH, 128), 1)
    chosen = jnp.where((source == place + rep * block_lanes) & (place < block_lanes), 1.0, 0.0).astype(BF16)
    nm_sel[...] = matmul(nm_rows, chosen).astype(BF16)
    finish(gb_partner)
    gb_rows = gb_full[...].reshape(all_rows, WIDTH)
    gate = jax.nn.sigmoid(1.702 * hid_s[...])
    gh_s[...] = (
        dot_rows(gb_rows, fc2[my_columns, :]) * (gate + 1.702 * hid_s[...] * gate * (1.0 - gate))
    ).astype(BF16)
    g_fc1[...] = dot_cols(nm_sel[...], gh_s[...])[0:block_lanes]
    out_lanes = WIDTH // dp_size
    source = lax.broadcasted_iota(jnp.int32, (WIDTH, 256), 0)
    place = lax.broadcasted_iota(jnp.int32, (WIDTH, 256), 1)
    chosen = jnp.where((source == place + dp * out_lanes) & (place < out_lanes), 1.0, 0.0).astype(BF16)
    g_fc2[...] = dot_cols(matmul(gb_rows, chosen).astype(BF16), act_s[...])[0:out_lanes]

    outs += [put_out(g_fc1, fc1_out), put_out(g_fc2, fc2_out)]
    finish(vec_line)
    vec_all[slot] = jnp.sum(vec_z[...], 0)
    vec_last = to_plane(lambda peer: vec_all.at[slot], vec_all.at[slot], vec_all.at[0:others])

    dense_out()
    outs += [dense_ff(0), dense_ff(1)]

    finish(pa_copies)
    summed = jnp.sum(pa_recv[...].astype(F32), 0)
    g_out[...] = summed[:, 0:192]
    g_ip[...] = summed[:, 256:384]
    finish(pt_copies)
    g_tp[...] = jnp.sum(pt_recv[...].astype(F32), 0)
    outs += [put_out(g_out, w_out_out), put_out(g_ip, ip_out), put_out(g_tp, tp_out)]
    finish(vec_last)
    g_vec[...] = vec_all[...].reshape(plane_size, 1152)
    finish(ps_copies)
    g_qkv[...] = jnp.sum(ps_recv[...].astype(F32), 0)
    outs += [put_out(g_qkv, qkv_out)]
    for copy in outs:
        copy.wait()
    assert used[0] <= counter


def finish_kernel(scale, *refs):
    sources, vec, targets, outs, holds, sem = refs[0:9], refs[9], refs[10:19], refs[19:30], refs[30:39], refs[39]
    pieces = []
    for source, target, hold in zip(sources, targets, holds):
        parts = 5 if source.shape[0] > 400 else 1
        size = source.shape[0] // parts
        for first in range(0, source.shape[0], size):
            rows = pl.ds(first, size)
            index = 2 * len(pieces)
            pieces.append((
                pltpu.make_async_copy(source.at[rows], hold.at[rows], sem.at[index]),
                pltpu.make_async_copy(hold.at[rows], target.at[rows], sem.at[index + 1]),
            ))
    for fetch, _ in pieces:
        fetch.start()
    for fetch, store in pieces:
        fetch.wait()
        store.start()
    fc1_bias, ln1_gain, ln1_bias, ln2_gain, ln2_bias, post_gain, post_bias, text_gain, text_bias, loss, log_scale = outs
    for index, out in enumerate((ln1_gain, ln1_bias, ln2_gain, ln2_bias, post_gain, post_bias)):
        out[...] = vec[index : index + 1, 0:WIDTH].reshape(WIDTH)
    text_gain[...] = vec[6:7, 0:EMBED].reshape(EMBED)
    text_bias[...] = vec[7:8, 0:EMBED].reshape(EMBED)
    fc1_bias[...] = jnp.concatenate([vec[index : index + 1, WIDTH:] for index in range(8)], 1).reshape(HIDDEN)
    loss[...] = (vec[6:7, EMBED : EMBED + 128] * scale).reshape(128)[0:1]
    log_scale[...] = vec[7:8, EMBED : EMBED + 128].reshape(128)[0:1]
    for _, store in pieces:
        store.wait()


def fused_shards(
    dp_size,
    rep_size,
    images,
    qkv_weight,
    out_weight,
    fc1_weight,
    fc1_bias,
    fc2_weight,
    ln1_gain,
    ln1_bias,
    ln2_gain,
    ln2_bias,
    post_gain,
    post_bias,
    image_proj,
    text_feats,
    text_gain,
    text_bias,
    text_proj,
    log_scale,
    caption_counts,
    positives,
):
    images_here, patches, width = images.shape
    captions_here = text_feats.shape[0]
    sides = 2
    planes = rep_size // sides
    plane_size = dp_size * sides
    rows_all = images_here * patches
    heads_here = 3 * HEADS // dp_size
    block = WIDTH // rep_size
    text_block = EMBED // rep_size
    spread = HEADS * images_here
    line = planes * captions_here
    total_images = plane_size * planes * images_here
    copies = 50
    vmem = pl.BlockSpec(memory_space=pltpu.VMEM)
    hbm = pl.BlockSpec(memory_space=pl.ANY)

    def f32(*shape):
        return pltpu.VMEM(shape, F32)

    def b16(*shape):
        return pltpu.VMEM(shape, BF16)

    out_shapes = (
        ((rows_all, WIDTH), BF16),
        ((rows_all, WIDTH), F32),
        ((block, 3 * WIDTH // dp_size), F32),
        ((block, WIDTH // dp_size), F32),
        ((block, HIDDEN // dp_size), F32),
        ((WIDTH // dp_size, HIDDEN // rep_size), F32),
        ((block, EMBED // dp_size), F32),
        ((captions_here, EMBED), F32),
        ((text_block, EMBED // dp_size), F32),
        ((8, 1152), F32),
    )
    scratch = [
        b16(rows_all, WIDTH), b16(WIDTH, 3 * WIDTH), b16(WIDTH, WIDTH), b16(WIDTH, HIDDEN), b16(HIDDEN, WIDTH),
        b16(WIDTH, EMBED), b16(EMBED, EMBED),
        b16(rows_all, WIDTH), b16(rows_all, 2 * WIDTH), b16(rows_all, WIDTH), b16(rows_all, WIDTH),
        f32(rows_all, WIDTH), b16(rows_all, WIDTH), b16(rows_all, WIDTH), f32(rows_all, WIDTH),
        *(pltpu.VMEM(shape, kind) for shape, kind in out_shapes[2:9]),
        f32(spread, rows_all), b16(spread, rows_all), b16(2 * spread, rows_all), b16(2 * spread, WIDTH),
        f32(images_here, HIDDEN), f32(2, images_here, WIDTH),
        b16(planes, captions_here, EMBED), f32(planes, captions_here, 128),
        b16(plane_size, images_here, EMBED), f32(plane_size, images_here, 128),
        f32(plane_size, 8, plane_size * images_here), f32(planes, 8, line),
        b16(plane_size, images_here, EMBED), b16(plane_size, images_here, EMBED),
        b16(planes, captions_here, EMBED), b16(planes, captions_here, EMBED),
        b16(planes, dp_size // 2, 2, sides, images_here, WIDTH), b16(planes, dp_size // 2, 2, sides, images_here, WIDTH),
        b16(sides, 2 * HEADS, images_here, planes * block),
        b16(heads_here, plane_size, images_here, planes * block),
        b16(sides, 2, images_here, planes * block), b16(2, plane_size, images_here, planes * block),
        b16(sides, images_here, planes * block), b16(plane_size, images_here, planes * block),
        b16(sides, captions_here, planes * text_block), b16(plane_size, captions_here, planes * text_block),
        b16(dp_size, images_here, 384), b16(plane_size, images_here, 384),
        b16(dp_size, images_here, 640), b16(plane_size, images_here, 640),
        b16(dp_size, captions_here, 128), b16(plane_size, captions_here, 128),
        b16(planes, block, 384), b16(planes, block, 384), b16(planes, block, 576), b16(planes, block, 576),
        b16(planes, text_block, 128), b16(planes, text_block, 128),
        f32(8, 1, 1152), f32(plane_size, 1, 1152), f32(planes, 1, 1152), f32(plane_size, 1, 1152),
        f32(total_images, HIDDEN // dp_size), b16(total_images, HIDDEN // rep_size),
        b16(total_images, HIDDEN // dp_size), b16(total_images, 128),
        pltpu.SemaphoreType.DMA((20,)), pltpu.SemaphoreType.DMA((copies,)), pltpu.SemaphoreType.DMA((copies,)),
    ]
    rows = images.transpose(1, 0, 2).reshape(rows_all, width)
    results = pl.pallas_call(
        functools.partial(
            fused_kernel, (images_here, captions_here, planes, sides, dp_size), copies
        ),
        out_shape=tuple(jax.ShapeDtypeStruct(shape, kind) for shape, kind in out_shapes),
        in_specs=[hbm] * 7 + [vmem] * 13,
        out_specs=(hbm,) * 9 + (vmem,),
        scratch_shapes=scratch,
        compiler_params=pltpu.CompilerParams(
            collective_id=1, has_side_effects=True, vmem_limit_bytes=62 * 2**20
        ),
        name="fused_block",
    )(
        rows, qkv_weight, out_weight, fc1_weight, fc2_weight, image_proj, text_proj,
        fc1_bias, ln1_gain, ln1_bias, ln2_gain, ln2_bias, post_gain, post_bias,
        text_feats, text_gain, text_bias, log_scale, caption_counts, positives,
    )
    vectors = (HIDDEN,) + (WIDTH,) * 6 + (EMBED,) * 2 + (1, 1)
    finals = pl.pallas_call(
        functools.partial(finish_kernel, 1.0 / (images_here * dp_size * rep_size)),
        out_shape=tuple(jax.ShapeDtypeStruct(shape, kind) for shape, kind in out_shapes[:9])
        + tuple(jax.ShapeDtypeStruct((size,), F32) for size in vectors),
        in_specs=[hbm] * 9 + [vmem],
        out_specs=(hbm,) * 9 + (vmem,) * 11,
        scratch_shapes=[pltpu.VMEM(shape, kind) for shape, kind in out_shapes[:9]]
        + [pltpu.SemaphoreType.DMA((64,))],
        compiler_params=pltpu.CompilerParams(vmem_limit_bytes=62 * 2**20),
        name="results",
    )(*results)
    block_out, grad_images, g_qkv, g_out, g_fc1, g_fc2, g_ip, g_text, g_tp = finals[:9]
    g_fc1_bias, ln1_gain, ln1_bias, ln2_gain, ln2_bias, post_gain, post_bias, text_gain, text_bias = finals[9:18]
    loss, g_log_scale = finals[18:]

    def restore(values):
        return values.reshape(patches, images_here, width).transpose(1, 0, 2)

    return (
        restore(block_out), loss.reshape(()), restore(grad_images), g_qkv, g_out, g_fc1, g_fc1_bias, g_fc2.T,
        ln1_gain, ln1_bias, ln2_gain, ln2_bias, post_gain, post_bias, g_ip, g_text, text_gain, text_bias,
        g_tp, g_log_scale,
    )


def solution(mesh):
    dp_size, rep_size = mesh.shape["dp"], mesh.shape["rep"]
    body = functools.partial(fused_shards, dp_size, rep_size) if fits(dp_size, rep_size) else shards

    return jax.shard_map(
        body,
        mesh=mesh,
        in_specs=(
            P(("dp", "rep"), None, None),
            P(),
            P(),
            P(),
            P(),
            P(),
            P(),
            P(),
            P(),
            P(),
            P(),
            P(),
            P(),
            P(("dp", "rep"), None),
            P(),
            P(),
            P(),
            P(),
            P(("dp", "rep")),
            P(("dp", "rep")),
        ),
        out_specs=(
            P(("dp", "rep"), None, None),
            P(),
            P(("dp", "rep"), None, None),
            P("rep", "dp"),
            P("rep", "dp"),
            P("rep", "dp"),
            P(),
            P("rep", "dp"),
            P(),
            P(),
            P(),
            P(),
            P(),
            P(),
            P("rep", "dp"),
            P(("dp", "rep"), None),
            P(),
            P(),
            P("rep", "dp"),
            P(),
        ),
        check_vma=False,
    )
```

```python
import functools

import jax
import jax.numpy as jnp
from jax import lax
from jax.experimental import pallas as pl
from jax.experimental.pallas import tpu as pltpu
from jax.sharding import PartitionSpec as P

HEADS = 12
HDIM = 64


def matmul(left, right):
    return jnp.dot(left, right, preferred_element_type=jnp.float32)


def matmul_left(left, right):
    return lax.dot_general(
        left, right, (((0,), (0,)), ((), ())), preferred_element_type=jnp.float32
    )


def matmul_right(left, right):
    return lax.dot_general(
        left, right, (((1,), (1,)), ((), ())), preferred_element_type=jnp.float32
    )


def layer_norm(values, gain, bias):
    centered = values - jnp.mean(values, -1, keepdims=True)
    factor = lax.rsqrt(jnp.mean(centered * centered, -1, keepdims=True) + 1e-05)
    normed = centered * factor
    return (normed * gain + bias, normed, factor)


def norm_back(grad_out, normed, factor, gain):
    scaled = grad_out * gain
    grad_in = factor * (
        scaled
        - jnp.mean(scaled, -1, keepdims=True)
        - normed * jnp.mean(scaled * normed, -1, keepdims=True)
    )
    return (grad_in, jnp.sum(grad_out * normed, 0), jnp.sum(grad_out, 0))


def unit_rows(values):
    factor = lax.rsqrt(jnp.sum(values * values, -1, keepdims=True) + 1e-06)
    return (values * factor, factor)


def unit_back(grad_unit, unit, factor):
    return factor * (grad_unit - unit * jnp.sum(grad_unit * unit, -1, keepdims=True))


def row_logsumexp(values):
    top_value = jnp.max(values, 1, keepdims=True)
    return top_value[:, 0] + jnp.log(jnp.sum(jnp.exp(values - top_value), 1))


def shards(
    images,
    qkv_weight,
    out_weight,
    fc1_weight,
    fc1_bias,
    fc2_weight,
    ln1_gain,
    ln1_bias,
    ln2_gain,
    ln2_bias,
    post_gain,
    post_bias,
    image_proj,
    text_feats,
    text_gain,
    text_bias,
    text_proj,
    log_scale,
    caption_counts,
    positives,
):
    images_here, patches, model_width = images.shape
    row_count = images_here * patches
    resid = images.reshape(row_count, model_width).astype(jnp.float32)
    normed_one, unit_one, factor_one = layer_norm(resid, ln1_gain, ln1_bias)
    normed_in = normed_one.astype(jnp.bfloat16)
    packed = (
        matmul(normed_in, qkv_weight)
        .astype(jnp.bfloat16)
        .reshape(images_here, patches, 3, HEADS, HDIM)
    )
    query, keys, values = (packed[:, :, 0], packed[:, :, 1], packed[:, :, 2])
    scores = 0.125 * jnp.einsum("bqhd,bkhd->bhqk", query, keys, preferred_element_type=jnp.float32)
    score_peak = jnp.max(scores, -1, keepdims=True)
    score_lse = score_peak + jnp.log(jnp.sum(jnp.exp(scores - score_peak), -1, keepdims=True))
    attn_low = jnp.exp(scores - score_lse).astype(jnp.bfloat16)
    mixed = jnp.einsum("bhqk,bkhd->bqhd", attn_low, values, preferred_element_type=jnp.float32)
    mixed = mixed.reshape(row_count, model_width).astype(jnp.bfloat16)
    middle = resid + matmul(mixed, out_weight)
    normed_two, unit_two, factor_two = layer_norm(middle, ln2_gain, ln2_bias)
    normed_mid = normed_two.astype(jnp.bfloat16)
    hidden = matmul(normed_mid, fc1_weight) + fc1_bias
    gate_sig = jax.nn.sigmoid(1.702 * hidden)
    activation = (hidden * gate_sig).astype(jnp.bfloat16)
    block = middle + matmul(activation, fc2_weight)
    block_out = block.reshape(images_here, patches, model_width).astype(jnp.bfloat16)
    class_rows = block.reshape(images_here, patches, model_width)[:, 0, :]
    class_full, unit_post, factor_post = layer_norm(class_rows, post_gain, post_bias)
    class_norm = class_full.astype(jnp.bfloat16)
    image_unit, image_factor = unit_rows(matmul(class_norm, image_proj))
    image_low = image_unit.astype(jnp.bfloat16)
    text_full, unit_text, factor_text = layer_norm(
        text_feats.astype(jnp.float32), text_gain, text_bias
    )
    text_norm = text_full.astype(jnp.bfloat16)
    text_unit, text_factor = unit_rows(matmul(text_norm, text_proj))
    text_low = text_unit.astype(jnp.bfloat16)
    all_images, all_texts = (
        lax.all_gather(image_low, ("dp", "rep"), axis=0, tiled=True),
        lax.all_gather(text_low, ("dp", "rep"), axis=0, tiled=True),
    )
    all_positives = lax.all_gather(positives, ("dp", "rep"), axis=0, tiled=True)
    image_total = all_images.shape[0]
    caption_total = all_texts.shape[0]
    text_ratio = image_total / caption_total
    logit_scale = jnp.exp(log_scale[0])
    image_ids = lax.axis_index(("dp", "rep")) * images_here + jnp.arange(
        images_here, dtype=jnp.int32
    )
    counts = caption_counts.astype(jnp.float32)
    row_logits = logit_scale * matmul_right(image_low, all_texts)
    row_match = (all_positives[None, :] == image_ids[:, None]).astype(jnp.float32)
    row_lse = row_logsumexp(row_logits)
    image_loss = row_lse - jnp.sum(row_match * row_logits, 1) / counts
    col_logits = logit_scale * matmul_right(text_low, all_images)
    col_match = (positives[:, None] == jnp.arange(image_total, dtype=jnp.int32)[None, :]).astype(
        jnp.float32
    )
    col_lse = row_logsumexp(col_logits)
    caption_loss = col_lse - jnp.sum(col_match * col_logits, 1)
    grad_rows = (
        0.5 * (jnp.exp(row_logits - row_lse[:, None]) - row_match / counts[:, None])
    ).astype(jnp.bfloat16)
    grad_cols = (0.5 * text_ratio * (jnp.exp(col_logits - col_lse[:, None]) - col_match)).astype(
        jnp.bfloat16
    )
    total_part = 0.5 * jnp.sum(image_loss) + 0.5 * text_ratio * jnp.sum(caption_loss)
    scale_part = jnp.sum(grad_rows.astype(jnp.float32) * row_logits) + jnp.sum(
        grad_cols.astype(jnp.float32) * col_logits
    )
    total, scale_grad = lax.psum((total_part, scale_part), ("dp", "rep"))
    loss = total / image_total
    grad_log_scale = scale_grad.reshape(1)
    columns = grad_cols
    grad_image_unit = logit_scale * matmul(grad_rows, all_texts) + lax.psum_scatter(
        logit_scale * matmul_left(columns, text_low), ("dp", "rep"), scatter_dimension=0, tiled=True
    )
    columns = grad_rows
    grad_text_unit = logit_scale * matmul(grad_cols, all_images) + lax.psum_scatter(
        logit_scale * matmul_left(columns, image_low),
        ("dp", "rep"),
        scatter_dimension=0,
        tiled=True,
    )
    grad_image_embed = unit_back(grad_image_unit, image_unit, image_factor).astype(jnp.bfloat16)
    grad_image_proj = matmul_left(class_norm, grad_image_embed)
    grad_class, grad_post_gain, grad_post_bias = norm_back(
        matmul_right(grad_image_embed, image_proj), unit_post, factor_post, post_gain
    )
    grad_text_embed = unit_back(grad_text_unit, text_unit, text_factor).astype(jnp.bfloat16)
    grad_text_proj = matmul_left(text_norm, grad_text_embed)
    grad_text_feats, grad_text_gain, grad_text_bias = norm_back(
        matmul_right(grad_text_embed, text_proj), unit_text, factor_text, text_gain
    )
    grad_block = (
        jnp.zeros((images_here, patches, model_width), jnp.float32)
        .at[:, 0, :]
        .set(grad_class)
        .reshape(row_count, model_width)
    )
    grad_block_low = grad_block.astype(jnp.bfloat16)
    grad_activation = matmul_right(grad_block_low, fc2_weight)
    grad_hidden = (
        grad_activation * (gate_sig + 1.702 * hidden * gate_sig * (1.0 - gate_sig))
    ).astype(jnp.bfloat16)
    grad_fc1_bias = jnp.sum(grad_hidden.astype(jnp.float32), 0)
    grad_mid_norm, grad_ln2_gain, grad_ln2_bias = norm_back(
        matmul_right(grad_hidden, fc1_weight), unit_two, factor_two, ln2_gain
    )
    grad_middle = grad_block + grad_mid_norm
    grad_middle_low = grad_middle.astype(jnp.bfloat16)
    grad_out_weight = matmul_left(mixed, grad_middle_low)
    grad_mixed = (
        matmul_right(grad_middle_low, out_weight)
        .astype(jnp.bfloat16)
        .reshape(images_here, patches, HEADS, HDIM)
    )
    again_scores = 0.125 * jnp.einsum(
        "bqhd,bkhd->bhqk", query, keys, preferred_element_type=jnp.float32
    )
    attn_full = jnp.exp(again_scores - score_lse)
    grad_values = jnp.einsum(
        "bhqk,bqhd->bkhd", attn_low, grad_mixed, preferred_element_type=jnp.float32
    )
    grad_attn = jnp.einsum(
        "bqhd,bkhd->bhqk", grad_mixed, values, preferred_element_type=jnp.float32
    )
    grad_scores = (
        attn_full * (grad_attn - jnp.sum(grad_attn * attn_full, -1, keepdims=True))
    ).astype(jnp.bfloat16)
    grad_query = 0.125 * jnp.einsum(
        "bhqk,bkhd->bqhd", grad_scores, keys, preferred_element_type=jnp.float32
    )
    grad_keys = 0.125 * jnp.einsum(
        "bhqk,bqhd->bkhd", grad_scores, query, preferred_element_type=jnp.float32
    )
    grad_packed = (
        jnp.stack([grad_query, grad_keys, grad_values], 2)
        .reshape(row_count, 3 * model_width)
        .astype(jnp.bfloat16)
    )
    grad_qkv_weight = matmul_left(normed_in, grad_packed)
    grad_in_norm, grad_ln1_gain, grad_ln1_bias = norm_back(
        matmul_right(grad_packed, qkv_weight), unit_one, factor_one, ln1_gain
    )
    grad_images = (grad_middle + grad_in_norm).reshape(images_here, patches, model_width)
    grad_fc2_weight = matmul_left(activation, grad_block_low)
    grad_fc1_weight = matmul_left(normed_mid, grad_hidden)
    first_qkv, first_out, first_fc1, first_fc2, first_image, first_text = (
        lax.psum_scatter(grad_qkv_weight, "dp", scatter_dimension=1, tiled=True),
        lax.psum_scatter(grad_out_weight, "dp", scatter_dimension=1, tiled=True),
        lax.psum_scatter(grad_fc1_weight, "dp", scatter_dimension=1, tiled=True),
        lax.psum_scatter(grad_fc2_weight, "dp", scatter_dimension=1, tiled=True),
        lax.psum_scatter(grad_image_proj, "dp", scatter_dimension=1, tiled=True),
        lax.psum_scatter(grad_text_proj, "dp", scatter_dimension=1, tiled=True),
    )
    summed_qkv, summed_out, summed_fc1, summed_fc2, summed_image, summed_text = (
        lax.psum_scatter(first_qkv, "rep", scatter_dimension=0, tiled=True),
        lax.psum_scatter(first_out, "rep", scatter_dimension=0, tiled=True),
        lax.psum_scatter(first_fc1, "rep", scatter_dimension=0, tiled=True),
        lax.psum_scatter(first_fc2, "rep", scatter_dimension=0, tiled=True),
        lax.psum_scatter(first_image, "rep", scatter_dimension=0, tiled=True),
        lax.psum_scatter(first_text, "rep", scatter_dimension=0, tiled=True),
    )
    vector_sums = lax.psum(
        (
            grad_ln1_gain,
            grad_ln1_bias,
            grad_ln2_gain,
            grad_ln2_bias,
            grad_fc1_bias,
            grad_post_gain,
            grad_post_bias,
            grad_text_gain,
            grad_text_bias,
        ),
        ("dp", "rep"),
    )
    return (
        block_out,
        loss,
        grad_images,
        summed_qkv,
        summed_out,
        summed_fc1,
        vector_sums[4],
        summed_fc2,
        vector_sums[0],
        vector_sums[1],
        vector_sums[2],
        vector_sums[3],
        vector_sums[5],
        vector_sums[6],
        summed_image,
        grad_text_feats,
        vector_sums[7],
        vector_sums[8],
        summed_text,
        grad_log_scale,
    )


MESH = pl.DeviceIdType.MESH
F32 = jnp.float32
BF16 = jnp.bfloat16
PATCHES = 50
WIDTH = 768
HIDDEN = 3072
EMBED = 512
GROUP = 8
STEP = 160


def fits(dp_size, rep_size):
    return dp_size == 4 and rep_size == 8


def dot_rows(left, right):
    return lax.dot_general(left, right, (((1,), (1,)), ((), ())), preferred_element_type=F32)


def dot_cols(left, right):
    return lax.dot_general(left, right, (((0,), (0,)), ((), ())), preferred_element_type=F32)


def lane_shift(values, amount):
    width = values.shape[1]
    amount = amount % width
    return values if amount == 0 else pltpu.roll(values, width - amount, 1)


def pick_blocks(values, side, sides, block, count):
    lanes = block * count
    place = lax.broadcasted_iota(jnp.int32, (values.shape[0], lanes), 1) // block
    picked = lane_shift(values, side * block)[:, :lanes]
    for index in range(1, count):
        offset = (side + index * sides) * block - index * block
        picked = jnp.where(place == index, lane_shift(values, offset)[:, :lanes], picked)
    return picked


def head_spread(rows):
    count = rows.shape[0]
    lane_head = lax.broadcasted_iota(jnp.int32, (HEADS, count, WIDTH), 2) // HDIM
    head = lax.broadcasted_iota(jnp.int32, (HEADS, count, WIDTH), 0)
    spread = jnp.where(lane_head == head, rows[None], 0.0)
    return spread.reshape(HEADS * count, WIDTH)


def head_gather(stacked):
    count = stacked.shape[0] // HEADS
    stacked = stacked.reshape(HEADS, count, WIDTH)
    lane_head = lax.broadcasted_iota(jnp.int32, stacked.shape, 2) // HDIM
    head = lax.broadcasted_iota(jnp.int32, stacked.shape, 0)
    return jnp.sum(jnp.where(lane_head == head, stacked, 0.0), 0)


def fused_kernel(dims, counter, *refs):
    (
        x_hbm, qkv_hbm, out_hbm, fc1_hbm, fc2_hbm, ip_hbm, tp_hbm
    ) = refs[:7]
    smalls = refs[7:20]
    (
        block_hbm, images_hbm, qkv_out, w_out_out, fc1_out, fc2_out, ip_out, text_out, tp_out, g_vec,
        x, qkv, w_out, fc1, fc2, ip, tp,
        ni, kv, qd, mixed, middle, nmd, block_out, grad_images,
        g_qkv, g_out, g_fc1, g_fc2, g_ip, g_text, g_tp,
        attn, attn_low, gsp, uu,
        hid_c, small,
        t_all, pos_all, i_all, cnt_all, row_sum, col_sum,
        gi_send, gi_recv, gt_send, gt_recv,
        nm_full, gb_full, rf_out, rf_in, ro_out, ro_in, cn_out, cn_in, tn_out, tn_in,
        ca_out, ca_in, co_out, co_in, te_out, te_in, pa_send, pa_recv, ps_send, ps_recv, pt_send, pt_recv,
        vec_out, vec_in, vec_mid, vec_all, hid_s, act_s, gh_s, nm_sel,
        local_sem, send_sem, recv_sem, *small_refs,
    ) = refs[20:]
    (
        fc1_bias_in, ln1_gain_in, ln1_bias_in, ln2_gain_in, ln2_bias_in, post_gain_in, post_bias_in,
        text_feats, text_gain_in, text_bias_in, log_scale_in, caption_counts, positives,
    ) = small_refs
    images_here, captions_here, planes, sides, dp_size = dims
    plane_size = dp_size * sides
    rep_size = planes * sides
    rows_all = images_here * PATCHES
    half = rows_all // 2
    dp = lax.axis_index("dp")
    rep = lax.axis_index("rep")
    z = rep // sides
    side = lax.rem(rep, sides)
    slot = dp * sides + side
    row_y = dp // 2
    core = lax.rem(dp, 2)
    plane_images = plane_size * images_here
    line_captions = planes * captions_here
    image_total = plane_images * planes
    caption_total = line_captions * plane_size
    text_ratio = image_total / caption_total

    used = [0]
    unsent = []

    def plane_peer(step):
        peer = lax.rem(slot + step, plane_size)
        return peer, (peer // sides, z * sides + lax.rem(peer, sides))

    def line_peer(step):
        peer = lax.rem(z + step, planes)
        return peer, (dp, peer * sides + side)

    def copy_to(source, target, device, sends, arrivals):
        return pltpu.make_async_remote_copy(
            src_ref=source, dst_ref=target, send_sem=send_sem.at[sends], recv_sem=recv_sem.at[arrivals],
            device_id=device, device_id_type=MESH,
        )

    def take(count=1):
        used[0] += count
        return used[0] - count

    def exchange(peers, source_of, target, whole):
        index = take()
        for peer, device in peers:
            copy_to(source_of(peer), target, device, index, index).start()
        return (whole, index)

    def to_plane(source_of, target, whole):
        return exchange([plane_peer(step) for step in range(1, plane_size)], source_of, target, whole)

    def to_line(source_of, target, whole):
        return exchange([line_peer(step) for step in range(1, planes)], source_of, target, whole)

    def to_chips(buffer):
        peers = []
        for step in range(1, 2 * sides):
            peer = lax.rem(row_y * sides + side + step, 2 * sides)
            peers.append((peer, ((peer // sides) * 2 + core, z * sides + lax.rem(peer, sides))))
        mine = buffer.at[:, row_y, core, side]
        return exchange(peers, lambda peer: mine, mine, buffer.at[0 : planes - 1, 0])

    def to_partner(buffer):
        device = (row_y * 2 + 1 - core, rep)
        mine = buffer.at[:, :, core]
        return exchange([(0, device)], lambda peer: mine, mine, mine)

    def finish(sent):
        whole, index = sent
        pltpu.make_async_copy(whole, whole, recv_sem.at[index]).wait()
        unsent.append(pltpu.make_async_copy(whole, whole, send_sem.at[index]))

    others = plane_size - 1
    lines = planes - 1

    small_loads = []
    for index, (source, target) in enumerate(zip(smalls, small_refs)):
        small_loads.append(pltpu.make_async_copy(source, target, local_sem.at[20 + index]))
        small_loads[-1].start()
    loads = []

    def put_out(source, target):
        copy = pltpu.make_async_copy(source, target, local_sem.at[len(loads)])
        loads.append(copy)
        copy.start()
        return copy

    for index, (source, target) in enumerate(
        (
            (tp_hbm, tp), (x_hbm, x), (qkv_hbm, qkv), (out_hbm, w_out), (fc1_hbm, fc1), (fc2_hbm, fc2),
            (ip_hbm, ip),
        )
    ):
        load = pltpu.make_async_copy(source, target, local_sem.at[index])
        load.start()
        loads.append(load)

    barrier = pltpu.get_barrier_semaphore()
    for step in range(1, plane_size):
        pl.semaphore_signal(barrier, inc=1, device_id=plane_peer(step)[1], device_id_type=MESH)
    for step in range(1, planes):
        pl.semaphore_signal(barrier, inc=1, device_id=line_peer(step)[1], device_id_type=MESH)

    for load in small_loads:
        load.wait()
    fc1_bias = fc1_bias_in[...].reshape(1, HIDDEN)
    ln1_gain, ln1_bias, ln2_gain, ln2_bias, post_gain, post_bias = (
        ref[...].reshape(1, WIDTH)
        for ref in (ln1_gain_in, ln1_bias_in, ln2_gain_in, ln2_bias_in, post_gain_in, post_bias_in)
    )
    text_gain, text_bias = (ref[...].reshape(1, EMBED) for ref in (text_gain_in, text_bias_in))

    text_full, _, _ = layer_norm(text_feats[...].astype(F32), text_gain, text_bias)
    text_norm = text_full.astype(BF16)
    loads[0].wait()
    text_unit, text_factor = unit_rows(matmul(text_norm, tp[...]))
    t_all[z] = text_unit.astype(BF16)
    pos_rows = jnp.broadcast_to(positives[...].reshape(1, captions_here).astype(F32), (128, captions_here))
    pos_all[z] = jnp.transpose(pos_rows)
    cnt_rows = jnp.broadcast_to(caption_counts[...].reshape(1, images_here).astype(F32), (128, images_here))
    cnt_all[slot] = jnp.transpose(cnt_rows)
    pl.semaphore_wait(barrier, plane_size - 1 + planes - 1)
    text_copies = to_line(lambda peer: t_all.at[z], t_all.at[z], t_all.at[0:lines])
    pos_copies = to_line(lambda peer: pos_all.at[z], pos_all.at[z], pos_all.at[0:lines])
    cnt_copies = to_plane(lambda peer: cnt_all.at[slot], cnt_all.at[slot], cnt_all.at[0:others])
    text_lanes = EMBED // rep_size
    for to_side in range(sides):
        tn_out[to_side] = pick_blocks(text_full, to_side, sides, text_lanes, planes).astype(BF16)
    tn_copies = to_plane(lambda peer: tn_out.at[lax.rem(peer, sides)], tn_in.at[slot], tn_in.at[0:others])
    tn_in[slot] = tn_out[side]

    loads[1].wait()
    for first in range(0, rows_all, STEP):
        full = layer_norm(x[first : first + STEP, :].astype(F32), ln1_gain, ln1_bias)[0]
        full = full.reshape(STEP // 16, 2, GROUP, WIDTH)
        for part in range(2):
            to = part * half + first // 2
            ni[to : to + STEP // 2, :] = full[:, part].reshape(STEP // 2, WIDTH).astype(BF16)

    loads[2].wait()
    for first in range(0, 2 * WIDTH, WIDTH):
        kv[:, first : first + WIDTH] = matmul(ni[...], qkv[:, WIDTH + first : 2 * WIDTH + first]).astype(BF16)

    resid_c = x[0:images_here, :].astype(F32)
    normed_c = layer_norm(resid_c, ln1_gain, ln1_bias)[0].astype(BF16)
    query_c = matmul(normed_c, qkv[:, 0:WIDTH]).astype(BF16)
    query_spread = head_spread(query_c.astype(F32)).astype(BF16)
    scores = 0.125 * dot_rows(query_spread, kv[:, 0:WIDTH])
    row_image = lax.broadcasted_iota(jnp.int32, scores.shape, 0) & (images_here - 1)
    column = lax.broadcasted_iota(jnp.int32, scores.shape, 1)
    column_image = jnp.where(column < half, 0, GROUP) + (column & (GROUP - 1))
    scores = jnp.where(row_image == column_image, scores, -1e30)
    weights = jnp.exp(scores - jnp.max(scores, 1, keepdims=True))
    weights = weights * (1.0 / jnp.sum(weights, 1, keepdims=True))
    attn[...] = weights
    attn_low[...] = weights.astype(BF16)
    mixed_c = head_gather(matmul(attn_low[...], kv[:, WIDTH:]))
    block_lanes = WIDTH // rep_size
    mixed_f, normed_f = mixed_c.astype(BF16).astype(F32), normed_c.astype(F32)
    for to_side in range(sides):
        ro_out[to_side, 0] = pick_blocks(mixed_f, to_side, sides, block_lanes, planes).astype(BF16)
        ro_out[to_side, 1] = pick_blocks(normed_f, to_side, sides, block_lanes, planes).astype(BF16)
    ro_copies = to_plane(
        lambda peer: ro_out.at[lax.rem(peer, sides)], ro_in.at[:, slot], ro_in.at[:, 0:others]
    )
    ro_in[:, slot] = ro_out[side]
    loads[3].wait()
    middle_c = resid_c + matmul(mixed_c.astype(BF16), w_out[...])
    full, unit_two, factor_two = layer_norm(middle_c, ln2_gain, ln2_bias)
    nm_full[z, row_y, core, side] = full.astype(BF16)
    nm_line = to_line(
        lambda peer: nm_full.at[z, row_y, core, side], nm_full.at[z, row_y, core, side], nm_full.at[0:lines, 0, 0, 0]
    )
    loads[4].wait()
    hid_c[...] = matmul(full.astype(BF16), fc1[...]) + fc1_bias
    act_c = (hid_c[...] * jax.nn.sigmoid(1.702 * hid_c[...])).astype(BF16)
    loads[5].wait()
    block_c = middle_c + matmul(act_c, fc2[...])
    full, unit_post, factor_post = layer_norm(block_c, post_gain, post_bias)
    class_norm = full.astype(BF16)
    loads[6].wait()
    image_unit, image_factor = unit_rows(matmul(class_norm, ip[...]))
    i_all[slot] = image_unit.astype(BF16)
    image_copies = to_plane(lambda peer: i_all.at[slot], i_all.at[slot], i_all.at[0:others])
    small[0] = unit_two
    small[1] = unit_post

    value_rows = matmul(attn_low[...], ni[...])
    for to_side in range(sides):
        picked = pick_blocks(value_rows, to_side, sides, block_lanes, planes).astype(BF16)
        rf_out[to_side, HEADS:] = picked.reshape(HEADS, images_here, planes * block_lanes)
        cn_out[to_side] = pick_blocks(full, to_side, sides, block_lanes, planes).astype(BF16)
    cn_in[slot] = cn_out[side]

    heads_here = 3 * HEADS // dp_size
    bundle = heads_here // 3
    rf_copies = []
    arrivals = take(3)
    for step in range(1, plane_size):
        peer, device = plane_peer(step)
        for part in range(3):
            first = (peer // sides) * heads_here + part * bundle
            copy = copy_to(
                rf_out.at[lax.rem(peer, sides), pl.ds(lax.rem(first + HEADS, 2 * HEADS), bundle)],
                rf_in.at[pl.ds(part * bundle, bundle), slot], device, take(), arrivals + part,
            )
            rf_copies.append((copy, first, part))

    def head_kind(first):
        return first // HEADS

    def dense_query():
        qd[...] = (0.125 * matmul(ni[...], qkv[:, 0:WIDTH]).astype(BF16).astype(F32)).astype(BF16)

    def dense_attention(first, last):
        lane = lax.broadcasted_iota(jnp.int32, (half, 128), 1)
        apart = lax.broadcasted_iota(jnp.int32, (GROUP, half), 0) != (
            lax.broadcasted_iota(jnp.int32, (GROUP, half), 1) & (GROUP - 1)
        )
        bias = jnp.where(apart, -1e30, 0.0)[None]
        for index in range(first, last):
            rows = slice((index % 2) * half, (index % 2) * half + half)
            lanes = slice((index // 2) * 128, (index // 2) * 128 + 128)
            query = qd[rows, lanes]
            keys = kv[rows, lanes]
            values = kv[rows, WIDTH + lanes.start : WIDTH + lanes.stop]
            result = None
            for which in range(2):
                own = (lane < HDIM) if which == 0 else (lane >= HDIM)
                logits = dot_rows(jnp.where(own, query, jnp.zeros_like(query)), keys)
                logits = (logits.reshape(half // GROUP, GROUP, half) + bias).reshape(half, half)
                top = jnp.exp(logits - jnp.max(logits, 1, keepdims=True))
                got = matmul(top.astype(BF16), values) * (1.0 / jnp.sum(top, 1, keepdims=True))
                result = got if which == 0 else jnp.where(own, got, result)
            mixed[rows, lanes] = result.astype(BF16)

    def join_groups(values, first):
        parts = [
            values[part * half + first // 2 : part * half + (first + STEP) // 2].reshape(STEP // 16, GROUP, WIDTH)
            for part in range(2)
        ]
        return jnp.stack(parts, 1).reshape(STEP, WIDTH)

    def dense_out():
        added = matmul(mixed[...], w_out[...])
        for first in range(0, rows_all, STEP):
            rows = slice(first, first + STEP)
            value = x[rows, :].astype(F32) + join_groups(added, first)
            middle[rows, :] = value
            nmd[rows, :] = layer_norm(value, ln2_gain, ln2_bias)[0].astype(BF16)

    def dense_ff(part):
        rows = slice(part * half, (part + 1) * half)
        hidden = matmul(nmd[rows, :], fc1[...]) + fc1_bias
        act = (hidden * jax.nn.sigmoid(1.702 * hidden)).astype(BF16)
        block_out[rows, :] = (middle[rows, :] + matmul(act, fc2[...])).astype(BF16)
        return put_out(block_out.at[rows], block_hbm.at[rows])

    dense_query()
    dense_attention(0, 2)

    finish(text_copies)
    finish(pos_copies)
    finish(cnt_copies)
    finish(image_copies)
    scale = jnp.exp(log_scale_in[...].reshape(1, 1))
    images_low = i_all[...].reshape(plane_images, EMBED)
    texts_low = t_all[...].reshape(line_captions, EMBED)
    logits = scale * dot_rows(images_low, texts_low)
    logits_t = scale * dot_rows(texts_low, images_low)

    def image_ids(dim, shape):
        index = lax.broadcasted_iota(jnp.int32, shape, dim)
        holder = index // images_here
        owner = (holder // sides) * rep_size + z * sides + lax.rem(holder, sides)
        return (owner * images_here + lax.rem(index, images_here)).astype(F32)

    pos_col = pos_all[...].reshape(line_captions, 128)
    match_t = (pos_col[:, 0:1] == image_ids(1, logits_t.shape)).astype(F32)
    match = (jnp.transpose(pos_col) == image_ids(0, logits.shape)).astype(F32)
    counts = jnp.transpose(cnt_all[...].reshape(plane_images, 128))[0:1, :]
    row_sum[slot] = jnp.broadcast_to(jnp.sum(jnp.exp(logits_t), 0, keepdims=True), (8, plane_images))
    col_sum[z] = jnp.broadcast_to(jnp.sum(jnp.exp(logits), 0, keepdims=True), (8, line_captions))
    row_copies = to_plane(lambda peer: row_sum.at[slot], row_sum.at[slot], row_sum.at[0:others])
    col_copies = to_line(lambda peer: col_sum.at[z], col_sum.at[z], col_sum.at[0:lines])

    for copy, first, part in rf_copies:
        if part < 2:
            pl.when(head_kind(first) == 2)(copy.start)
    dense_attention(2, 8)

    finish(row_copies)
    finish(col_copies)
    row_lse = jnp.log(jnp.sum(row_sum[...], 0)[0:1])
    col_lse = jnp.log(jnp.sum(col_sum[...], 0)[0:1])
    grad_cols = (0.5 * text_ratio * (jnp.exp(logits - col_lse) - match)).astype(BF16)
    grad_rows_t = (0.5 * (jnp.exp(logits_t - row_lse) - match_t / counts)).astype(BF16)
    loss_part = 0.5 * (jnp.sum(row_lse) / plane_size - jnp.sum(match_t * logits_t / counts)) + (
        0.5 * text_ratio
    ) * (jnp.sum(col_lse) / planes - jnp.sum(match * logits))
    scale_part = jnp.sum(grad_cols.astype(F32) * logits) + jnp.sum(grad_rows_t.astype(F32) * logits_t)
    gi_send[...] = (
        (scale * (dot_cols(grad_rows_t, texts_low) + matmul(grad_cols, texts_low)))
        .astype(BF16)
        .reshape(plane_size, images_here, EMBED)
    )
    gi_copies = to_plane(lambda peer: gi_send.at[peer], gi_recv.at[slot], gi_recv.at[0:others])
    gi_recv[slot] = gi_send[slot]
    gt_send[...] = (
        (scale * (dot_cols(grad_cols, images_low) + matmul(grad_rows_t, images_low)))
        .astype(BF16)
        .reshape(planes, captions_here, EMBED)
    )
    gt_copies = to_line(lambda peer: gt_send.at[peer], gt_recv.at[z], gt_recv.at[0:lines])
    gt_recv[z] = gt_send[z]

    dense_attention(8, 12)
    dense_out()

    finish(gi_copies)
    cn_copies = to_plane(lambda peer: cn_out.at[lax.rem(peer, sides)], cn_in.at[slot], cn_in.at[0:others])
    for copy, first, part in rf_copies:
        if part == 2:
            pl.when(head_kind(first) == 2)(copy.start)
    grad_embed = unit_back(jnp.sum(gi_recv[...].astype(F32), 0), image_unit, image_factor).astype(BF16)
    grad_class, g_post_gain, g_post_bias = norm_back(
        dot_rows(grad_embed, ip[...]), small[1], factor_post, post_gain
    )
    gb_low = grad_class.astype(BF16)
    gb_full[z, row_y, core, side] = gb_low
    gb_line = to_line(
        lambda peer: gb_full.at[z, row_y, core, side], gb_full.at[z, row_y, core, side], gb_full.at[0:lines, 0, 0, 0]
    )
    gate = jax.nn.sigmoid(1.702 * hid_c[...])
    grad_hidden = (
        dot_rows(gb_low, fc2[...]) * (gate + 1.702 * hid_c[...] * gate * (1.0 - gate))
    ).astype(BF16)
    g_fc1_bias = jnp.sum(grad_hidden.astype(F32), 0, keepdims=True)
    grad_two, g_ln2_gain, g_ln2_bias = norm_back(
        dot_rows(grad_hidden, fc1[...]), small[0], factor_two, ln2_gain
    )
    grad_middle = grad_class + grad_two
    grad_middle_low = grad_middle.astype(BF16)
    m_plain = grad_middle_low.astype(F32)
    m_shift = lane_shift(m_plain, 64)
    cuts = (m_plain[:, 0:192], m_shift[:, 128:320], m_plain[:, 384:576], m_shift[:, 512:704])
    for to_dp, source in enumerate(cuts):
        ca_out[to_dp, :, 0:192] = source.astype(BF16)
        ca_out[to_dp, :, 256:384] = grad_embed[:, to_dp * 128 : to_dp * 128 + 128]
    ca_copies = to_plane(lambda peer: ca_out.at[peer // sides], ca_in.at[slot], ca_in.at[0:others])
    ca_in[slot] = ca_out[dp]
    grad_mixed = dot_rows(grad_middle_low, w_out[...]).astype(BF16)
    mixed_spread = head_spread(grad_mixed.astype(F32)).astype(BF16)
    grad_attn = dot_rows(mixed_spread, kv[:, WIDTH:])
    weights = attn[...]
    grad_scores = weights * (grad_attn - jnp.sum(grad_attn * weights, 1, keepdims=True))
    grad_scores = 0.125 * grad_scores.astype(BF16).astype(F32)
    gsp[0 : HEADS * images_here] = grad_scores.astype(BF16)
    gsp[HEADS * images_here :] = attn_low[...]
    score_low = gsp[0 : HEADS * images_here]
    grad_query = head_gather(matmul(score_low, kv[:, 0:WIDTH])).astype(BF16)
    key_rows = matmul(score_low, ni[...])
    for to_side in range(sides):
        picked = pick_blocks(key_rows, to_side, sides, block_lanes, planes).astype(BF16)
        rf_out[to_side, 0:HEADS] = picked.reshape(HEADS, images_here, planes * block_lanes)

    grad_q = grad_query.astype(F32)
    query_f = query_c.astype(F32)
    grad_v = grad_mixed.astype(F32)
    lane = lax.broadcasted_iota(jnp.int32, (images_here, 128), 1)
    q_shift, k_shift, v_shift = lane_shift(grad_q, 64), lane_shift(query_f, -64), lane_shift(grad_v, 64)
    co_out[0, :, 0:576] = grad_q[:, 0:576].astype(BF16)
    co_out[1, :, 0:128] = q_shift[:, 512:640].astype(BF16)
    co_out[1, :, 128:256] = jnp.where(lane < 64, q_shift[:, 640:768], k_shift[:, 0:128]).astype(BF16)
    co_out[1, :, 256:576] = k_shift[:, 128:448].astype(BF16)
    co_out[2, :, 0:384] = query_f[:, 384:768].astype(BF16)
    co_out[2, :, 384:576] = grad_v[:, 0:192].astype(BF16)
    co_out[3, :, 0:576] = v_shift[:, 128:704].astype(BF16)
    co_copies = to_plane(lambda peer: co_out.at[peer // sides], co_in.at[slot], co_in.at[0:others])
    for copy, first, _ in rf_copies:
        pl.when(head_kind(first) == 1)(copy.start)
    co_in[slot] = co_out[dp]
    for part in range(3):
        mine = dp * heads_here + part * bundle

        def keep(part=part, mine=mine):
            own = rf_out[side, pl.ds(lax.rem(mine + HEADS, 2 * HEADS), bundle)]
            rf_in[part * bundle : (part + 1) * bundle, slot] = own

        pl.when(head_kind(mine) > 0)(keep)

    finish(gt_copies)
    grad_text = unit_back(jnp.sum(gt_recv[...].astype(F32), 0), text_unit, text_factor).astype(BF16)
    for to_dp in range(dp_size):
        te_out[to_dp] = grad_text[:, to_dp * 128 : to_dp * 128 + 128]
    te_copies = to_plane(lambda peer: te_out.at[peer // sides], te_in.at[slot], te_in.at[0:others])
    te_in[slot] = te_out[dp]
    _, unit_text, factor_text = layer_norm(text_feats[...].astype(F32), text_gain, text_bias)
    g_feats, g_text_gain, g_text_bias = norm_back(
        dot_rows(grad_text, tp[...]), unit_text, factor_text, text_gain
    )
    g_text[...] = g_feats


    finish(nm_line)
    nm_chips = to_chips(nm_full)

    uu[0 : HEADS * images_here] = dot_rows(query_spread, qkv[:, WIDTH : 2 * WIDTH]).astype(BF16)
    uu[HEADS * images_here :] = dot_rows(mixed_spread, qkv[:, 2 * WIDTH :]).astype(BF16)
    class_in = dot_rows(grad_query, qkv[:, 0:WIDTH])

    spread = dot_cols(gsp[...], uu[...])
    g_ln1_gain = jnp.zeros((1, WIDTH), F32)
    g_ln1_bias = jnp.zeros((1, WIDTH), F32)
    for first in range(0, rows_all, STEP):
        rows = slice(first, first + STEP)
        _, unit, factor = layer_norm(x[rows, :].astype(F32), ln1_gain, ln1_bias)
        grad_out = join_groups(spread, first)
        if first == 0:
            grad_out = jnp.concatenate([grad_out[0:images_here] + class_in, grad_out[images_here:]], 0)
        grad_in, gain_part, bias_part = norm_back(grad_out, unit, factor, ln1_gain)
        grad_images[rows, :] = grad_in
        g_ln1_gain += gain_part[None]
        g_ln1_bias += bias_part[None]
    grad_images[0:images_here] += grad_middle
    outs = [put_out(grad_images, images_hbm), put_out(g_text, text_out)]

    vectors = (
        g_ln1_gain, g_ln1_bias, g_ln2_gain[None], g_ln2_bias[None], g_post_gain[None], g_post_bias[None],
        g_text_gain[None], g_text_bias[None],
    )
    for index, vector in enumerate(vectors):
        row = slice(index % 2, index % 2 + 1)
        vec_out[index // 2, row, 0 : vector.shape[1]] = vector
        vec_out[index // 2, row, WIDTH:] = g_fc1_bias[:, index * 384 : index * 384 + 384]
    first_lane = lax.broadcasted_iota(jnp.int32, (1, 256), 1) == 0
    vec_out[3, 0:1, EMBED:WIDTH] = jnp.where(first_lane, loss_part, 0.0)
    vec_out[3, 1:2, EMBED:WIDTH] = jnp.where(first_lane, scale_part, 0.0)
    vec_line = to_line(lambda peer: vec_out.at[peer], vec_in.at[z], vec_in.at[0:lines])
    vec_in[z] = vec_out[z]

    rows_here = planes * block_lanes
    finish(ro_copies)
    finish(cn_copies)
    finish(ca_copies)
    columns_in = ca_in[...].reshape(plane_images, 384)
    got = dot_cols(ro_in[0].reshape(plane_images, rows_here), columns_in[:, 0:256])
    pa_send[:, :, 0:256] = got.astype(BF16).reshape(planes, block_lanes, 256)
    got = dot_cols(cn_in[...].reshape(plane_images, rows_here), columns_in[:, 256:384])
    pa_send[:, :, 256:384] = got.astype(BF16).reshape(planes, block_lanes, 128)
    pa_copies = to_line(lambda peer: pa_send.at[peer], pa_recv.at[z], pa_recv.at[0:lines])
    pa_recv[z] = pa_send[z]

    for part in range(3):
        mine = dp * heads_here + part * bundle
        here = rf_in.at[part * bundle : (part + 1) * bundle, 0:others]
        pl.when(head_kind(mine) > 0)(pltpu.make_async_copy(here, here, recv_sem.at[arrivals + part]).wait)

        def repeat(part=part):
            rf_in[part * bundle : (part + 1) * bundle] = jnp.broadcast_to(
                ro_in[1][None], (bundle, plane_size, images_here, rows_here)
            )

        pl.when(head_kind(mine) == 0)(repeat)
    finish(co_copies)
    columns_in = co_in[...].reshape(plane_images, 640)
    lane = lax.broadcasted_iota(jnp.int32, (rows_here, 128), 1)
    for tile in range(5):
        right = columns_in[:, tile * 128 : tile * 128 + 128]
        got = dot_cols(rf_in[2 * tile].reshape(plane_images, rows_here), right)
        if 2 * tile + 1 < heads_here:
            other = dot_cols(rf_in[2 * tile + 1].reshape(plane_images, rows_here), right)
            got = jnp.where(lane < HDIM, got, other)
        width = min(128, 576 - tile * 128)
        ps_send[:, :, tile * 128 : tile * 128 + width] = (
            got[:, 0:width].astype(BF16).reshape(planes, block_lanes, width)
        )
    ps_copies = to_line(lambda peer: ps_send.at[peer], ps_recv.at[z], ps_recv.at[0:lines])
    ps_recv[z] = ps_send[z]
    finish(tn_copies)
    finish(te_copies)
    got = dot_cols(
        tn_in[...].reshape(plane_size * captions_here, planes * text_lanes),
        te_in[...].reshape(plane_size * captions_here, 128),
    )
    pt_send[...] = got.astype(BF16).reshape(planes, text_lanes, 128)
    pt_copies = to_line(lambda peer: pt_send.at[peer], pt_recv.at[z], pt_recv.at[0:lines])
    pt_recv[z] = pt_send[z]

    finish(vec_line)
    vec_mid[slot] = jnp.sum(vec_in[...], 0)
    vec_plane = to_plane(lambda peer: vec_mid.at[slot], vec_mid.at[slot], vec_mid.at[0:others])
    finish(gb_line)
    gb_chips = to_chips(gb_full)

    outs += [dense_ff(0)]
    finish(vec_plane)
    vec_all[z] = jnp.sum(vec_mid[...], 0)
    vec_last = to_line(lambda peer: vec_all.at[z], vec_all.at[z], vec_all.at[0:lines])
    finish(nm_chips)
    nm_partner = to_partner(nm_full)
    finish(gb_chips)
    gb_partner = to_partner(gb_full)
    outs += [dense_ff(1)]

    finish(nm_partner)
    all_rows = plane_images * planes
    nm_rows = nm_full[...].reshape(all_rows, WIDTH)
    my_columns = pl.ds(pl.multiple_of(dp * (HIDDEN // dp_size), 128), HIDDEN // dp_size)
    my_rows = pl.ds(pl.multiple_of(rep * (HIDDEN // rep_size), 128), HIDDEN // rep_size)
    hid_s[...] = matmul(nm_rows, fc1[:, my_columns]) + fc1_bias_in[my_columns].reshape(1, HIDDEN // dp_size)
    hidden = matmul(nm_rows, fc1[:, my_rows]) + fc1_bias_in[my_rows].reshape(1, HIDDEN // rep_size)
    act_s[...] = (hidden * jax.nn.sigmoid(1.702 * hidden)).astype(BF16)
    source = lax.broadcasted_iota(jnp.int32, (WIDTH, 128), 0)
    place = lax.broadcasted_iota(jnp.int32, (WIDTH, 128), 1)
    chosen = jnp.where((source == place + rep * block_lanes) & (place < block_lanes), 1.0, 0.0).astype(BF16)
    nm_sel[...] = matmul(nm_rows, chosen).astype(BF16)

    finish(gb_partner)
    gb_rows = gb_full[...].reshape(all_rows, WIDTH)
    gate = jax.nn.sigmoid(1.702 * hid_s[...])
    gh_s[...] = (
        dot_rows(gb_rows, fc2[my_columns, :]) * (gate + 1.702 * hid_s[...] * gate * (1.0 - gate))
    ).astype(BF16)
    g_fc1[...] = dot_cols(nm_sel[...], gh_s[...])[0:block_lanes]
    out_lanes = WIDTH // dp_size
    source = lax.broadcasted_iota(jnp.int32, (WIDTH, 256), 0)
    place = lax.broadcasted_iota(jnp.int32, (WIDTH, 256), 1)
    chosen = jnp.where((source == place + dp * out_lanes) & (place < out_lanes), 1.0, 0.0).astype(BF16)
    g_fc2[...] = dot_cols(matmul(gb_rows, chosen).astype(BF16), act_s[...])[0:out_lanes]

    outs += [put_out(g_fc1, fc1_out), put_out(g_fc2, fc2_out)]

    finish(pa_copies)
    summed = jnp.sum(pa_recv[...].astype(F32), 0)
    g_out[...] = summed[:, 0:192]
    g_ip[...] = summed[:, 256:384]
    finish(pt_copies)
    g_tp[...] = jnp.sum(pt_recv[...].astype(F32), 0)
    outs += [put_out(g_out, w_out_out), put_out(g_ip, ip_out), put_out(g_tp, tp_out)]
    finish(vec_last)
    g_vec[...] = vec_all[...].reshape(8, 1152)
    finish(ps_copies)
    g_qkv[...] = jnp.sum(ps_recv[...].astype(F32), 0)
    outs += [put_out(g_qkv, qkv_out)]
    for copy in outs + unsent:
        copy.wait()
    for copy, first, _ in rf_copies:
        pl.when(head_kind(first) > 0)(copy.wait_send)
    assert used[0] <= counter


def finish_kernel(scale, *refs):
    sources, vec_hbm, targets, outs_hbm = refs[0:9], refs[9], refs[10:19], refs[19:30]
    holds, vec, outs, sem = refs[30:39], refs[39], refs[40:51], refs[51]
    count = 0

    def copy(source, target):
        nonlocal count
        count += 1
        return pltpu.make_async_copy(source, target, sem.at[count - 1])

    vec_load = copy(vec_hbm, vec)
    vec_load.start()
    pieces = []
    for source, target, hold in zip(sources, targets, holds):
        parts = 5 if source.shape[0] > 400 else 1
        size = source.shape[0] // parts
        for first in range(0, source.shape[0], size):
            rows = pl.ds(first, size)
            pieces.append((copy(source.at[rows], hold.at[rows]), copy(hold.at[rows], target.at[rows])))
            pieces[-1][0].start()
    fc1_bias, ln1_gain, ln1_bias, ln2_gain, ln2_bias, post_gain, post_bias, text_gain, text_bias, loss, log_scale = outs
    vec_load.wait()
    for index, out in enumerate((ln1_gain, ln1_bias, ln2_gain, ln2_bias, post_gain, post_bias)):
        out[...] = vec[index : index + 1, 0:WIDTH].reshape(WIDTH)
    text_gain[...] = vec[6:7, 0:EMBED].reshape(EMBED)
    text_bias[...] = vec[7:8, 0:EMBED].reshape(EMBED)
    fc1_bias[...] = jnp.concatenate([vec[index : index + 1, WIDTH:] for index in range(8)], 1).reshape(HIDDEN)
    loss[...] = (vec[6:7, EMBED : EMBED + 128] * scale).reshape(128)[0:1]
    log_scale[...] = vec[7:8, EMBED : EMBED + 128].reshape(128)[0:1]
    stores = []
    for out, target in zip(outs, outs_hbm):
        stores.append(copy(out, target))
        stores[-1].start()
    for fetch, store in pieces:
        fetch.wait()
        store.start()
        stores.append(store)
    for store in stores:
        store.wait()


def fused_shards(
    dp_size,
    rep_size,
    images,
    qkv_weight,
    out_weight,
    fc1_weight,
    fc1_bias,
    fc2_weight,
    ln1_gain,
    ln1_bias,
    ln2_gain,
    ln2_bias,
    post_gain,
    post_bias,
    image_proj,
    text_feats,
    text_gain,
    text_bias,
    text_proj,
    log_scale,
    caption_counts,
    positives,
):
    images_here, patches, width = images.shape
    captions_here = text_feats.shape[0]
    sides = 2
    planes = rep_size // sides
    plane_size = dp_size * sides
    rows_all = images_here * patches
    heads_here = 3 * HEADS // dp_size
    block = WIDTH // rep_size
    text_block = EMBED // rep_size
    spread = HEADS * images_here
    line = planes * captions_here
    total_images = plane_size * planes * images_here
    copies = 50
    vmem = pl.BlockSpec(memory_space=pltpu.VMEM)
    hbm = pl.BlockSpec(memory_space=pl.ANY)

    def f32(*shape):
        return pltpu.VMEM(shape, F32)

    def b16(*shape):
        return pltpu.VMEM(shape, BF16)

    out_shapes = (
        ((rows_all, WIDTH), BF16),
        ((rows_all, WIDTH), F32),
        ((block, 3 * WIDTH // dp_size), F32),
        ((block, WIDTH // dp_size), F32),
        ((block, HIDDEN // dp_size), F32),
        ((WIDTH // dp_size, HIDDEN // rep_size), F32),
        ((block, EMBED // dp_size), F32),
        ((captions_here, EMBED), F32),
        ((text_block, EMBED // dp_size), F32),
        ((8, 1152), F32),
    )
    vectors = (
        fc1_bias, ln1_gain, ln1_bias, ln2_gain, ln2_bias, post_gain, post_bias,
        text_feats, text_gain, text_bias, log_scale, caption_counts, positives,
    )
    scratch = [
        b16(rows_all, WIDTH), b16(WIDTH, 3 * WIDTH), b16(WIDTH, WIDTH), b16(WIDTH, HIDDEN), b16(HIDDEN, WIDTH),
        b16(WIDTH, EMBED), b16(EMBED, EMBED),
        b16(rows_all, WIDTH), b16(rows_all, 2 * WIDTH), b16(rows_all, WIDTH), b16(rows_all, WIDTH),
        f32(rows_all, WIDTH), b16(rows_all, WIDTH), b16(rows_all, WIDTH), f32(rows_all, WIDTH),
        *(pltpu.VMEM(shape, kind) for shape, kind in out_shapes[2:9]),
        f32(spread, rows_all), b16(spread, rows_all), b16(2 * spread, rows_all), b16(2 * spread, WIDTH),
        f32(images_here, HIDDEN), f32(2, images_here, WIDTH),
        b16(planes, captions_here, EMBED), f32(planes, captions_here, 128),
        b16(plane_size, images_here, EMBED), f32(plane_size, images_here, 128),
        f32(plane_size, 8, plane_size * images_here), f32(planes, 8, line),
        b16(plane_size, images_here, EMBED), b16(plane_size, images_here, EMBED),
        b16(planes, captions_here, EMBED), b16(planes, captions_here, EMBED),
        b16(planes, dp_size // 2, 2, sides, images_here, WIDTH), b16(planes, dp_size // 2, 2, sides, images_here, WIDTH),
        b16(sides, 2 * HEADS, images_here, planes * block),
        b16(heads_here, plane_size, images_here, planes * block),
        b16(sides, 2, images_here, planes * block), b16(2, plane_size, images_here, planes * block),
        b16(sides, images_here, planes * block), b16(plane_size, images_here, planes * block),
        b16(sides, captions_here, planes * text_block), b16(plane_size, captions_here, planes * text_block),
        b16(dp_size, images_here, 384), b16(plane_size, images_here, 384),
        b16(dp_size, images_here, 640), b16(plane_size, images_here, 640),
        b16(dp_size, captions_here, 128), b16(plane_size, captions_here, 128),
        b16(planes, block, 384), b16(planes, block, 384), b16(planes, block, 576), b16(planes, block, 576),
        b16(planes, text_block, 128), b16(planes, text_block, 128),
        f32(4, 2, 1152), f32(planes, 2, 1152), f32(plane_size, 2, 1152), f32(planes, 2, 1152),
        f32(total_images, HIDDEN // dp_size), b16(total_images, HIDDEN // rep_size),
        b16(total_images, HIDDEN // dp_size), b16(total_images, 128),
        pltpu.SemaphoreType.DMA((33,)), pltpu.SemaphoreType.DMA((copies,)), pltpu.SemaphoreType.DMA((copies,)),
        *(pltpu.VMEM(value.shape, value.dtype) for value in vectors),
    ]
    rows = images.transpose(1, 0, 2).reshape(rows_all, width)
    results = pl.pallas_call(
        functools.partial(
            fused_kernel, (images_here, captions_here, planes, sides, dp_size), copies
        ),
        out_shape=tuple(jax.ShapeDtypeStruct(shape, kind) for shape, kind in out_shapes),
        in_specs=[hbm] * 20,
        out_specs=(hbm,) * 9 + (vmem,),
        scratch_shapes=scratch,
        compiler_params=pltpu.CompilerParams(
            collective_id=1, has_side_effects=True, vmem_limit_bytes=62 * 2**20
        ),
        name="fused_block",
    )(
        rows, qkv_weight, out_weight, fc1_weight, fc2_weight, image_proj, text_proj,
        *vectors,
    )
    sizes = (HIDDEN,) + (WIDTH,) * 6 + (EMBED,) * 2 + (1, 1)
    finals = pl.pallas_call(
        functools.partial(finish_kernel, 1.0 / (images_here * dp_size * rep_size)),
        out_shape=tuple(jax.ShapeDtypeStruct(shape, kind) for shape, kind in out_shapes[:9])
        + tuple(jax.ShapeDtypeStruct((size,), F32) for size in sizes),
        in_specs=[hbm] * 10,
        out_specs=(hbm,) * 20,
        scratch_shapes=[pltpu.VMEM(shape, kind) for shape, kind in out_shapes]
        + [pltpu.VMEM((size,), F32) for size in sizes]
        + [pltpu.SemaphoreType.DMA((46,))],
        compiler_params=pltpu.CompilerParams(vmem_limit_bytes=62 * 2**20),
        name="results",
    )(*results)
    block_out, grad_images, g_qkv, g_out, g_fc1, g_fc2, g_ip, g_text, g_tp = finals[:9]
    g_fc1_bias, ln1_gain, ln1_bias, ln2_gain, ln2_bias, post_gain, post_bias, text_gain, text_bias = finals[9:18]
    loss, g_log_scale = finals[18:]

    def restore(values):
        return values.reshape(patches, images_here, width).transpose(1, 0, 2)

    return (
        restore(block_out), loss.reshape(()), restore(grad_images), g_qkv, g_out, g_fc1, g_fc1_bias, g_fc2.T,
        ln1_gain, ln1_bias, ln2_gain, ln2_bias, post_gain, post_bias, g_ip, g_text, text_gain, text_bias,
        g_tp, g_log_scale,
    )


def solution(mesh):
    dp_size, rep_size = mesh.shape["dp"], mesh.shape["rep"]
    body = functools.partial(fused_shards, dp_size, rep_size) if fits(dp_size, rep_size) else shards

    return jax.shard_map(
        body,
        mesh=mesh,
        in_specs=(
            P(("dp", "rep"), None, None),
            P(),
            P(),
            P(),
            P(),
            P(),
            P(),
            P(),
            P(),
            P(),
            P(),
            P(),
            P(),
            P(("dp", "rep"), None),
            P(),
            P(),
            P(),
            P(),
            P(("dp", "rep")),
            P(("dp", "rep")),
        ),
        out_specs=(
            P(("dp", "rep"), None, None),
            P(),
            P(("dp", "rep"), None, None),
            P("rep", "dp"),
            P("rep", "dp"),
            P("rep", "dp"),
            P(),
            P("rep", "dp"),
            P(),
            P(),
            P(),
            P(),
            P(),
            P(),
            P("rep", "dp"),
            P(("dp", "rep"), None),
            P(),
            P(),
            P("rep", "dp"),
            P(),
        ),
        check_vma=False,
    )
```

```python
import functools

import jax
import jax.numpy as jnp
from jax import lax
from jax.experimental import pallas as pl
from jax.experimental.pallas import tpu as pltpu
from jax.sharding import PartitionSpec as P

HEADS = 12
HDIM = 64


def matmul(left, right):
    return jnp.dot(left, right, preferred_element_type=jnp.float32)


def matmul_left(left, right):
    return lax.dot_general(
        left, right, (((0,), (0,)), ((), ())), preferred_element_type=jnp.float32
    )


def matmul_right(left, right):
    return lax.dot_general(
        left, right, (((1,), (1,)), ((), ())), preferred_element_type=jnp.float32
    )


def layer_norm(values, gain, bias):
    centered = values - jnp.mean(values, -1, keepdims=True)
    factor = lax.rsqrt(jnp.mean(centered * centered, -1, keepdims=True) + 1e-05)
    normed = centered * factor
    return (normed * gain + bias, normed, factor)


def norm_back(grad_out, normed, factor, gain):
    scaled = grad_out * gain
    grad_in = factor * (
        scaled
        - jnp.mean(scaled, -1, keepdims=True)
        - normed * jnp.mean(scaled * normed, -1, keepdims=True)
    )
    return (grad_in, jnp.sum(grad_out * normed, 0), jnp.sum(grad_out, 0))


def unit_rows(values):
    factor = lax.rsqrt(jnp.sum(values * values, -1, keepdims=True) + 1e-06)
    return (values * factor, factor)


def unit_back(grad_unit, unit, factor):
    return factor * (grad_unit - unit * jnp.sum(grad_unit * unit, -1, keepdims=True))


def row_logsumexp(values):
    top_value = jnp.max(values, 1, keepdims=True)
    return top_value[:, 0] + jnp.log(jnp.sum(jnp.exp(values - top_value), 1))


def shards(
    images,
    qkv_weight,
    out_weight,
    fc1_weight,
    fc1_bias,
    fc2_weight,
    ln1_gain,
    ln1_bias,
    ln2_gain,
    ln2_bias,
    post_gain,
    post_bias,
    image_proj,
    text_feats,
    text_gain,
    text_bias,
    text_proj,
    log_scale,
    caption_counts,
    positives,
):
    images_here, patches, model_width = images.shape
    row_count = images_here * patches
    resid = images.reshape(row_count, model_width).astype(jnp.float32)
    normed_one, unit_one, factor_one = layer_norm(resid, ln1_gain, ln1_bias)
    normed_in = normed_one.astype(jnp.bfloat16)
    packed = (
        matmul(normed_in, qkv_weight)
        .astype(jnp.bfloat16)
        .reshape(images_here, patches, 3, HEADS, HDIM)
    )
    query, keys, values = (packed[:, :, 0], packed[:, :, 1], packed[:, :, 2])
    scores = 0.125 * jnp.einsum("bqhd,bkhd->bhqk", query, keys, preferred_element_type=jnp.float32)
    score_peak = jnp.max(scores, -1, keepdims=True)
    score_lse = score_peak + jnp.log(jnp.sum(jnp.exp(scores - score_peak), -1, keepdims=True))
    attn_low = jnp.exp(scores - score_lse).astype(jnp.bfloat16)
    mixed = jnp.einsum("bhqk,bkhd->bqhd", attn_low, values, preferred_element_type=jnp.float32)
    mixed = mixed.reshape(row_count, model_width).astype(jnp.bfloat16)
    middle = resid + matmul(mixed, out_weight)
    normed_two, unit_two, factor_two = layer_norm(middle, ln2_gain, ln2_bias)
    normed_mid = normed_two.astype(jnp.bfloat16)
    hidden = matmul(normed_mid, fc1_weight) + fc1_bias
    gate_sig = jax.nn.sigmoid(1.702 * hidden)
    activation = (hidden * gate_sig).astype(jnp.bfloat16)
    block = middle + matmul(activation, fc2_weight)
    block_out = block.reshape(images_here, patches, model_width).astype(jnp.bfloat16)
    class_rows = block.reshape(images_here, patches, model_width)[:, 0, :]
    class_full, unit_post, factor_post = layer_norm(class_rows, post_gain, post_bias)
    class_norm = class_full.astype(jnp.bfloat16)
    image_unit, image_factor = unit_rows(matmul(class_norm, image_proj))
    image_low = image_unit.astype(jnp.bfloat16)
    text_full, unit_text, factor_text = layer_norm(
        text_feats.astype(jnp.float32), text_gain, text_bias
    )
    text_norm = text_full.astype(jnp.bfloat16)
    text_unit, text_factor = unit_rows(matmul(text_norm, text_proj))
    text_low = text_unit.astype(jnp.bfloat16)
    all_images, all_texts = (
        lax.all_gather(image_low, ("dp", "rep"), axis=0, tiled=True),
        lax.all_gather(text_low, ("dp", "rep"), axis=0, tiled=True),
    )
    all_positives = lax.all_gather(positives, ("dp", "rep"), axis=0, tiled=True)
    image_total = all_images.shape[0]
    caption_total = all_texts.shape[0]
    text_ratio = image_total / caption_total
    logit_scale = jnp.exp(log_scale[0])
    image_ids = lax.axis_index(("dp", "rep")) * images_here + jnp.arange(
        images_here, dtype=jnp.int32
    )
    counts = caption_counts.astype(jnp.float32)
    row_logits = logit_scale * matmul_right(image_low, all_texts)
    row_match = (all_positives[None, :] == image_ids[:, None]).astype(jnp.float32)
    row_lse = row_logsumexp(row_logits)
    image_loss = row_lse - jnp.sum(row_match * row_logits, 1) / counts
    col_logits = logit_scale * matmul_right(text_low, all_images)
    col_match = (positives[:, None] == jnp.arange(image_total, dtype=jnp.int32)[None, :]).astype(
        jnp.float32
    )
    col_lse = row_logsumexp(col_logits)
    caption_loss = col_lse - jnp.sum(col_match * col_logits, 1)
    grad_rows = (
        0.5 * (jnp.exp(row_logits - row_lse[:, None]) - row_match / counts[:, None])
    ).astype(jnp.bfloat16)
    grad_cols = (0.5 * text_ratio * (jnp.exp(col_logits - col_lse[:, None]) - col_match)).astype(
        jnp.bfloat16
    )
    total_part = 0.5 * jnp.sum(image_loss) + 0.5 * text_ratio * jnp.sum(caption_loss)
    scale_part = jnp.sum(grad_rows.astype(jnp.float32) * row_logits) + jnp.sum(
        grad_cols.astype(jnp.float32) * col_logits
    )
    total, scale_grad = lax.psum((total_part, scale_part), ("dp", "rep"))
    loss = total / image_total
    grad_log_scale = scale_grad.reshape(1)
    columns = grad_cols
    grad_image_unit = logit_scale * matmul(grad_rows, all_texts) + lax.psum_scatter(
        logit_scale * matmul_left(columns, text_low), ("dp", "rep"), scatter_dimension=0, tiled=True
    )
    columns = grad_rows
    grad_text_unit = logit_scale * matmul(grad_cols, all_images) + lax.psum_scatter(
        logit_scale * matmul_left(columns, image_low),
        ("dp", "rep"),
        scatter_dimension=0,
        tiled=True,
    )
    grad_image_embed = unit_back(grad_image_unit, image_unit, image_factor).astype(jnp.bfloat16)
    grad_image_proj = matmul_left(class_norm, grad_image_embed)
    grad_class, grad_post_gain, grad_post_bias = norm_back(
        matmul_right(grad_image_embed, image_proj), unit_post, factor_post, post_gain
    )
    grad_text_embed = unit_back(grad_text_unit, text_unit, text_factor).astype(jnp.bfloat16)
    grad_text_proj = matmul_left(text_norm, grad_text_embed)
    grad_text_feats, grad_text_gain, grad_text_bias = norm_back(
        matmul_right(grad_text_embed, text_proj), unit_text, factor_text, text_gain
    )
    grad_block = (
        jnp.zeros((images_here, patches, model_width), jnp.float32)
        .at[:, 0, :]
        .set(grad_class)
        .reshape(row_count, model_width)
    )
    grad_block_low = grad_block.astype(jnp.bfloat16)
    grad_activation = matmul_right(grad_block_low, fc2_weight)
    grad_hidden = (
        grad_activation * (gate_sig + 1.702 * hidden * gate_sig * (1.0 - gate_sig))
    ).astype(jnp.bfloat16)
    grad_fc1_bias = jnp.sum(grad_hidden.astype(jnp.float32), 0)
    grad_mid_norm, grad_ln2_gain, grad_ln2_bias = norm_back(
        matmul_right(grad_hidden, fc1_weight), unit_two, factor_two, ln2_gain
    )
    grad_middle = grad_block + grad_mid_norm
    grad_middle_low = grad_middle.astype(jnp.bfloat16)
    grad_out_weight = matmul_left(mixed, grad_middle_low)
    grad_mixed = (
        matmul_right(grad_middle_low, out_weight)
        .astype(jnp.bfloat16)
        .reshape(images_here, patches, HEADS, HDIM)
    )
    again_scores = 0.125 * jnp.einsum(
        "bqhd,bkhd->bhqk", query, keys, preferred_element_type=jnp.float32
    )
    attn_full = jnp.exp(again_scores - score_lse)
    grad_values = jnp.einsum(
        "bhqk,bqhd->bkhd", attn_low, grad_mixed, preferred_element_type=jnp.float32
    )
    grad_attn = jnp.einsum(
        "bqhd,bkhd->bhqk", grad_mixed, values, preferred_element_type=jnp.float32
    )
    grad_scores = (
        attn_full * (grad_attn - jnp.sum(grad_attn * attn_full, -1, keepdims=True))
    ).astype(jnp.bfloat16)
    grad_query = 0.125 * jnp.einsum(
        "bhqk,bkhd->bqhd", grad_scores, keys, preferred_element_type=jnp.float32
    )
    grad_keys = 0.125 * jnp.einsum(
        "bhqk,bqhd->bkhd", grad_scores, query, preferred_element_type=jnp.float32
    )
    grad_packed = (
        jnp.stack([grad_query, grad_keys, grad_values], 2)
        .reshape(row_count, 3 * model_width)
        .astype(jnp.bfloat16)
    )
    grad_qkv_weight = matmul_left(normed_in, grad_packed)
    grad_in_norm, grad_ln1_gain, grad_ln1_bias = norm_back(
        matmul_right(grad_packed, qkv_weight), unit_one, factor_one, ln1_gain
    )
    grad_images = (grad_middle + grad_in_norm).reshape(images_here, patches, model_width)
    grad_fc2_weight = matmul_left(activation, grad_block_low)
    grad_fc1_weight = matmul_left(normed_mid, grad_hidden)
    first_qkv, first_out, first_fc1, first_fc2, first_image, first_text = (
        lax.psum_scatter(grad_qkv_weight, "dp", scatter_dimension=1, tiled=True),
        lax.psum_scatter(grad_out_weight, "dp", scatter_dimension=1, tiled=True),
        lax.psum_scatter(grad_fc1_weight, "dp", scatter_dimension=1, tiled=True),
        lax.psum_scatter(grad_fc2_weight, "dp", scatter_dimension=1, tiled=True),
        lax.psum_scatter(grad_image_proj, "dp", scatter_dimension=1, tiled=True),
        lax.psum_scatter(grad_text_proj, "dp", scatter_dimension=1, tiled=True),
    )
    summed_qkv, summed_out, summed_fc1, summed_fc2, summed_image, summed_text = (
        lax.psum_scatter(first_qkv, "rep", scatter_dimension=0, tiled=True),
        lax.psum_scatter(first_out, "rep", scatter_dimension=0, tiled=True),
        lax.psum_scatter(first_fc1, "rep", scatter_dimension=0, tiled=True),
        lax.psum_scatter(first_fc2, "rep", scatter_dimension=0, tiled=True),
        lax.psum_scatter(first_image, "rep", scatter_dimension=0, tiled=True),
        lax.psum_scatter(first_text, "rep", scatter_dimension=0, tiled=True),
    )
    vector_sums = lax.psum(
        (
            grad_ln1_gain,
            grad_ln1_bias,
            grad_ln2_gain,
            grad_ln2_bias,
            grad_fc1_bias,
            grad_post_gain,
            grad_post_bias,
            grad_text_gain,
            grad_text_bias,
        ),
        ("dp", "rep"),
    )
    return (
        block_out,
        loss,
        grad_images,
        summed_qkv,
        summed_out,
        summed_fc1,
        vector_sums[4],
        summed_fc2,
        vector_sums[0],
        vector_sums[1],
        vector_sums[2],
        vector_sums[3],
        vector_sums[5],
        vector_sums[6],
        summed_image,
        grad_text_feats,
        vector_sums[7],
        vector_sums[8],
        summed_text,
        grad_log_scale,
    )


MESH = pl.DeviceIdType.MESH
F32 = jnp.float32
BF16 = jnp.bfloat16
PATCHES = 50
WIDTH = 768
HIDDEN = 3072
EMBED = 512
GROUP = 8
STEP = 160


def fits(dp_size, rep_size):
    return dp_size == 4 and rep_size == 8


def dot_rows(left, right):
    return lax.dot_general(left, right, (((1,), (1,)), ((), ())), preferred_element_type=F32)


def dot_cols(left, right):
    return lax.dot_general(left, right, (((0,), (0,)), ((), ())), preferred_element_type=F32)


def lane_shift(values, amount):
    width = values.shape[1]
    amount = amount % width
    return values if amount == 0 else pltpu.roll(values, width - amount, 1)


def pick_blocks(values, side, sides, block, count):
    lanes = block * count
    place = lax.broadcasted_iota(jnp.int32, (values.shape[0], lanes), 1) // block
    picked = lane_shift(values, side * block)[:, :lanes]
    for index in range(1, count):
        offset = (side + index * sides) * block - index * block
        picked = jnp.where(place == index, lane_shift(values, offset)[:, :lanes], picked)
    return picked


def head_spread(rows):
    count = rows.shape[0]
    lane_head = lax.broadcasted_iota(jnp.int32, (HEADS, count, WIDTH), 2) // HDIM
    head = lax.broadcasted_iota(jnp.int32, (HEADS, count, WIDTH), 0)
    spread = jnp.where(lane_head == head, rows[None], 0.0)
    return spread.reshape(HEADS * count, WIDTH)


def head_gather(stacked):
    count = stacked.shape[0] // HEADS
    stacked = stacked.reshape(HEADS, count, WIDTH)
    lane_head = lax.broadcasted_iota(jnp.int32, stacked.shape, 2) // HDIM
    head = lax.broadcasted_iota(jnp.int32, stacked.shape, 0)
    return jnp.sum(jnp.where(lane_head == head, stacked, 0.0), 0)


def fused_kernel(dims, counter, *refs):
    (
        x_hbm, qkv_hbm, out_hbm, fc1_hbm, fc2_hbm, ip_hbm, tp_hbm
    ) = refs[:7]
    smalls = refs[7:20]
    (
        block_hbm, images_hbm, qkv_out, w_out_out, fc1_out, fc2_out, ip_out, text_out, tp_out, g_vec,
        x, qkv, w_out, fc1, fc2, ip, tp,
        ni, kv, qd, mixed, middle, nmd, block_out, grad_images,
        g_qkv, g_out, g_fc1, g_fc2, g_ip, g_text, g_tp,
        attn, attn_low, gsp, uu,
        hid_c, small,
        t_all, pos_all, i_all, cnt_all, row_sum, col_sum,
        gi_send, gi_recv, gt_send, gt_recv,
        nm_full, gb_full, rf_out, rf_in, ro_out, ro_in, cn_out, cn_in, tn_out, tn_in,
        ca_out, ca_in, co_out, co_in, te_out, te_in, pa_send, pa_recv, ps_send, ps_recv, pt_send, pt_recv,
        vec_out, vec_in, vec_mid, vec_all, hid_s, act_s, gh_s, nm_sel,
        local_sem, send_sem, recv_sem, *small_refs,
    ) = refs[20:]
    (
        fc1_bias_in, ln1_gain_in, ln1_bias_in, ln2_gain_in, ln2_bias_in, post_gain_in, post_bias_in,
        text_feats, text_gain_in, text_bias_in, log_scale_in, caption_counts, positives,
    ) = small_refs
    images_here, captions_here, planes, sides, dp_size = dims
    plane_size = dp_size * sides
    rep_size = planes * sides
    rows_all = images_here * PATCHES
    half = rows_all // 2
    dp = lax.axis_index("dp")
    rep = lax.axis_index("rep")
    z = rep // sides
    side = lax.rem(rep, sides)
    slot = dp * sides + side
    row_y = dp // 2
    core = lax.rem(dp, 2)
    chip = row_y * sides + side
    plane_images = plane_size * images_here
    line_captions = planes * captions_here
    image_total = plane_images * planes
    caption_total = line_captions * plane_size
    text_ratio = image_total / caption_total

    used = [0]
    unsent = []

    def plane_peer(step):
        peer = lax.rem(slot + step, plane_size)
        return peer, (peer // sides, z * sides + lax.rem(peer, sides))

    def line_peer(step):
        peer = lax.rem(z + step, planes)
        return peer, (dp, peer * sides + side)

    def copy_to(source, target, device, sends, arrivals):
        return pltpu.make_async_remote_copy(
            src_ref=source, dst_ref=target, send_sem=send_sem.at[sends], recv_sem=recv_sem.at[arrivals],
            device_id=device, device_id_type=MESH,
        )

    def take(count=1):
        used[0] += count
        return used[0] - count

    def exchange(peers, source_of, target, whole):
        index = take()
        for peer, device in peers:
            copy_to(source_of(peer), target, device, index, index).start()
        return (whole, index)

    def to_plane(source_of, target, whole):
        return exchange([plane_peer(step) for step in range(1, plane_size)], source_of, target, whole)

    def to_line(source_of, target, whole):
        return exchange([line_peer(step) for step in range(1, planes)], source_of, target, whole)

    def to_chips(buffer):
        peers = []
        for step in range(1, 2 * sides):
            peer = lax.rem(chip + step, 2 * sides)
            peers.append((peer, ((peer // sides) * 2 + core, z * sides + lax.rem(peer, sides))))
        mine = buffer.at[core, chip]
        return exchange(peers, lambda peer: mine, mine, buffer.at[0, 0 : 2 * sides - 1])

    def to_partner(buffer):
        device = (row_y * 2 + 1 - core, rep)
        mine = buffer.at[core]
        return exchange([(0, device)], lambda peer: mine, mine, mine)

    def finish(sent):
        whole, index = sent
        pltpu.make_async_copy(whole, whole, recv_sem.at[index]).wait()
        unsent.append(pltpu.make_async_copy(whole, whole, send_sem.at[index]))

    others = plane_size - 1
    lines = planes - 1

    small_loads = []
    for index, (source, target) in enumerate(zip(smalls, small_refs)):
        small_loads.append(pltpu.make_async_copy(source, target, local_sem.at[20 + index]))
        small_loads[-1].start()
    loads = []

    def put_out(source, target):
        copy = pltpu.make_async_copy(source, target, local_sem.at[len(loads)])
        loads.append(copy)
        copy.start()
        return copy

    for index, (source, target) in enumerate(
        (
            (tp_hbm, tp), (x_hbm, x), (qkv_hbm, qkv), (out_hbm, w_out), (fc1_hbm, fc1), (fc2_hbm, fc2),
            (ip_hbm, ip),
        )
    ):
        load = pltpu.make_async_copy(source, target, local_sem.at[index])
        load.start()
        loads.append(load)

    barrier = pltpu.get_barrier_semaphore()
    for step in range(1, plane_size):
        pl.semaphore_signal(barrier, inc=1, device_id=plane_peer(step)[1], device_id_type=MESH)
    for step in range(1, planes):
        pl.semaphore_signal(barrier, inc=1, device_id=line_peer(step)[1], device_id_type=MESH)

    for load in small_loads:
        load.wait()
    fc1_bias = fc1_bias_in[...].reshape(1, HIDDEN)
    ln1_gain, ln1_bias, ln2_gain, ln2_bias, post_gain, post_bias = (
        ref[...].reshape(1, WIDTH)
        for ref in (ln1_gain_in, ln1_bias_in, ln2_gain_in, ln2_bias_in, post_gain_in, post_bias_in)
    )
    text_gain, text_bias = (ref[...].reshape(1, EMBED) for ref in (text_gain_in, text_bias_in))

    text_full, _, _ = layer_norm(text_feats[...].astype(F32), text_gain, text_bias)
    text_norm = text_full.astype(BF16)
    loads[0].wait()
    text_unit, text_factor = unit_rows(matmul(text_norm, tp[...]))
    t_all[z] = text_unit.astype(BF16)
    pos_rows = jnp.broadcast_to(positives[...].reshape(1, captions_here).astype(F32), (128, captions_here))
    pos_all[z] = jnp.transpose(pos_rows)
    cnt_rows = jnp.broadcast_to(caption_counts[...].reshape(1, images_here).astype(F32), (128, images_here))
    cnt_all[slot] = jnp.transpose(cnt_rows)
    loads[1].wait()
    for first in range(0, rows_all, STEP):
        full = layer_norm(x[first : first + STEP, :].astype(F32), ln1_gain, ln1_bias)[0]
        full = full.reshape(STEP // 16, 2, GROUP, WIDTH)
        for part in range(2):
            to = part * half + first // 2
            ni[to : to + STEP // 2, :] = full[:, part].reshape(STEP // 2, WIDTH).astype(BF16)

    loads[2].wait()
    for first in range(0, 2 * WIDTH, WIDTH):
        kv[:, first : first + WIDTH] = matmul(ni[...], qkv[:, WIDTH + first : 2 * WIDTH + first]).astype(BF16)

    pl.semaphore_wait(barrier, plane_size - 1 + planes - 1)
    text_copies = to_line(lambda peer: t_all.at[z], t_all.at[z], t_all.at[0:lines])
    pos_copies = to_line(lambda peer: pos_all.at[z], pos_all.at[z], pos_all.at[0:lines])
    cnt_copies = to_plane(lambda peer: cnt_all.at[slot], cnt_all.at[slot], cnt_all.at[0:others])
    text_lanes = EMBED // rep_size
    for to_side in range(sides):
        tn_out[to_side] = pick_blocks(text_full, to_side, sides, text_lanes, planes).astype(BF16)
    tn_copies = to_plane(lambda peer: tn_out.at[lax.rem(peer, sides)], tn_in.at[slot], tn_in.at[0:others])
    tn_in[slot] = tn_out[side]

    resid_c = x[0:images_here, :].astype(F32)
    normed_c = layer_norm(resid_c, ln1_gain, ln1_bias)[0].astype(BF16)
    query_c = matmul(normed_c, qkv[:, 0:WIDTH]).astype(BF16)
    query_spread = head_spread(query_c.astype(F32)).astype(BF16)
    scores = 0.125 * dot_rows(query_spread, kv[:, 0:WIDTH])
    row_image = lax.broadcasted_iota(jnp.int32, scores.shape, 0) & (images_here - 1)
    column = lax.broadcasted_iota(jnp.int32, scores.shape, 1)
    column_image = jnp.where(column < half, 0, GROUP) + (column & (GROUP - 1))
    scores = jnp.where(row_image == column_image, scores, -1e30)
    weights = jnp.exp(scores - jnp.max(scores, 1, keepdims=True))
    weights = weights * (1.0 / jnp.sum(weights, 1, keepdims=True))
    attn[...] = weights
    attn_low[...] = weights.astype(BF16)
    mixed_c = head_gather(matmul(attn_low[...], kv[:, WIDTH:]))
    block_lanes = WIDTH // rep_size
    mixed_f, normed_f = mixed_c.astype(BF16).astype(F32), normed_c.astype(F32)
    for to_side in range(sides):
        ro_out[to_side, 0] = pick_blocks(mixed_f, to_side, sides, block_lanes, planes).astype(BF16)
        ro_out[to_side, 1] = pick_blocks(normed_f, to_side, sides, block_lanes, planes).astype(BF16)
    ro_copies = to_plane(
        lambda peer: ro_out.at[lax.rem(peer, sides)], ro_in.at[slot], ro_in.at[0:others]
    )
    ro_in[slot] = ro_out[side]
    loads[3].wait()
    middle_c = resid_c + matmul(mixed_c.astype(BF16), w_out[...])
    full, unit_two, factor_two = layer_norm(middle_c, ln2_gain, ln2_bias)
    nm_full[core, chip, z] = full.astype(BF16)
    nm_line = to_line(
        lambda peer: nm_full.at[core, chip, z], nm_full.at[core, chip, z], nm_full.at[0, 0, 0:lines]
    )
    loads[4].wait()
    hid_c[...] = matmul(full.astype(BF16), fc1[...]) + fc1_bias
    act_c = (hid_c[...] * jax.nn.sigmoid(1.702 * hid_c[...])).astype(BF16)
    loads[5].wait()
    block_c = middle_c + matmul(act_c, fc2[...])
    full, unit_post, factor_post = layer_norm(block_c, post_gain, post_bias)
    class_norm = full.astype(BF16)
    loads[6].wait()
    image_unit, image_factor = unit_rows(matmul(class_norm, ip[...]))
    i_all[slot] = image_unit.astype(BF16)
    image_copies = to_plane(lambda peer: i_all.at[slot], i_all.at[slot], i_all.at[0:others])
    small[0] = unit_two
    small[1] = unit_post

    value_rows = matmul(attn_low[...], ni[...])
    for to_side in range(sides):
        picked = pick_blocks(value_rows, to_side, sides, block_lanes, planes).astype(BF16)
        rf_out[to_side, HEADS:] = picked.reshape(HEADS, images_here, planes * block_lanes)
        cn_out[to_side] = pick_blocks(full, to_side, sides, block_lanes, planes).astype(BF16)
    cn_in[slot] = cn_out[side]

    heads_here = 3 * HEADS // dp_size
    bundle = heads_here // 3
    rf_copies = []
    arrivals = take(3)
    for step in range(1, plane_size):
        peer, device = plane_peer(step)
        for part in range(3):
            first = (peer // sides) * heads_here + part * bundle
            copy = copy_to(
                rf_out.at[lax.rem(peer, sides), pl.ds(lax.rem(first + HEADS, 2 * HEADS), bundle)],
                rf_in.at[slot, pl.ds(part * bundle, bundle)], device, 32 + len(rf_copies), arrivals + part,
            )
            rf_copies.append((copy, first, part))

    def head_kind(first):
        return first // HEADS

    def dense_query():
        qd[...] = (0.125 * matmul(ni[...], qkv[:, 0:WIDTH]).astype(BF16).astype(F32)).astype(BF16)

    def dense_attention(first, last):
        lane = lax.broadcasted_iota(jnp.int32, (half, 128), 1)
        apart = lax.broadcasted_iota(jnp.int32, (GROUP, half), 0) != (
            lax.broadcasted_iota(jnp.int32, (GROUP, half), 1) & (GROUP - 1)
        )
        bias = jnp.where(apart, -1e30, 0.0)[None]
        for index in range(first, last):
            rows = slice((index % 2) * half, (index % 2) * half + half)
            lanes = slice((index // 2) * 128, (index // 2) * 128 + 128)
            query = qd[rows, lanes]
            keys = kv[rows, lanes]
            values = kv[rows, WIDTH + lanes.start : WIDTH + lanes.stop]
            result = None
            for which in range(2):
                own = (lane < HDIM) if which == 0 else (lane >= HDIM)
                logits = dot_rows(jnp.where(own, query, jnp.zeros_like(query)), keys)
                logits = (logits.reshape(half // GROUP, GROUP, half) + bias).reshape(half, half)
                top = jnp.exp(logits - jnp.max(logits, 1, keepdims=True))
                got = matmul(top.astype(BF16), values) * (1.0 / jnp.sum(top, 1, keepdims=True))
                result = got if which == 0 else jnp.where(own, got, result)
            mixed[rows, lanes] = result.astype(BF16)

    def join_groups(values, first):
        parts = [
            values[part * half + first // 2 : part * half + (first + STEP) // 2].reshape(STEP // 16, GROUP, WIDTH)
            for part in range(2)
        ]
        return jnp.stack(parts, 1).reshape(STEP, WIDTH)

    def dense_out():
        added = matmul(mixed[...], w_out[...])
        for first in range(0, rows_all, STEP):
            rows = slice(first, first + STEP)
            value = x[rows, :].astype(F32) + join_groups(added, first)
            middle[rows, :] = value
            nmd[rows, :] = layer_norm(value, ln2_gain, ln2_bias)[0].astype(BF16)

    def dense_ff(part):
        rows = slice(part * half, (part + 1) * half)
        hidden = matmul(nmd[rows, :], fc1[...]) + fc1_bias
        act = (hidden * jax.nn.sigmoid(1.702 * hidden)).astype(BF16)
        block_out[rows, :] = (middle[rows, :] + matmul(act, fc2[...])).astype(BF16)
        return put_out(block_out.at[rows], block_hbm.at[rows])

    dense_query()
    uu[0 : HEADS * images_here] = dot_rows(query_spread, qkv[:, WIDTH : 2 * WIDTH]).astype(BF16)
    dense_attention(0, 2)

    finish(text_copies)
    finish(pos_copies)
    finish(cnt_copies)
    finish(image_copies)
    scale = jnp.exp(log_scale_in[...].reshape(1, 1))
    images_low = i_all[...].reshape(plane_images, EMBED)
    texts_low = t_all[...].reshape(line_captions, EMBED)
    logits = scale * dot_rows(images_low, texts_low)
    logits_t = scale * dot_rows(texts_low, images_low)

    def image_ids(dim, shape):
        index = lax.broadcasted_iota(jnp.int32, shape, dim)
        holder = index // images_here
        owner = (holder // sides) * rep_size + z * sides + lax.rem(holder, sides)
        return (owner * images_here + lax.rem(index, images_here)).astype(F32)

    pos_col = pos_all[...].reshape(line_captions, 128)
    match_t = (pos_col[:, 0:1] == image_ids(1, logits_t.shape)).astype(F32)
    match = (jnp.transpose(pos_col) == image_ids(0, logits.shape)).astype(F32)
    counts = jnp.transpose(cnt_all[...].reshape(plane_images, 128))[0:1, :]
    row_sum[slot] = jnp.broadcast_to(jnp.sum(jnp.exp(logits_t), 0, keepdims=True), (8, plane_images))
    col_sum[z] = jnp.broadcast_to(jnp.sum(jnp.exp(logits), 0, keepdims=True), (8, line_captions))
    row_copies = to_plane(lambda peer: row_sum.at[slot], row_sum.at[slot], row_sum.at[0:others])
    col_copies = to_line(lambda peer: col_sum.at[z], col_sum.at[z], col_sum.at[0:lines])

    for copy, first, part in rf_copies:
        if part < 2:
            pl.when(head_kind(first) == 2)(copy.start)
    dense_attention(2, 8)

    finish(row_copies)
    finish(col_copies)
    row_lse = jnp.log(jnp.sum(row_sum[...], 0)[0:1])
    col_lse = jnp.log(jnp.sum(col_sum[...], 0)[0:1])
    grad_cols = (0.5 * text_ratio * (jnp.exp(logits - col_lse) - match)).astype(BF16)
    grad_rows_t = (0.5 * (jnp.exp(logits_t - row_lse) - match_t / counts)).astype(BF16)
    loss_part = 0.5 * (jnp.sum(row_lse) / plane_size - jnp.sum(match_t * logits_t / counts)) + (
        0.5 * text_ratio
    ) * (jnp.sum(col_lse) / planes - jnp.sum(match * logits))
    scale_part = jnp.sum(grad_cols.astype(F32) * logits) + jnp.sum(grad_rows_t.astype(F32) * logits_t)
    gi_send[...] = (
        (scale * (dot_cols(grad_rows_t, texts_low) + matmul(grad_cols, texts_low)))
        .astype(BF16)
        .reshape(plane_size, images_here, EMBED)
    )
    gi_copies = to_plane(lambda peer: gi_send.at[peer], gi_recv.at[slot], gi_recv.at[0:others])
    gi_recv[slot] = gi_send[slot]
    gt_send[...] = (
        (scale * (dot_cols(grad_cols, images_low) + matmul(grad_rows_t, images_low)))
        .astype(BF16)
        .reshape(planes, captions_here, EMBED)
    )
    gt_copies = to_line(lambda peer: gt_send.at[peer], gt_recv.at[z], gt_recv.at[0:lines])
    gt_recv[z] = gt_send[z]

    dense_attention(8, 12)
    dense_out()

    finish(gi_copies)
    cn_copies = to_plane(lambda peer: cn_out.at[lax.rem(peer, sides)], cn_in.at[slot], cn_in.at[0:others])
    for copy, first, part in rf_copies:
        if part == 2:
            pl.when(head_kind(first) == 2)(copy.start)
    grad_embed = unit_back(jnp.sum(gi_recv[...].astype(F32), 0), image_unit, image_factor).astype(BF16)
    grad_class, g_post_gain, g_post_bias = norm_back(
        dot_rows(grad_embed, ip[...]), small[1], factor_post, post_gain
    )
    gb_low = grad_class.astype(BF16)
    gb_full[core, chip, z] = gb_low
    gb_line = to_line(
        lambda peer: gb_full.at[core, chip, z], gb_full.at[core, chip, z], gb_full.at[0, 0, 0:lines]
    )
    gate = jax.nn.sigmoid(1.702 * hid_c[...])
    grad_hidden = (
        dot_rows(gb_low, fc2[...]) * (gate + 1.702 * hid_c[...] * gate * (1.0 - gate))
    ).astype(BF16)
    g_fc1_bias = jnp.sum(grad_hidden.astype(F32), 0, keepdims=True)
    grad_two, g_ln2_gain, g_ln2_bias = norm_back(
        dot_rows(grad_hidden, fc1[...]), small[0], factor_two, ln2_gain
    )
    grad_middle = grad_class + grad_two
    grad_middle_low = grad_middle.astype(BF16)
    m_plain = grad_middle_low.astype(F32)
    m_shift = lane_shift(m_plain, 64)
    cuts = (m_plain[:, 0:192], m_shift[:, 128:320], m_plain[:, 384:576], m_shift[:, 512:704])
    for to_dp, source in enumerate(cuts):
        ca_out[to_dp, :, 0:192] = source.astype(BF16)
        ca_out[to_dp, :, 256:384] = grad_embed[:, to_dp * 128 : to_dp * 128 + 128]
    ca_copies = to_plane(lambda peer: ca_out.at[peer // sides], ca_in.at[slot], ca_in.at[0:others])
    ca_in[slot] = ca_out[dp]
    grad_mixed = dot_rows(grad_middle_low, w_out[...]).astype(BF16)
    mixed_spread = head_spread(grad_mixed.astype(F32)).astype(BF16)
    grad_attn = dot_rows(mixed_spread, kv[:, WIDTH:])
    weights = attn[...]
    grad_scores = weights * (grad_attn - jnp.sum(grad_attn * weights, 1, keepdims=True))
    grad_scores = 0.125 * grad_scores.astype(BF16).astype(F32)
    gsp[0 : HEADS * images_here] = grad_scores.astype(BF16)
    gsp[HEADS * images_here :] = attn_low[...]
    score_low = gsp[0 : HEADS * images_here]
    key_rows = matmul(score_low, ni[...])
    for to_side in range(sides):
        picked = pick_blocks(key_rows, to_side, sides, block_lanes, planes).astype(BF16)
        rf_out[to_side, 0:HEADS] = picked.reshape(HEADS, images_here, planes * block_lanes)

    for copy, first, _ in rf_copies:
        pl.when(head_kind(first) == 1)(copy.start)
    grad_query = head_gather(matmul(score_low, kv[:, 0:WIDTH])).astype(BF16)

    grad_q = grad_query.astype(F32)
    query_f = query_c.astype(F32)
    grad_v = grad_mixed.astype(F32)
    lane = lax.broadcasted_iota(jnp.int32, (images_here, 128), 1)
    q_shift, k_shift, v_shift = lane_shift(grad_q, 64), lane_shift(query_f, -64), lane_shift(grad_v, 64)
    co_out[0, :, 0:576] = grad_q[:, 0:576].astype(BF16)
    co_out[1, :, 0:128] = q_shift[:, 512:640].astype(BF16)
    co_out[1, :, 128:256] = jnp.where(lane < 64, q_shift[:, 640:768], k_shift[:, 0:128]).astype(BF16)
    co_out[1, :, 256:576] = k_shift[:, 128:448].astype(BF16)
    co_out[2, :, 0:384] = query_f[:, 384:768].astype(BF16)
    co_out[2, :, 384:576] = grad_v[:, 0:192].astype(BF16)
    co_out[3, :, 0:576] = v_shift[:, 128:704].astype(BF16)
    co_copies = to_plane(lambda peer: co_out.at[peer // sides], co_in.at[slot], co_in.at[0:others])
    co_in[slot] = co_out[dp]
    for part in range(3):
        mine = dp * heads_here + part * bundle

        def keep(part=part, mine=mine):
            own = rf_out[side, pl.ds(lax.rem(mine + HEADS, 2 * HEADS), bundle)]
            rf_in[slot, part * bundle : (part + 1) * bundle] = own

        pl.when(head_kind(mine) > 0)(keep)

    finish(gt_copies)
    grad_text = unit_back(jnp.sum(gt_recv[...].astype(F32), 0), text_unit, text_factor).astype(BF16)
    for to_dp in range(dp_size):
        te_out[to_dp] = grad_text[:, to_dp * 128 : to_dp * 128 + 128]
    te_copies = to_plane(lambda peer: te_out.at[peer // sides], te_in.at[slot], te_in.at[0:others])
    te_in[slot] = te_out[dp]
    _, unit_text, factor_text = layer_norm(text_feats[...].astype(F32), text_gain, text_bias)
    g_feats, g_text_gain, g_text_bias = norm_back(
        dot_rows(grad_text, tp[...]), unit_text, factor_text, text_gain
    )
    g_text[...] = g_feats


    finish(nm_line)
    nm_chips = to_chips(nm_full)

    uu[HEADS * images_here :] = dot_rows(mixed_spread, qkv[:, 2 * WIDTH :]).astype(BF16)
    class_in = dot_rows(grad_query, qkv[:, 0:WIDTH])

    spread = dot_cols(gsp[...], uu[...])
    g_ln1_gain = jnp.zeros((1, WIDTH), F32)
    g_ln1_bias = jnp.zeros((1, WIDTH), F32)
    for first in range(0, rows_all, STEP):
        rows = slice(first, first + STEP)
        _, unit, factor = layer_norm(x[rows, :].astype(F32), ln1_gain, ln1_bias)
        grad_out = join_groups(spread, first)
        if first == 0:
            grad_out = jnp.concatenate([grad_out[0:images_here] + class_in, grad_out[images_here:]], 0)
        grad_in, gain_part, bias_part = norm_back(grad_out, unit, factor, ln1_gain)
        grad_images[rows, :] = grad_in
        g_ln1_gain += gain_part[None]
        g_ln1_bias += bias_part[None]
    grad_images[0:images_here] += grad_middle
    outs = [put_out(grad_images, images_hbm), put_out(g_text, text_out)]

    vectors = (
        g_ln1_gain, g_ln1_bias, g_ln2_gain[None], g_ln2_bias[None], g_post_gain[None], g_post_bias[None],
        g_text_gain[None], g_text_bias[None],
    )
    for index, vector in enumerate(vectors):
        row = slice(index % 2, index % 2 + 1)
        vec_out[index // 2, row, 0 : vector.shape[1]] = vector
        vec_out[index // 2, row, WIDTH:] = g_fc1_bias[:, index * 384 : index * 384 + 384]
    first_lane = lax.broadcasted_iota(jnp.int32, (1, 256), 1) == 0
    vec_out[3, 0:1, EMBED:WIDTH] = jnp.where(first_lane, loss_part, 0.0)
    vec_out[3, 1:2, EMBED:WIDTH] = jnp.where(first_lane, scale_part, 0.0)
    vec_line = to_line(lambda peer: vec_out.at[peer], vec_in.at[z], vec_in.at[0:lines])
    vec_in[z] = vec_out[z]

    rows_here = planes * block_lanes
    finish(ro_copies)
    finish(cn_copies)
    finish(ca_copies)
    columns_in = ca_in[...].reshape(plane_images, 384)
    got = dot_cols(ro_in[:, 0].reshape(plane_images, rows_here), columns_in[:, 0:256])
    pa_send[:, :, 0:256] = got.astype(BF16).reshape(planes, block_lanes, 256)
    got = dot_cols(cn_in[...].reshape(plane_images, rows_here), columns_in[:, 256:384])
    pa_send[:, :, 256:384] = got.astype(BF16).reshape(planes, block_lanes, 128)
    pa_copies = to_line(lambda peer: pa_send.at[peer], pa_recv.at[z], pa_recv.at[0:lines])
    pa_recv[z] = pa_send[z]

    for part in range(3):
        mine = dp * heads_here + part * bundle
        here = rf_in.at[0:others, part * bundle : (part + 1) * bundle]
        pl.when(head_kind(mine) > 0)(pltpu.make_async_copy(here, here, recv_sem.at[arrivals + part]).wait)

        def repeat(part=part):
            rf_in[:, part * bundle : (part + 1) * bundle] = jnp.broadcast_to(
                ro_in[:, 1][:, None], (plane_size, bundle, images_here, rows_here)
            )

        pl.when(head_kind(mine) == 0)(repeat)
    finish(co_copies)
    columns_in = co_in[...].reshape(plane_images, 640)
    lane = lax.broadcasted_iota(jnp.int32, (rows_here, 128), 1)
    for tile in range(5):
        right = columns_in[:, tile * 128 : tile * 128 + 128]
        got = dot_cols(rf_in[:, 2 * tile].reshape(plane_images, rows_here), right)
        if 2 * tile + 1 < heads_here:
            other = dot_cols(rf_in[:, 2 * tile + 1].reshape(plane_images, rows_here), right)
            got = jnp.where(lane < HDIM, got, other)
        width = min(128, 576 - tile * 128)
        ps_send[:, :, tile * 128 : tile * 128 + width] = (
            got[:, 0:width].astype(BF16).reshape(planes, block_lanes, width)
        )
    ps_copies = to_line(lambda peer: ps_send.at[peer], ps_recv.at[z], ps_recv.at[0:lines])
    ps_recv[z] = ps_send[z]
    finish(tn_copies)
    finish(te_copies)
    got = dot_cols(
        tn_in[...].reshape(plane_size * captions_here, planes * text_lanes),
        te_in[...].reshape(plane_size * captions_here, 128),
    )
    pt_send[...] = got.astype(BF16).reshape(planes, text_lanes, 128)
    pt_copies = to_line(lambda peer: pt_send.at[peer], pt_recv.at[z], pt_recv.at[0:lines])
    pt_recv[z] = pt_send[z]

    finish(vec_line)
    vec_mid[slot] = jnp.sum(vec_in[...], 0)
    vec_plane = to_plane(lambda peer: vec_mid.at[slot], vec_mid.at[slot], vec_mid.at[0:others])
    finish(gb_line)
    gb_chips = to_chips(gb_full)

    outs += [dense_ff(0)]
    finish(vec_plane)
    vec_all[z] = jnp.sum(vec_mid[...], 0)
    vec_last = to_line(lambda peer: vec_all.at[z], vec_all.at[z], vec_all.at[0:lines])
    finish(nm_chips)
    nm_partner = to_partner(nm_full)
    finish(gb_chips)
    gb_partner = to_partner(gb_full)
    outs += [dense_ff(1)]

    finish(nm_partner)
    all_rows = plane_images * planes
    nm_rows = nm_full[...].reshape(all_rows, WIDTH)
    my_columns = pl.ds(pl.multiple_of(dp * (HIDDEN // dp_size), 128), HIDDEN // dp_size)
    my_rows = pl.ds(pl.multiple_of(rep * (HIDDEN // rep_size), 128), HIDDEN // rep_size)
    hid_s[...] = matmul(nm_rows, fc1[:, my_columns]) + fc1_bias_in[my_columns].reshape(1, HIDDEN // dp_size)
    hidden = matmul(nm_rows, fc1[:, my_rows]) + fc1_bias_in[my_rows].reshape(1, HIDDEN // rep_size)
    act_s[...] = (hidden * jax.nn.sigmoid(1.702 * hidden)).astype(BF16)
    source = lax.broadcasted_iota(jnp.int32, (WIDTH, 128), 0)
    place = lax.broadcasted_iota(jnp.int32, (WIDTH, 128), 1)
    chosen = jnp.where((source == place + rep * block_lanes) & (place < block_lanes), 1.0, 0.0).astype(BF16)
    nm_sel[...] = matmul(nm_rows, chosen).astype(BF16)

    finish(gb_partner)
    gb_rows = gb_full[...].reshape(all_rows, WIDTH)
    gate = jax.nn.sigmoid(1.702 * hid_s[...])
    gh_s[...] = (
        dot_rows(gb_rows, fc2[my_columns, :]) * (gate + 1.702 * hid_s[...] * gate * (1.0 - gate))
    ).astype(BF16)
    g_fc1[...] = dot_cols(nm_sel[...], gh_s[...])[0:block_lanes]
    out_lanes = WIDTH // dp_size
    source = lax.broadcasted_iota(jnp.int32, (WIDTH, 256), 0)
    place = lax.broadcasted_iota(jnp.int32, (WIDTH, 256), 1)
    chosen = jnp.where((source == place + dp * out_lanes) & (place < out_lanes), 1.0, 0.0).astype(BF16)
    g_fc2[...] = dot_cols(matmul(gb_rows, chosen).astype(BF16), act_s[...])[0:out_lanes]

    outs += [put_out(g_fc1, fc1_out), put_out(g_fc2, fc2_out)]

    finish(pa_copies)
    summed = jnp.sum(pa_recv[...].astype(F32), 0)
    g_out[...] = summed[:, 0:192]
    g_ip[...] = summed[:, 256:384]
    finish(pt_copies)
    g_tp[...] = jnp.sum(pt_recv[...].astype(F32), 0)
    outs += [put_out(g_out, w_out_out), put_out(g_ip, ip_out), put_out(g_tp, tp_out)]
    finish(vec_last)
    g_vec[...] = vec_all[...].reshape(8, 1152)
    finish(ps_copies)
    g_qkv[...] = jnp.sum(ps_recv[...].astype(F32), 0)
    outs += [put_out(g_qkv, qkv_out)]
    for copy in outs + unsent:
        copy.wait()
    for copy, first, _ in rf_copies:
        pl.when(head_kind(first) > 0)(copy.wait_send)
    assert used[0] <= counter


def finish_kernel(scale, *refs):
    sources, vec_hbm, targets, outs_hbm = refs[0:9], refs[9], refs[10:19], refs[19:30]
    holds, vec, outs, sem = refs[30:39], refs[39], refs[40:51], refs[51]
    count = 0

    def copy(source, target):
        nonlocal count
        count += 1
        return pltpu.make_async_copy(source, target, sem.at[count - 1])

    vec_load = copy(vec_hbm, vec)
    vec_load.start()
    pieces = []
    for source, target, hold in zip(sources, targets, holds):
        parts = 2 if source.shape[0] > 400 else 1
        size = source.shape[0] // parts
        for first in range(0, source.shape[0], size):
            rows = pl.ds(first, size)
            pieces.append((copy(source.at[rows], hold.at[rows]), copy(hold.at[rows], target.at[rows])))
            pieces[-1][0].start()
    fc1_bias, ln1_gain, ln1_bias, ln2_gain, ln2_bias, post_gain, post_bias, text_gain, text_bias, loss, log_scale = outs
    vec_load.wait()
    for index, out in enumerate((ln1_gain, ln1_bias, ln2_gain, ln2_bias, post_gain, post_bias)):
        out[...] = vec[index : index + 1, 0:WIDTH].reshape(WIDTH)
    text_gain[...] = vec[6:7, 0:EMBED].reshape(EMBED)
    text_bias[...] = vec[7:8, 0:EMBED].reshape(EMBED)
    fc1_bias[...] = jnp.concatenate([vec[index : index + 1, WIDTH:] for index in range(8)], 1).reshape(HIDDEN)
    loss[...] = (vec[6:7, EMBED : EMBED + 128] * scale).reshape(128)[0:1]
    log_scale[...] = vec[7:8, EMBED : EMBED + 128].reshape(128)[0:1]
    stores = []
    for out, target in zip(outs, outs_hbm):
        stores.append(copy(out, target))
        stores[-1].start()
    for fetch, store in pieces:
        fetch.wait()
        store.start()
        stores.append(store)
    for store in stores:
        store.wait()


def fused_shards(
    dp_size,
    rep_size,
    images,
    qkv_weight,
    out_weight,
    fc1_weight,
    fc1_bias,
    fc2_weight,
    ln1_gain,
    ln1_bias,
    ln2_gain,
    ln2_bias,
    post_gain,
    post_bias,
    image_proj,
    text_feats,
    text_gain,
    text_bias,
    text_proj,
    log_scale,
    caption_counts,
    positives,
):
    images_here, patches, width = images.shape
    captions_here = text_feats.shape[0]
    sides = 2
    planes = rep_size // sides
    plane_size = dp_size * sides
    rows_all = images_here * patches
    heads_here = 3 * HEADS // dp_size
    block = WIDTH // rep_size
    text_block = EMBED // rep_size
    spread = HEADS * images_here
    line = planes * captions_here
    total_images = plane_size * planes * images_here
    copies = 32
    vmem = pl.BlockSpec(memory_space=pltpu.VMEM)
    hbm = pl.BlockSpec(memory_space=pl.ANY)

    def f32(*shape):
        return pltpu.VMEM(shape, F32)

    def b16(*shape):
        return pltpu.VMEM(shape, BF16)

    out_shapes = (
        ((rows_all, WIDTH), BF16),
        ((rows_all, WIDTH), F32),
        ((block, 3 * WIDTH // dp_size), F32),
        ((block, WIDTH // dp_size), F32),
        ((block, HIDDEN // dp_size), F32),
        ((WIDTH // dp_size, HIDDEN // rep_size), F32),
        ((block, EMBED // dp_size), F32),
        ((captions_here, EMBED), F32),
        ((text_block, EMBED // dp_size), F32),
        ((8, 1152), F32),
    )
    vectors = (
        fc1_bias, ln1_gain, ln1_bias, ln2_gain, ln2_bias, post_gain, post_bias,
        text_feats, text_gain, text_bias, log_scale, caption_counts, positives,
    )
    scratch = [
        b16(rows_all, WIDTH), b16(WIDTH, 3 * WIDTH), b16(WIDTH, WIDTH), b16(WIDTH, HIDDEN), b16(HIDDEN, WIDTH),
        b16(WIDTH, EMBED), b16(EMBED, EMBED),
        b16(rows_all, WIDTH), b16(rows_all, 2 * WIDTH), b16(rows_all, WIDTH), b16(rows_all, WIDTH),
        f32(rows_all, WIDTH), b16(rows_all, WIDTH), b16(rows_all, WIDTH), f32(rows_all, WIDTH),
        *(pltpu.VMEM(shape, kind) for shape, kind in out_shapes[2:9]),
        f32(spread, rows_all), b16(spread, rows_all), b16(2 * spread, rows_all), b16(2 * spread, WIDTH),
        f32(images_here, HIDDEN), f32(2, images_here, WIDTH),
        b16(planes, captions_here, EMBED), f32(planes, captions_here, 128),
        b16(plane_size, images_here, EMBED), f32(plane_size, images_here, 128),
        f32(plane_size, 8, plane_size * images_here), f32(planes, 8, line),
        b16(plane_size, images_here, EMBED), b16(plane_size, images_here, EMBED),
        b16(planes, captions_here, EMBED), b16(planes, captions_here, EMBED),
        b16(2, dp_size // 2 * sides, planes, images_here, WIDTH), b16(2, dp_size // 2 * sides, planes, images_here, WIDTH),
        b16(sides, 2 * HEADS, images_here, planes * block),
        b16(plane_size, heads_here, images_here, planes * block),
        b16(sides, 2, images_here, planes * block), b16(plane_size, 2, images_here, planes * block),
        b16(sides, images_here, planes * block), b16(plane_size, images_here, planes * block),
        b16(sides, captions_here, planes * text_block), b16(plane_size, captions_here, planes * text_block),
        b16(dp_size, images_here, 384), b16(plane_size, images_here, 384),
        b16(dp_size, images_here, 640), b16(plane_size, images_here, 640),
        b16(dp_size, captions_here, 128), b16(plane_size, captions_here, 128),
        b16(planes, block, 384), b16(planes, block, 384), b16(planes, block, 576), b16(planes, block, 576),
        b16(planes, text_block, 128), b16(planes, text_block, 128),
        f32(4, 2, 1152), f32(planes, 2, 1152), f32(plane_size, 2, 1152), f32(planes, 2, 1152),
        f32(total_images, HIDDEN // dp_size), b16(total_images, HIDDEN // rep_size),
        b16(total_images, HIDDEN // dp_size), b16(total_images, 128),
        pltpu.SemaphoreType.DMA((33,)), pltpu.SemaphoreType.DMA((32 + 3 * (plane_size - 1),)), pltpu.SemaphoreType.DMA((copies,)),
        *(pltpu.VMEM(value.shape, value.dtype) for value in vectors),
    ]
    rows = images.transpose(1, 0, 2).reshape(rows_all, width)
    results = pl.pallas_call(
        functools.partial(
            fused_kernel, (images_here, captions_here, planes, sides, dp_size), copies
        ),
        out_shape=tuple(jax.ShapeDtypeStruct(shape, kind) for shape, kind in out_shapes),
        in_specs=[hbm] * 20,
        out_specs=(hbm,) * 9 + (vmem,),
        scratch_shapes=scratch,
        compiler_params=pltpu.CompilerParams(
            collective_id=1, has_side_effects=True, vmem_limit_bytes=62 * 2**20
        ),
        name="fused_block",
    )(
        rows, qkv_weight, out_weight, fc1_weight, fc2_weight, image_proj, text_proj,
        *vectors,
    )
    sizes = (HIDDEN,) + (WIDTH,) * 6 + (EMBED,) * 2 + (1, 1)
    finals = pl.pallas_call(
        functools.partial(finish_kernel, 1.0 / (images_here * dp_size * rep_size)),
        out_shape=tuple(jax.ShapeDtypeStruct(shape, kind) for shape, kind in out_shapes[:9])
        + tuple(jax.ShapeDtypeStruct((size,), F32) for size in sizes),
        in_specs=[hbm] * 10,
        out_specs=(hbm,) * 20,
        scratch_shapes=[pltpu.VMEM(shape, kind) for shape, kind in out_shapes]
        + [pltpu.VMEM((size,), F32) for size in sizes]
        + [pltpu.SemaphoreType.DMA((34,))],
        compiler_params=pltpu.CompilerParams(vmem_limit_bytes=62 * 2**20),
        name="results",
    )(*results)
    block_out, grad_images, g_qkv, g_out, g_fc1, g_fc2, g_ip, g_text, g_tp = finals[:9]
    g_fc1_bias, ln1_gain, ln1_bias, ln2_gain, ln2_bias, post_gain, post_bias, text_gain, text_bias = finals[9:18]
    loss, g_log_scale = finals[18:]

    def restore(values):
        return values.reshape(patches, images_here, width).transpose(1, 0, 2)

    return (
        restore(block_out), loss.reshape(()), restore(grad_images), g_qkv, g_out, g_fc1, g_fc1_bias, g_fc2.T,
        ln1_gain, ln1_bias, ln2_gain, ln2_bias, post_gain, post_bias, g_ip, g_text, text_gain, text_bias,
        g_tp, g_log_scale,
    )


def solution(mesh):
    dp_size, rep_size = mesh.shape["dp"], mesh.shape["rep"]
    body = functools.partial(fused_shards, dp_size, rep_size) if fits(dp_size, rep_size) else shards

    return jax.shard_map(
        body,
        mesh=mesh,
        in_specs=(
            P(("dp", "rep"), None, None),
            P(),
            P(),
            P(),
            P(),
            P(),
            P(),
            P(),
            P(),
            P(),
            P(),
            P(),
            P(),
            P(("dp", "rep"), None),
            P(),
            P(),
            P(),
            P(),
            P(("dp", "rep")),
            P(("dp", "rep")),
        ),
        out_specs=(
            P(("dp", "rep"), None, None),
            P(),
            P(("dp", "rep"), None, None),
            P("rep", "dp"),
            P("rep", "dp"),
            P("rep", "dp"),
            P(),
            P("rep", "dp"),
            P(),
            P(),
            P(),
            P(),
            P(),
            P(),
            P("rep", "dp"),
            P(("dp", "rep"), None),
            P(),
            P(),
            P("rep", "dp"),
            P(),
        ),
        check_vma=False,
    )
```
